32 devices in a mesh: dp: 8 (over z, x), tensor: 4 (over y, core).
Axes of the slice: x: 2, y: 2, z: 4, core: 2. Of those that a mesh axis runs over, the one named last changes fastest.
Arguments:
- tokens: bfloat16 [4096, 768], P(('dp', 'tensor')), may hold values from -6 to 6
- block_count: int32 [32], P('dp'), may hold values from 0 to 128, as said below
- block_first: int32 [32], P('dp'), may hold values from 0 to 1, as said below
- norm1_gain: bfloat16 [768], replicated, may hold values from 0.5 to 1.5
- w_qkv: bfloat16 [768, 3, 768], P('dp', None, 'tensor'), may hold values from -0.3125 to 0.3125
- w_out: bfloat16 [768, 768], P('tensor', 'dp'), may hold values from -0.875 to 0.875
- norm2_gain: bfloat16 [768], replicated, may hold values from 0.5 to 1.5
- w_in: bfloat16 [768, 2, 1152], P('dp', None, 'tensor'), may hold values from -0.21875 to 0.21875
- w_down: bfloat16 [1152, 768], P('tensor', 'dp'), may hold values from -0.375 to 0.375
- cotangent: bfloat16 [4096, 768], P(('dp', 'tensor')), may hold values from -6 to 6
Outputs:
- mixed: bfloat16 [4096, 768], P(('dp', 'tensor'))
- input_grad: bfloat16 [4096, 768], P(('dp', 'tensor'))
- grad_norm1: float32 [768], replicated
- grad_qkv: float32 [768, 3, 768], P('dp', None, 'tensor')
- grad_out: float32 [768, 768], P('tensor', 'dp')
- grad_norm2: float32 [768], replicated
- grad_in: float32 [768, 2, 1152], P('dp', None, 'tensor')
- grad_down: float32 [1152, 768], P('tensor', 'dp')
The draws below stay inside these ranges and needn't reach their ends.
Inputs may be any that keep to these rules, and one draw needn't show every extreme that they name: `block_count`: A dp index's 4 blocks hold its sequences in order, each starting at a block's start, all its blocks full but the last; the blocks after a dp index's last sequence hold 0; every dp index uses its first block; on some dp index one sequence fills all 512 rows, on another only the first half of the blocks is used. `block_first`: 1 exactly on the first block of each sequence; the first block of every dp index is 1; unused blocks are 0.
All inputs are finite; a program needn't handle non-finite values.
Results may differ from the reference program's by a relative error of at most 0.023.
Values may be sent and summed in bfloat16 or wider, within the bound.
No kernel may reach another device: no remote copies, remote signals or barrier semaphores. Data moves between devices by JAX's collectives and lax.ppermute only.
A program may use at most 64 MiB of HBM per device.

```python
import jax
import jax.numpy as jnp
from jax import lax

HEADS = 12
HEAD_DIM = 64
D = 768
FF = 1152
WINDOW = 128
TOK_DEV = 512
BLOCKS = 4
TOKENS = 4096
N_DP = 8


def block_layout(key):
    keys = jax.random.split(key, 5)
    blocks = BLOCKS
    devices = N_DP
    used = jax.random.randint(keys[0], (devices,), (blocks + 1) // 2, blocks + 1)
    full_device = jax.random.randint(keys[1], (), 0, devices)
    other_device = (full_device + 1 + jax.random.randint(keys[2], (), 0, devices - 1)) % devices
    used = used.at[other_device].set((blocks + 1) // 2).at[full_device].set(blocks)
    column = jnp.arange(blocks, dtype=jnp.int32)[None, :]
    device_row = jnp.arange(devices, dtype=jnp.int32)[:, None]
    inside = column < used[:, None]
    starts = (jax.random.randint(keys[3], (devices, blocks), 0, 4) == 0) | (column == 0)
    starts = starts & inside & ((device_row != full_device) | (column == 0))
    following = jnp.concatenate([starts[:, 1:], jnp.ones((devices, 1), dtype=bool)], axis=1)
    ending = inside & (following | (column + 1 == used[:, None]))
    tails = jax.random.randint(keys[4], (devices, blocks), 1, WINDOW + 1)
    tails = jnp.where(device_row == full_device, WINDOW, tails)
    counts = jnp.where(inside, jnp.where(ending, tails, WINDOW), 0)
    return (counts.reshape(-1).astype(jnp.int32), starts.reshape(-1).astype(jnp.int32))


def draw_block_count(key, part):
    return block_layout(key)[0]


def draw_block_first(key, part):
    return block_layout(key)[1]


def shard_levels(rng, shape, cuts, smallest, high):
    def one(axis_at, blocks):
        heights = jax.random.uniform(jax.random.fold_in(jax.random.fold_in(rng, 6), axis_at), (blocks,), jnp.float32, smallest / len(cuts), high / len(cuts))
        return jnp.repeat(jnp.exp(heights), shape[axis_at] // blocks).reshape((-1,) + (1,) * (len(shape) - axis_at - 1))

    loudness = one(*cuts[0])
    for cut in cuts[1:]:
        loudness = loudness * one(*cut)
    return loudness


def normal_values(stream_key, shape, scale, most, cuts=(), kind=jnp.bfloat16):
    level = shard_levels(stream_key, shape, cuts, -0.22, 0.18) if cuts else 1.0
    drawn = jax.random.normal(stream_key, shape, jnp.float32) * scale * level
    return jnp.minimum(jnp.maximum(drawn, -most), most).astype(kind)


def setup_inputs(seed: int = 0) -> dict:
    seeds = jax.random.split(jax.random.key(seed), 11)
    tokens = normal_values(seeds[0], (TOKENS, D), 1.0, 6.0, ((0, 32),))
    block_count = draw_block_count(jax.random.fold_in(seeds[10], 71), 0)
    block_first = draw_block_first(jax.random.fold_in(seeds[10], 71), 0)
    norm1_gain = jnp.clip(1.0 + 0.1 * jax.random.normal(seeds[3], (D,), jnp.float32), 0.5, 1.5).astype(jnp.bfloat16)
    w_qkv = normal_values(seeds[4], (D, 3, D), (D // 2) ** -0.5, 0.3125, ((0, 8), (2, 4)))
    w_out = normal_values(seeds[5], (D, D), (D // 16) ** -0.5, 0.875, ((0, 4), (1, 8)))
    norm2_gain = jnp.clip(1.0 + 0.1 * jax.random.normal(seeds[6], (D,), jnp.float32), 0.5, 1.5).astype(jnp.bfloat16)
    w_in = normal_values(seeds[7], (D, 2, FF), D ** -0.5, 0.21875, ((0, 8), (2, 4)))
    w_down = normal_values(seeds[8], (FF, D), (FF // 4) ** -0.5, 0.375, ((0, 4), (1, 8)))
    cotangent = normal_values(seeds[9], (TOKENS, D), 1.0, 6.0, ((0, 32),))
    return {"tokens": tokens, "block_count": block_count, "block_first": block_first, "norm1_gain": norm1_gain, "w_qkv": w_qkv, "w_out": w_out, "norm2_gain": norm2_gain, "w_in": w_in, "w_down": w_down, "cotangent": cotangent}


EPS = 1e-05
ROPE_BASE = 10000.0
NEG_FILL = -1e+30

@jax.custom_vjp
def low(v):
    return lax.optimization_barrier(v.astype(jnp.bfloat16)).astype(jnp.float32)

@jax.custom_vjp
def low_back(v):
    return v

def low_keep(v):
    return (low(v), None)

def low_pass(kept, grad):
    return (grad,)

def back_keep(v):
    return (v, None)

def back_low(kept, grad):
    return (low(grad),)
low.defvjp(low_keep, low_pass)
low_back.defvjp(back_keep, back_low)

def matmul(left, right):
    return jnp.dot(left, right, precision=lax.Precision.HIGHEST, preferred_element_type=jnp.float32)

def normalize(values, gain):
    center = lax.optimization_barrier(jnp.mean(values, axis=-1, keepdims=True))
    centred = values - center
    spread = lax.optimization_barrier(jnp.mean(centred * centred, axis=-1, keepdims=True))
    return centred * lax.rsqrt(spread + EPS) * gain

def layout(count, first):
    blocks = count.shape[0]
    total_rows = blocks * WINDOW
    within = jnp.broadcast_to(jnp.arange(WINDOW, dtype=jnp.int32)[None, :], (blocks, WINDOW))
    usable = (within < count[:, None]).reshape(total_rows)
    seq_blocks = jnp.cumsum(first).astype(jnp.int32)
    start_block = lax.cummax(jnp.where(first > 0, jnp.arange(blocks, dtype=jnp.int32), 0), axis=0).astype(jnp.int32)
    seq_ids = jnp.broadcast_to(seq_blocks[:, None], (blocks, WINDOW)).reshape(total_rows)
    offsets = jnp.broadcast_to((start_block * WINDOW)[:, None], (blocks, WINDOW)).reshape(total_rows)
    places = jnp.arange(total_rows, dtype=jnp.int32) - offsets
    return (usable, seq_ids, places)

def rope_tables(places, head_dim):
    freqs = ROPE_BASE ** (-(jnp.arange(head_dim // 2, dtype=jnp.float32) * 2.0) / head_dim)
    angles = places.astype(jnp.float32)[:, None] * freqs[None, :]
    return (jnp.cos(angles)[:, None, :], jnp.sin(angles)[:, None, :])

def rotate(values, cosine, sine):
    middle = values.shape[-1] // 2
    first_half, second_half = (values[..., :middle], values[..., middle:])
    return jnp.concatenate([first_half * cosine - second_half * sine, second_half * cosine + first_half * sine], axis=-1)

def window_mask(start, qrows, usable_pad, seq_pad):
    half = WINDOW // 2
    span = qrows + 2 * half
    query_ok = lax.dynamic_slice_in_dim(usable_pad, start + half, qrows, 0)
    key_ok = lax.dynamic_slice_in_dim(usable_pad, start, span, 0)
    query_seq = lax.dynamic_slice_in_dim(seq_pad, start + half, qrows, 0)
    key_seq = lax.dynamic_slice_in_dim(seq_pad, start, span, 0)
    offset = jnp.arange(qrows, dtype=jnp.int32)[:, None] + half - jnp.arange(span, dtype=jnp.int32)[None, :]
    allowed = (jnp.abs(offset) <= half) & (query_seq[:, None] == key_seq[None, :]) & query_ok[:, None] & key_ok[None, :]
    return (allowed, query_ok)

def attend(query, keys, values, usable, seq_ids):
    total_rows = query.shape[0]
    qrows = min(512, total_rows)
    half = WINDOW // 2
    span = qrows + 2 * half
    scale = HEAD_DIM ** (-0.5)
    keys_pad = jnp.pad(keys, ((half, half), (0, 0), (0, 0)))
    values_pad = jnp.pad(values, ((half, half), (0, 0), (0, 0)))
    usable_pad = jnp.pad(usable, (half, half))
    seq_pad = jnp.pad(seq_ids, (half, half), constant_values=-1)

    def one_block(index):
        start = index * qrows
        query_rows = lax.dynamic_slice_in_dim(query, start, qrows, 0)
        key_rows = lax.dynamic_slice_in_dim(keys_pad, start, span, 0)
        value_rows = lax.dynamic_slice_in_dim(values_pad, start, span, 0)
        allowed, query_ok = window_mask(start, qrows, usable_pad, seq_pad)
        scores = low_back(jnp.einsum('qhd,khd->hqk', query_rows, key_rows, precision=lax.Precision.HIGHEST) * scale)
        masked = jnp.where(allowed[None], scores, NEG_FILL)
        peak = lax.optimization_barrier(jnp.max(masked, axis=-1, keepdims=True))
        raised = jnp.where(allowed[None], jnp.exp(masked - peak), 0.0)
        total = lax.optimization_barrier(jnp.sum(raised, axis=-1, keepdims=True)) + (1.0 - query_ok.astype(jnp.float32))[None, :, None]
        probs = low(raised / total)
        return jnp.einsum('hqk,khd->qhd', probs, value_rows, precision=lax.Precision.HIGHEST)
    pieces = lax.map(jax.checkpoint(one_block), jnp.arange(total_rows // qrows, dtype=jnp.int32))
    return pieces.reshape(total_rows, HEADS, HEAD_DIM)

def layer(inputs, params, usable, seq_ids, places):
    gain_one, qkv_weight, out_weight, gain_two, in_weight, down_weight = params
    total_rows = inputs.shape[0]
    normed_one = low(normalize(inputs, gain_one))
    raw = low_back(matmul(normed_one, qkv_weight.reshape(D, 3 * D))).reshape(total_rows, 3, HEADS, HEAD_DIM)
    cosine, sine = rope_tables(places, HEAD_DIM)
    query = low(rotate(raw[:, 0], cosine, sine))
    keys = low(rotate(raw[:, 1], cosine, sine))
    values = low(raw[:, 2])
    attended = attend(query, keys, values, usable, seq_ids)
    heads_flat = low(low_back(attended)).reshape(total_rows, D)
    residual = inputs + low_back(matmul(heads_flat, out_weight))
    normed_two = low(normalize(residual, gain_two))
    both = matmul(normed_two, in_weight.reshape(D, 2 * FF)).reshape(total_rows, 2, FF)
    gate_pre = low_back(both[:, 0])
    up_pre = low_back(both[:, 1])
    activated = low(jax.nn.gelu(gate_pre, approximate=False) * up_pre)
    return residual + low_back(matmul(activated, down_weight))

def reference(tokens, block_count, block_first, norm1_gain, w_qkv, w_out, norm2_gain, w_in, w_down, cotangent):
    params = (norm1_gain.astype(jnp.float32), w_qkv.astype(jnp.float32), w_out.astype(jnp.float32), norm2_gain.astype(jnp.float32), w_in.astype(jnp.float32), w_down.astype(jnp.float32))
    inputs_all = tokens.astype(jnp.float32).reshape(N_DP, TOK_DEV, D)
    grads_all = cotangent.astype(jnp.float32).reshape(N_DP, TOK_DEV, D)
    counts_all = block_count.reshape(N_DP, BLOCKS)
    firsts_all = block_first.reshape(N_DP, BLOCKS)

    def buffer_step(summed, element):
        inputs, grad_rows, count, first = element
        usable, seq_ids, places = layout(count, first)

        def forward(inputs_in, params_in):
            return layer(inputs_in, params_in, usable, seq_ids, places)
        result, pull = jax.vjp(forward, inputs, params)
        grad_inputs, grad_params = pull(grad_rows)
        summed = jax.tree.map(lambda left, right: left + right, summed, grad_params)
        return (summed, (result.astype(jnp.bfloat16), grad_inputs.astype(jnp.bfloat16)))
    start_sums = jax.tree.map(jnp.zeros_like, params)
    sums, (mixed, input_grad) = lax.scan(buffer_step, start_sums, (inputs_all, grads_all, counts_all, firsts_all))
    return (mixed.reshape(TOKENS, D), input_grad.reshape(TOKENS, D), sums[0], sums[1], sums[2], sums[3], sums[4], sums[5])
```

```python
import functools

import jax
import jax.numpy as jnp
import numpy as np
from jax import lax
from jax.experimental import pallas as pl
from jax.experimental.pallas import tpu as pltpu
from jax.sharding import PartitionSpec as P

HEAD_DIM = 64
WINDOW = 128
EPS = 1e-05
ROPE_BASE = 10000.0
NEG_FILL = -1e30
BF = jnp.bfloat16
F32 = jnp.float32

NN = (((1,), (0,)), ((), ()))
NT = (((1,), (1,)), ((), ()))
TN = (((0,), (0,)), ((), ()))


def dot(left, right, dims=NN):
    return lax.dot_general(left, right, dims, preferred_element_type=F32)


def call(kernel, outs, args, scalars=(), scratch=(), flops=0):
    size = sum(int(np.prod(a.shape)) * a.dtype.itemsize for a in list(args) + list(outs))
    return pl.pallas_call(
        kernel,
        out_shape=tuple(outs),
        in_specs=[pl.BlockSpec(memory_space=pltpu.SMEM)] * len(scalars)
        + [pl.BlockSpec(memory_space=pltpu.VMEM)] * len(args),
        out_specs=tuple(pl.BlockSpec(memory_space=pltpu.VMEM) for _ in outs),
        scratch_shapes=list(scratch),
        compiler_params=pltpu.CompilerParams(vmem_limit_bytes=48 * 1024 * 1024),
        cost_estimate=pl.CostEstimate(flops=flops, bytes_accessed=size, transcendentals=0),
    )(*scalars, *args)


def shape(*dims, dtype=BF):
    return jax.ShapeDtypeStruct(dims, dtype)


def rows_of(index, count=WINDOW):
    return pl.ds(pl.multiple_of(index * count, 16), count)


def normed(values):
    center = jnp.mean(values, axis=-1, keepdims=True)
    centred = values - center
    spread = jnp.mean(centred * centred, axis=-1, keepdims=True)
    scale = lax.rsqrt(spread + EPS)
    return centred * scale, scale


def norm_back(grad, gain, unit, scale):
    scaled = grad * gain
    first = jnp.mean(scaled, axis=-1, keepdims=True)
    second = jnp.mean(scaled * unit, axis=-1, keepdims=True)
    return scale * (scaled - first - unit * second)


def swap_halves(values):
    width = values.shape[1]
    lane = lax.broadcasted_iota(jnp.int32, values.shape, 1)
    return jnp.where(
        lane % HEAD_DIM < HEAD_DIM // 2,
        pltpu.roll(values, width - HEAD_DIM // 2, 1),
        pltpu.roll(values, HEAD_DIM // 2, 1),
    )


def head_lanes(shape_of, head):
    lane = lax.broadcasted_iota(jnp.int32, shape_of, 1)
    return (lane >= head * HEAD_DIM) & (lane < (head + 1) * HEAD_DIM)


def prepare_kernel(ids, first, pair, other, gain, freq, n1, cosine, sine):
    gain_row = gain[...].astype(F32)
    for i in range(4):
        source = pair if i < 2 else other
        unit, _ = normed(source[(i % 2) * WINDOW : (i % 2 + 1) * WINDOW, :].astype(F32))
        n1[rows_of(ids[i]), :] = (unit * gain_row).astype(BF)
    start = jnp.int32(0)
    lane = lax.broadcasted_iota(jnp.int32, (WINDOW, 128), 1)
    sign = jnp.where(lane % HEAD_DIM < HEAD_DIM // 2, -1.0, 1.0)
    for b in range(4):
        start = jnp.where(first[b] > 0, b, start)
        place = lax.broadcasted_iota(jnp.int32, (WINDOW, 128), 0) + (b - start) * WINDOW
        angle = place.astype(F32) * freq[...]
        cosine[b * WINDOW : (b + 1) * WINDOW, :] = jnp.cos(angle)
        sine[b * WINDOW : (b + 1) * WINDOW, :] = jnp.sin(angle) * sign


def put_pieces(ids, offsets, pieces, whole, rows):
    if offsets is None:
        whole[...] = pieces[0][...]
        return
    for offset, piece in zip(offsets, pieces):
        whole[rows_of(jnp.bitwise_xor(ids[4], offset), rows), :] = piece[...]


def attend_kernel(offsets, n_pieces, rows, ids, count, first, n1, cosine, sine, *rest):
    pieces = rest[:n_pieces]
    q_out, k_out, v_out, probs_out, att_out, whole = rest[n_pieces : n_pieces + 6]
    k_pad, v_pad = rest[n_pieces + 6 :]
    put_pieces(ids, offsets, pieces, whole, rows)
    half = WINDOW // 2
    width = q_out.shape[1]
    heads = width // HEAD_DIM
    total_rows = q_out.shape[0]
    blocks = total_rows // WINDOW
    for pad in (k_pad, v_pad):
        pad[0:half, :] = jnp.zeros((half, width), BF)
        pad[half + total_rows :, :] = jnp.zeros((half, width), BF)
    for b in range(blocks):
        rows_b = slice(b * WINDOW, (b + 1) * WINDOW)
        raw = dot(n1[rows_b, :], whole[...])
        c = jnp.concatenate([cosine[rows_b, :]] * 3, axis=1)
        s = jnp.concatenate([sine[rows_b, :]] * 3, axis=1)
        qk = raw[:, : 2 * width]
        turned = (qk * c + swap_halves(qk) * s).astype(BF)
        q_out[rows_b, :] = turned[:, :width]
        k_b = turned[:, width:]
        v_b = raw[:, 2 * width :].astype(BF)
        k_out[rows_b, :] = k_b
        v_out[rows_b, :] = v_b
        k_pad[half + b * WINDOW : half + (b + 1) * WINDOW, :] = k_b
        v_pad[half + b * WINDOW : half + (b + 1) * WINDOW, :] = v_b
    span = 2 * WINDOW
    column = lax.broadcasted_iota(jnp.int32, (WINDOW, span), 1)
    row = lax.broadcasted_iota(jnp.int32, (WINDOW, span), 0)
    near = jnp.abs(row + half - column) <= half
    for b in range(blocks):
        rows_b = slice(b * WINDOW, (b + 1) * WINDOW)
        span_b = slice(b * WINDOW, b * WINDOW + span)
        before = jnp.where(first[b] == 0, count[b - 1], 0) if b > 0 else 0
        after = jnp.where(first[b + 1] == 0, count[b + 1], 0) if b + 1 < blocks else 0
        limit = jnp.where(
            column < half,
            before - half,
            jnp.where(column < half + WINDOW, count[b] + half, after + half + WINDOW),
        )
        allowed = near & (column < limit) & (row < count[b])
        spare = (lax.broadcasted_iota(jnp.int32, (WINDOW, 1), 0) >= count[b]).astype(F32)
        q_b = q_out[rows_b, :]
        keys = k_pad[span_b, :]
        values = v_pad[span_b, :]
        mixed = jnp.zeros((WINDOW, width), F32)
        for h in range(heads):
            mine = head_lanes((WINDOW, width), h)
            scores = dot(jnp.where(mine, q_b, 0), keys, NT) * (HEAD_DIM**-0.5)
            masked = jnp.where(allowed, scores, NEG_FILL)
            peak = jnp.max(masked, axis=-1, keepdims=True)
            raised = jnp.where(allowed, jnp.exp(masked - peak), 0.0)
            total = jnp.sum(raised, axis=-1, keepdims=True) + spare
            probs = (raised * (1.0 / total)).astype(BF)
            probs_out[h, rows_b, :] = probs
            mixed = jnp.where(mine, dot(probs, values), mixed)
        att_out[rows_b, :] = mixed.astype(BF)


def collect_kernel(offsets, n_pieces, rows, widths, ids, *rest):
    pieces = rest[:n_pieces]
    in_w, out_w, down_w = rest[n_pieces:]
    units2, heads_w, units = widths
    for j, piece in enumerate(pieces):
        if offsets is None:
            at = slice(None)
        else:
            at = rows_of(jnp.bitwise_xor(ids[4], offsets[j]), rows)
        value = piece[...]
        in_w[at, :] = value[:, :units2]
        out_w[at, :] = value[:, units2 : units2 + heads_w]
        down_w[at, :] = value[:, units2 + heads_w :]


def project_kernel(ids, att, out_w, send, keep):
    for i in range(4):
        part = dot(att[rows_of(ids[i]), :], out_w[...], NT)
        at = slice((i % 2) * WINDOW, (i % 2 + 1) * WINDOW)
        if i < 2:
            keep[at, :] = part
        else:
            send[at, :] = part.astype(BF)


def middle_kernel(own, received, tokens, gain, h_out, n2_out):
    for i in range(2):
        at = slice(i * WINDOW, (i + 1) * WINDOW)
        back = slice((1 - i) * WINDOW, (2 - i) * WINDOW)
        branch = own[at, :].astype(F32) + received[back, :].astype(F32)
        h = tokens[at, :].astype(F32) + branch
        h_out[at, :] = h
        unit, _ = normed(h)
        n2_out[at, :] = (unit * gain[...].astype(F32)).astype(BF)


def units_kernel(n2, n2_far, gz, gz_far, in_w, down_w, send, keep, both_out, act_out):
    units = act_out.shape[1]
    gate_w, up_w = in_w[:, :units], in_w[:, units:]
    for i in (2, 3, 0, 1):
        at = slice((i % 2) * WINDOW, (i % 2 + 1) * WINDOW)
        rows_n = (n2 if i < 2 else n2_far)[at, :]
        rows_g = (gz if i < 2 else gz_far)[at, :]
        gate = dot(rows_n, gate_w)
        up = dot(rows_n, up_w)
        g_act = dot(rows_g, down_w[...])
        phi = 0.5 * (1.0 + lax.erf(gate * np.float32(np.sqrt(0.5))))
        gelu = gate * phi
        slope = phi + gate * (jnp.exp(-0.5 * gate * gate) * np.float32(1.0 / np.sqrt(2.0 * np.pi)))
        act_out[i * WINDOW : (i + 1) * WINDOW, :] = (gelu * up).astype(BF)
        g_both = jnp.concatenate([g_act * up * slope, g_act * gelu], axis=1).astype(BF)
        both_out[i * WINDOW : (i + 1) * WINDOW, :] = g_both
        part = dot(g_both, in_w[...], NT)
        if i < 2:
            keep[at, :] = part
        else:
            send[at, :] = part.astype(BF)


def emit_slots(ids, slots, rows, total, send, keep):
    for k in range(slots):
        near = jnp.bitwise_xor(ids[4], 2 * k)
        far = jnp.bitwise_xor(ids[4], 2 * k + 1)
        send[k] = total[rows_of(far, rows), :].astype(BF)
        keep[k] = total[rows_of(near, rows), :].astype(BF)


def unit_grads_kernel(
    slots, rows, ids, n2, n2_far, gz, gz_far, both, act, down_w, send, keep, b_send, b_keep, total
):
    pair = 2 * WINDOW
    units2 = both.shape[1]
    in_part = dot(n2[...], both[:pair, :], TN) + dot(n2_far[...], both[pair:, :], TN)
    total[:, :units2] = in_part
    down_part = dot(gz[...], act[:pair, :], TN) + dot(gz_far[...], act[pair:, :], TN)
    total[:, units2:] = down_part
    if slots:
        emit_slots(ids, slots, rows, total, send, keep)
    else:
        send[...] = total[...]
        keep[...] = jnp.zeros(keep.shape, BF)
    b_keep[...] = dot(act[:pair, :], down_w[...], NT)
    b_send[...] = dot(act[pair:, :], down_w[...], NT).astype(BF)


def residual_kernel(own, received, h, cot, gain, gh_out, gy_out, gain_out):
    gain_row = gain[...].astype(F32)
    for i in range(2):
        at = slice(i * WINDOW, (i + 1) * WINDOW)
        back = slice((1 - i) * WINDOW, (2 - i) * WINDOW)
        grad = own[at, :].astype(F32) + received[back, :].astype(F32)
        unit, scale = normed(h[at, :])
        gh = cot[at, :].astype(F32) + norm_back(grad, gain_row, unit, scale)
        gy_out[at, :] = gh.astype(BF)
        if i == 0:
            gh_out[...] = gh
            gain_out[...] = jnp.sum(grad * unit, axis=0, keepdims=True)


def attend_back_kernel(
    slots, rows, ids, gy, gy_far, out_w, att, q_in, k_in, v_in, probs_in, cosine, sine, n1, qkv_w, gain,
    g_send, g_keep, send, keep, gain_out,
    gy_all, k_pad, v_pad, gk_pad, gv_pad, gq_all, g_raw, total,
):
    half = WINDOW // 2
    total_rows, width = q_in.shape
    heads = width // HEAD_DIM
    blocks = total_rows // WINDOW
    span = 2 * WINDOW
    for i in range(4):
        source = gy if i < 2 else gy_far
        gy_all[rows_of(ids[i]), :] = source[(i % 2) * WINDOW : (i % 2 + 1) * WINDOW, :]
    for pad, source in ((k_pad, k_in), (v_pad, v_in)):
        pad[0:half, :] = jnp.zeros((half, width), BF)
        pad[half + total_rows :, :] = jnp.zeros((half, width), BF)
        pad[half : half + total_rows, :] = source[...]
    gk_pad[...] = jnp.zeros(gk_pad.shape, F32)
    gv_pad[...] = jnp.zeros(gv_pad.shape, F32)
    for b in range(blocks):
        rows_b = slice(b * WINDOW, (b + 1) * WINDOW)
        span_b = slice(b * WINDOW, b * WINDOW + span)
        g_att = dot(gy_all[rows_b, :], out_w[...]).astype(BF)
        q_b = q_in[rows_b, :]
        keys = k_pad[span_b, :]
        values = v_pad[span_b, :]
        gq = jnp.zeros((WINDOW, width), F32)
        gk = jnp.zeros((span, width), F32)
        gv = jnp.zeros((span, width), F32)
        for h in range(heads):
            mine = head_lanes((WINDOW, width), h)
            g_mine = jnp.where(mine, g_att, 0)
            probs = probs_in[h, rows_b, :]
            wide = probs.astype(F32)
            g_probs = dot(g_mine, values, NT)
            delta = jnp.sum(wide * g_probs, axis=-1, keepdims=True)
            g_scores = (wide * (g_probs - delta)).astype(BF)
            gq = jnp.where(mine, dot(g_scores, keys), gq)
            gk = gk + dot(g_scores, jnp.where(mine, q_b, 0), TN)
            gv = gv + dot(probs, g_mine, TN)
        gq_all[rows_b, :] = gq
        gk_pad[span_b, :] += gk
        gv_pad[span_b, :] += gv
    scale = HEAD_DIM**-0.5
    columns = 3 * width
    for b in range(blocks):
        rows_b = slice(b * WINDOW, (b + 1) * WINDOW)
        inner = slice(half + b * WINDOW, half + (b + 1) * WINDOW)
        c = jnp.concatenate([cosine[rows_b, :]] * 3, axis=1)
        s = jnp.concatenate([sine[rows_b, :]] * 3, axis=1)
        qk = jnp.concatenate([gq_all[rows_b, :], gk_pad[inner, :]], axis=1) * scale
        turned = qk * c - swap_halves(qk) * s
        g_raw[rows_b, : 2 * width] = turned.astype(BF)
        g_raw[rows_b, 2 * width :] = gv_pad[inner, :].astype(BF)
    total[:, :columns] = dot(n1[...], g_raw[...], TN)
    total[:, columns:] = dot(gy_all[...], att[...], TN)
    if slots:
        emit_slots(ids, slots, rows, total, send, keep)
    else:
        send[...] = total[...]
        keep[...] = jnp.zeros(keep.shape, BF)
    gain_sum = jnp.zeros(gain_out.shape, F32)
    for i in range(4):
        at = slice((i % 2) * WINDOW, (i % 2 + 1) * WINDOW)
        g_n1 = dot(g_raw[rows_of(ids[i]), :], qkv_w[...], NT)
        gain_sum += jnp.sum(g_n1 * n1[rows_of(ids[i]), :].astype(F32), axis=0, keepdims=True)
        if i < 2:
            g_keep[at, :] = g_n1
        else:
            g_send[at, :] = g_n1.astype(BF)
    gain_out[...] = gain_sum / gain[...].astype(F32)


def finish_kernel(
    g_keep, g_core, b_keep, b_core, received, h, tokens, gain, gh, mixed_out, grad_out
):
    gain_row = gain[...].astype(F32)
    grad = g_keep[:WINDOW, :] + g_core[:WINDOW, :].astype(F32) + received[:WINDOW, :].astype(F32)
    unit, scale = normed(tokens[:WINDOW, :].astype(F32))
    grad_out[...] = (gh[...] + norm_back(grad, gain_row, unit, scale)).astype(BF)
    branch = b_keep[:WINDOW, :] + b_core[:WINDOW, :].astype(F32) + received[WINDOW:, :].astype(F32)
    mixed_out[...] = (h[:WINDOW, :] + branch).astype(BF)


def swap(values, axis, bit, size):
    return lax.ppermute(values, axis, [(i, i ^ bit) for i in range(size)])


def local(
    tokens, block_count, block_first, norm1_gain, w_qkv, w_out, norm2_gain, w_in, w_down, cotangent
):
    n_dp = lax.axis_size("dp")
    width = tokens.shape[1]
    shard = width // n_dp
    head_width = w_qkv.shape[2]
    units = w_in.shape[2]
    heads = head_width // HEAD_DIM
    total_rows = block_count.shape[0] * WINDOW
    pair_rows = 2 * WINDOW
    slots = n_dp // 2 if shard % 16 == 0 and n_dp % 2 == 0 and n_dp <= 8 else 0
    place = lax.axis_index("tensor").astype(jnp.int32)
    ids = jnp.stack(
        [place, place ^ 2, place ^ 1, place ^ 3, lax.axis_index("dp").astype(jnp.int32)]
    )
    core = functools.partial(swap, axis="tensor", bit=1, size=4)
    across = functools.partial(swap, axis="tensor", bit=2, size=4)
    dp = functools.partial(swap, axis="dp", size=n_dp)

    def gather(value):
        if not slots:
            return (lax.all_gather(value, "dp", axis=0, tiled=True),), None
        near = [value] + [dp(value, bit=2 * k) for k in range(1, slots)]
        far = [dp(piece, bit=1) for piece in near]
        offsets = [2 * k for k in range(slots)] + [2 * k + 1 for k in range(slots)]
        return tuple(near + far), tuple(offsets)

    def reduce(send, keep):
        if not slots:
            return lax.psum_scatter(send, "dp", scatter_dimension=0, tiled=True)
        part = keep.astype(F32) + dp(send, bit=1).astype(F32)
        rounded = part.astype(BF)
        total = part[0]
        for k in range(1, slots):
            total = total + dp(rounded[k], bit=2 * k).astype(F32)
        return total

    def slot_shapes(columns):
        if not slots:
            return (shape(width, columns, dtype=F32), shape(16, 128))
        return (shape(slots, shard, columns), shape(slots, shard, columns))

    gain_one = norm1_gain.reshape(1, width)
    gain_two = norm2_gain.reshape(1, width)
    freqs = ROPE_BASE ** (-(np.arange(HEAD_DIM // 2, dtype=np.float32) * 2.0) / HEAD_DIM)
    freq = jnp.asarray(np.tile(freqs, 128 // (HEAD_DIM // 2))[None, :], F32)

    qkv_pieces, offsets = gather(w_qkv.reshape(shard, 3 * head_width))
    staged = jnp.stack([tokens, cotangent])
    pair = jnp.concatenate([staged, across(staged)], axis=1)
    other = core(pair)
    own_tokens, own_cot = pair[0], pair[1]
    far_tokens, far_cot = other[0], other[1]
    rest_pieces, _ = gather(
        jnp.concatenate([w_in.reshape(shard, 2 * units), w_out.T, w_down.T], axis=1)
    )

    n1, cosine, sine = call(
        prepare_kernel,
        (shape(total_rows, width), shape(total_rows, 128, dtype=F32), shape(total_rows, 128, dtype=F32)),
        (own_tokens, far_tokens, gain_one, freq),
        (ids, block_first),
    )
    flat = shape(total_rows, head_width)
    query, keys, values, probs, attended, qkv_w = call(
        functools.partial(attend_kernel, offsets, len(qkv_pieces), shard),
        (flat, flat, flat, shape(heads, total_rows, 2 * WINDOW), flat, shape(width, 3 * head_width)),
        (n1, cosine, sine) + qkv_pieces,
        (ids, block_count, block_first),
        [pltpu.VMEM((total_rows + WINDOW, head_width), BF)] * 2,
        flops=2 * total_rows * width * 3 * head_width,
    )
    in_w, out_w, down_w = call(
        functools.partial(
            collect_kernel, offsets, len(rest_pieces), shard, (2 * units, head_width, units)
        ),
        (shape(width, 2 * units), shape(width, head_width), shape(width, units)),
        rest_pieces,
        (ids,),
    )
    pair_f32 = shape(pair_rows, width, dtype=F32)
    pair_bf = shape(pair_rows, width)
    a_send, a_keep = call(
        project_kernel, (pair_bf, pair_f32), (attended, out_w), (ids,),
        flops=2 * total_rows * width * head_width,
    )
    a_sum = (a_keep + core(a_send).astype(F32)).astype(BF)
    h, n2 = call(middle_kernel, (pair_f32, pair_bf), (a_sum, across(a_sum), own_tokens, gain_two))
    n2_far = core(n2)
    u_send, u_keep, both, act = call(
        units_kernel,
        (pair_bf, pair_f32, shape(total_rows, 2 * units), shape(total_rows, units)),
        (n2, n2_far, own_cot, far_cot, in_w, down_w),
        flops=2 * total_rows * width * 5 * units,
    )
    u_sum = (u_keep + core(u_send).astype(F32)).astype(BF)
    u_got = across(u_sum)
    s_shapes = slot_shapes(3 * units)
    in_send, in_keep, b_send, b_keep = call(
        functools.partial(unit_grads_kernel, slots, shard),
        s_shapes + (pair_bf, pair_f32),
        (n2, n2_far, own_cot, far_cot, both, act, down_w),
        (ids,),
        [pltpu.VMEM((width, 3 * units), F32)],
        flops=2 * total_rows * width * 4 * units,
    )
    b_core = core(b_send)
    unit_grads = reduce(in_send, in_keep)
    gh, gy, gain_part_two = call(
        residual_kernel,
        (shape(WINDOW, width, dtype=F32), pair_bf, shape(1, width, dtype=F32)),
        (u_sum, u_got, h, own_cot, gain_two),
    )
    gy_far = core(gy)
    g_send, g_keep, att_send, att_keep, gain_part_one = call(
        functools.partial(attend_back_kernel, slots, shard),
        (pair_bf, pair_f32) + slot_shapes(4 * head_width) + (shape(1, width, dtype=F32),),
        (gy, gy_far, out_w, attended, query, keys, values, probs, cosine, sine, n1, qkv_w, gain_one),
        (ids,),
        [
            pltpu.VMEM((total_rows, width), BF),
            pltpu.VMEM((total_rows + WINDOW, head_width), BF),
            pltpu.VMEM((total_rows + WINDOW, head_width), BF),
            pltpu.VMEM((total_rows + WINDOW, head_width), F32),
            pltpu.VMEM((total_rows + WINDOW, head_width), F32),
            pltpu.VMEM((total_rows, head_width), F32),
            pltpu.VMEM((total_rows, 3 * head_width), BF),
            pltpu.VMEM((width, 4 * head_width), F32),
        ],
        flops=2 * total_rows * width * 8 * head_width,
    )
    att_grads = reduce(att_send, att_keep)
    g_core = core(g_send)
    back = jnp.concatenate(
        [
            (g_keep[WINDOW:] + g_core[WINDOW:].astype(F32)).astype(BF),
            (b_keep[WINDOW:] + b_core[WINDOW:].astype(F32)).astype(BF),
        ],
        axis=0,
    )
    mixed, input_grad = call(
        finish_kernel,
        (shape(WINDOW, width), shape(WINDOW, width)),
        (g_keep, g_core, b_keep, b_core, across(back), h, own_tokens, gain_one, gh),
    )
    gains = jnp.concatenate([gain_part_one, gain_part_two], axis=0)
    if slots:
        gains = gains + core(gains)
        gains = gains + across(gains)
        gains = gains + dp(gains, bit=1)
        total = gains
        for k in range(1, slots):
            total = total + dp(gains, bit=2 * k)
        gains = total
    else:
        gains = lax.psum(gains, ("dp", "tensor"))
    columns = 3 * head_width
    return (
        mixed,
        input_grad,
        gains[0],
        att_grads[:, :columns].reshape(shard, 3, head_width),
        att_grads[:, columns:].T,
        gains[1],
        unit_grads[:, : 2 * units].reshape(shard, 2, units),
        unit_grads[:, 2 * units :].T,
    )


def solution(mesh):
    return jax.shard_map(
        local,
        mesh=mesh,
        in_specs=(
            P(("dp", "tensor"), None),
            P("dp"),
            P("dp"),
            P(),
            P("dp", None, "tensor"),
            P("tensor", "dp"),
            P(),
            P("dp", None, "tensor"),
            P("tensor", "dp"),
            P(("dp", "tensor"), None),
        ),
        out_specs=(
            P(("dp", "tensor"), None),
            P(("dp", "tensor"), None),
            P(),
            P("dp", None, "tensor"),
            P("tensor", "dp"),
            P(),
            P("dp", None, "tensor"),
            P("tensor", "dp"),
        ),
        check_vma=False,
    )
```

```python
import functools

import jax
import jax.numpy as jnp
import numpy as np
from jax import lax
from jax.experimental import pallas as pl
from jax.experimental.pallas import tpu as pltpu
from jax.sharding import PartitionSpec as P

HEAD_DIM = 64
WINDOW = 128
EPS = 1e-05
ROPE_BASE = 10000.0
NEG_FILL = -1e30
BF = jnp.bfloat16
F32 = jnp.float32

NN = (((1,), (0,)), ((), ()))
NT = (((1,), (1,)), ((), ()))
TN = (((0,), (0,)), ((), ()))


def dot(left, right, dims=NN):
    return lax.dot_general(left, right, dims, preferred_element_type=F32)


def call(kernel, outs, args, scalars=(), scratch=(), flops=0):
    size = sum(int(np.prod(a.shape)) * a.dtype.itemsize for a in list(args) + list(outs))
    return pl.pallas_call(
        kernel,
        out_shape=tuple(outs),
        in_specs=[pl.BlockSpec(memory_space=pltpu.SMEM)] * len(scalars)
        + [pl.BlockSpec(memory_space=pltpu.VMEM)] * len(args),
        out_specs=tuple(pl.BlockSpec(memory_space=pltpu.VMEM) for _ in outs),
        scratch_shapes=list(scratch),
        compiler_params=pltpu.CompilerParams(vmem_limit_bytes=48 * 1024 * 1024),
        cost_estimate=pl.CostEstimate(flops=flops, bytes_accessed=size, transcendentals=0),
    )(*scalars, *args)


def shape(*dims, dtype=BF):
    return jax.ShapeDtypeStruct(dims, dtype)


def rows_of(index, count=WINDOW):
    return pl.ds(pl.multiple_of(index * count, 16), count)


def normed(values):
    center = jnp.mean(values, axis=-1, keepdims=True)
    centred = values - center
    spread = jnp.mean(centred * centred, axis=-1, keepdims=True)
    scale = lax.rsqrt(spread + EPS)
    return centred * scale, scale


def norm_back(grad, gain, unit, scale):
    scaled = grad * gain
    first = jnp.mean(scaled, axis=-1, keepdims=True)
    second = jnp.mean(scaled * unit, axis=-1, keepdims=True)
    return scale * (scaled - first - unit * second)


def swap_halves(values):
    width = values.shape[1]
    lane = lax.broadcasted_iota(jnp.int32, values.shape, 1)
    return jnp.where(
        lane % HEAD_DIM < HEAD_DIM // 2,
        pltpu.roll(values, width - HEAD_DIM // 2, 1),
        pltpu.roll(values, HEAD_DIM // 2, 1),
    )


def head_lanes(shape_of, head):
    lane = lax.broadcasted_iota(jnp.int32, shape_of, 1)
    return (lane >= head * HEAD_DIM) & (lane < (head + 1) * HEAD_DIM)


def prepare_kernel(ids, first, t0, t1, t2, t3, gain, freq, n1, cosine, sine):
    gain_row = gain[...].astype(F32)
    for i, source in enumerate((t0, t1, t2, t3)):
        unit, _ = normed(source[...].astype(F32))
        n1[rows_of(ids[i]), :] = (unit * gain_row).astype(BF)
    start = jnp.int32(0)
    lane = lax.broadcasted_iota(jnp.int32, (WINDOW, 128), 1)
    sign = jnp.where(lane % HEAD_DIM < HEAD_DIM // 2, -1.0, 1.0)
    for b in range(4):
        start = jnp.where(first[b] > 0, b, start)
        place = lax.broadcasted_iota(jnp.int32, (WINDOW, 128), 0) + (b - start) * WINDOW
        angle = place.astype(F32) * freq[...]
        cosine[b * WINDOW : (b + 1) * WINDOW, :] = jnp.cos(angle)
        sine[b * WINDOW : (b + 1) * WINDOW, :] = jnp.sin(angle) * sign


def put_pieces(ids, offsets, pieces, whole, rows):
    if offsets is None:
        whole[...] = pieces[0][...]
        return
    for offset, piece in zip(offsets, pieces):
        whole[rows_of(jnp.bitwise_xor(ids[4], offset), rows), :] = piece[...]


def attend_kernel(offsets, n_pieces, rows, ids, count, first, n1, cosine, sine, *rest):
    pieces = rest[:n_pieces]
    q_out, k_out, v_out, probs_out, att_out, whole = rest[n_pieces : n_pieces + 6]
    k_pad, v_pad = rest[n_pieces + 6 :]
    put_pieces(ids, offsets, pieces, whole, rows)
    half = WINDOW // 2
    width = q_out.shape[1]
    heads = width // HEAD_DIM
    total_rows = q_out.shape[0]
    blocks = total_rows // WINDOW
    for pad in (k_pad, v_pad):
        pad[0:half, :] = jnp.zeros((half, width), BF)
        pad[half + total_rows :, :] = jnp.zeros((half, width), BF)
    for b in range(blocks):
        rows_b = slice(b * WINDOW, (b + 1) * WINDOW)
        raw = dot(n1[rows_b, :], whole[...])
        c = jnp.concatenate([cosine[rows_b, :]] * 3, axis=1)
        s = jnp.concatenate([sine[rows_b, :]] * 3, axis=1)
        qk = raw[:, : 2 * width]
        turned = (qk * c + swap_halves(qk) * s).astype(BF)
        q_out[rows_b, :] = turned[:, :width]
        k_b = turned[:, width:]
        v_b = raw[:, 2 * width :].astype(BF)
        k_out[rows_b, :] = k_b
        v_out[rows_b, :] = v_b
        k_pad[half + b * WINDOW : half + (b + 1) * WINDOW, :] = k_b
        v_pad[half + b * WINDOW : half + (b + 1) * WINDOW, :] = v_b
    span = 2 * WINDOW
    column = lax.broadcasted_iota(jnp.int32, (WINDOW, span), 1)
    row = lax.broadcasted_iota(jnp.int32, (WINDOW, span), 0)
    near = jnp.abs(row + half - column) <= half
    for b in range(blocks):
        rows_b = slice(b * WINDOW, (b + 1) * WINDOW)
        span_b = slice(b * WINDOW, b * WINDOW + span)
        before = jnp.where(first[b] == 0, count[b - 1], 0) if b > 0 else 0
        after = jnp.where(first[b + 1] == 0, count[b + 1], 0) if b + 1 < blocks else 0
        limit = jnp.where(
            column < half,
            before - half,
            jnp.where(column < half + WINDOW, count[b] + half, after + half + WINDOW),
        )
        allowed = near & (column < limit) & (row < count[b])
        spare = (lax.broadcasted_iota(jnp.int32, (WINDOW, 1), 0) >= count[b]).astype(F32)
        q_b = q_out[rows_b, :]
        keys = k_pad[span_b, :]
        values = v_pad[span_b, :]
        mixed = jnp.zeros((WINDOW, width), F32)
        for h in range(heads):
            mine = head_lanes((WINDOW, width), h)
            scores = dot(jnp.where(mine, q_b, 0), keys, NT) * (HEAD_DIM**-0.5)
            masked = jnp.where(allowed, scores, NEG_FILL)
            peak = jnp.max(masked, axis=-1, keepdims=True)
            raised = jnp.where(allowed, jnp.exp(masked - peak), 0.0)
            total = jnp.sum(raised, axis=-1, keepdims=True) + spare
            probs = (raised * (1.0 / total)).astype(BF)
            probs_out[h, rows_b, :] = probs
            mixed = jnp.where(mine, dot(probs, values), mixed)
        att_out[rows_b, :] = mixed.astype(BF)


def collect_kernel(offsets, n_pieces, rows, units2, ids, *rest):
    pieces = rest[:n_pieces]
    in_w, down_w = rest[n_pieces:]
    for j, piece in enumerate(pieces):
        if offsets is None:
            at = slice(None)
        else:
            at = rows_of(jnp.bitwise_xor(ids[4], offsets[j]), rows)
        value = piece[...]
        in_w[at, :] = value[:, :units2]
        down_w[at, :] = value[:, units2:]


def project_kernel(offsets, n_pieces, rows, ids, att, *rest):
    pieces = rest[:n_pieces]
    send, keep, out_w = rest[n_pieces:]
    put_pieces(ids, offsets, pieces, out_w, rows)
    for i in range(4):
        part = dot(att[rows_of(ids[i]), :], out_w[...], NT)
        at = slice((i % 2) * WINDOW, (i % 2 + 1) * WINDOW)
        if i < 2:
            keep[at, :] = part
        else:
            send[at, :] = part.astype(BF)


def middle_kernel(own, received, t0, t1, gain, h_out, n2_out):
    for i, tokens in enumerate((t0, t1)):
        at = slice(i * WINDOW, (i + 1) * WINDOW)
        back = slice((1 - i) * WINDOW, (2 - i) * WINDOW)
        branch = own[at, :].astype(F32) + received[back, :].astype(F32)
        h = tokens[...].astype(F32) + branch
        h_out[at, :] = h
        unit, _ = normed(h)
        n2_out[at, :] = (unit * gain[...].astype(F32)).astype(BF)


def units_kernel(n2, n2_far, c0, c1, c2, c3, in_w, down_w, send, keep, both_out, act_out):
    units = act_out.shape[1]
    gate_w, up_w = in_w[:, :units], in_w[:, units:]
    for i in (2, 3, 0, 1):
        at = slice((i % 2) * WINDOW, (i % 2 + 1) * WINDOW)
        rows_n = (n2 if i < 2 else n2_far)[at, :]
        rows_g = (c0, c1, c2, c3)[i][...]
        gate = dot(rows_n, gate_w)
        up = dot(rows_n, up_w)
        g_act = dot(rows_g, down_w[...])
        phi = 0.5 * (1.0 + lax.erf(gate * np.float32(np.sqrt(0.5))))
        gelu = gate * phi
        slope = phi + gate * (jnp.exp(-0.5 * gate * gate) * np.float32(1.0 / np.sqrt(2.0 * np.pi)))
        act_out[i * WINDOW : (i + 1) * WINDOW, :] = (gelu * up).astype(BF)
        g_both = jnp.concatenate([g_act * up * slope, g_act * gelu], axis=1).astype(BF)
        both_out[i * WINDOW : (i + 1) * WINDOW, :] = g_both
        part = dot(g_both, in_w[...], NT)
        if i < 2:
            keep[at, :] = part
        else:
            send[at, :] = part.astype(BF)


def emit_slots(ids, slots, rows, total, send, keep):
    for k in range(slots):
        near = jnp.bitwise_xor(ids[4], 2 * k)
        far = jnp.bitwise_xor(ids[4], 2 * k + 1)
        send[k] = total[rows_of(far, rows), :].astype(BF)
        keep[k] = total[rows_of(near, rows), :].astype(BF)


def unit_grads_kernel(
    slots, rows, ids, n2, n2_far, c0, c1, c2, c3, both, act, down_w, send, keep, b_send, b_keep, total
):
    pair = 2 * WINDOW
    units2 = both.shape[1]
    in_part = dot(n2[...], both[:pair, :], TN) + dot(n2_far[...], both[pair:, :], TN)
    total[:, :units2] = in_part
    gz = jnp.concatenate([c0[...], c1[...], c2[...], c3[...]], axis=0)
    down_part = dot(gz, act[...], TN)
    total[:, units2:] = down_part
    if slots:
        emit_slots(ids, slots, rows, total, send, keep)
    else:
        send[...] = total[...]
        keep[...] = jnp.zeros(keep.shape, BF)
    b_keep[...] = dot(act[:pair, :], down_w[...], NT)
    b_send[...] = dot(act[pair:, :], down_w[...], NT).astype(BF)


def residual_kernel(own, received, h, c0, c1, gain, gh_out, gy_out, gain_out):
    gain_row = gain[...].astype(F32)
    for i, cot in enumerate((c0, c1)):
        at = slice(i * WINDOW, (i + 1) * WINDOW)
        back = slice((1 - i) * WINDOW, (2 - i) * WINDOW)
        grad = own[at, :].astype(F32) + received[back, :].astype(F32)
        unit, scale = normed(h[at, :])
        gh = cot[...].astype(F32) + norm_back(grad, gain_row, unit, scale)
        gy_out[at, :] = gh.astype(BF)
        if i == 0:
            gh_out[...] = gh
            gain_out[...] = jnp.sum(grad * unit, axis=0, keepdims=True)


def attend_back_kernel(
    ids, gy, gy_far, out_w, q_in, k_in, v_in, probs_in, cosine, sine,
    g_raw,
    g_att_all, k_pad, v_pad, gk_pad, gv_pad, gq_all,
):
    half = WINDOW // 2
    total_rows, width = q_in.shape
    heads = width // HEAD_DIM
    blocks = total_rows // WINDOW
    span = 2 * WINDOW
    for i in range(4):
        source = gy if i < 2 else gy_far
        part = dot(source[(i % 2) * WINDOW : (i % 2 + 1) * WINDOW, :], out_w[...])
        g_att_all[rows_of(ids[i]), :] = part.astype(BF)
    for pad, source in ((k_pad, k_in), (v_pad, v_in)):
        pad[0:half, :] = jnp.zeros((half, width), BF)
        pad[half + total_rows :, :] = jnp.zeros((half, width), BF)
        pad[half : half + total_rows, :] = source[...]
    gk_pad[...] = jnp.zeros(gk_pad.shape, F32)
    gv_pad[...] = jnp.zeros(gv_pad.shape, F32)
    for b in range(blocks):
        rows_b = slice(b * WINDOW, (b + 1) * WINDOW)
        span_b = slice(b * WINDOW, b * WINDOW + span)
        g_att = g_att_all[rows_b, :]
        q_b = q_in[rows_b, :]
        keys = k_pad[span_b, :]
        values = v_pad[span_b, :]
        gq = jnp.zeros((WINDOW, width), F32)
        gk = jnp.zeros((span, width), F32)
        gv = jnp.zeros((span, width), F32)
        for h in range(heads):
            mine = head_lanes((WINDOW, width), h)
            g_mine = jnp.where(mine, g_att, 0)
            probs = probs_in[h, rows_b, :]
            wide = probs.astype(F32)
            g_probs = dot(g_mine, values, NT)
            delta = jnp.sum(wide * g_probs, axis=-1, keepdims=True)
            g_scores = (wide * (g_probs - delta)).astype(BF)
            gq = jnp.where(mine, dot(g_scores, keys), gq)
            gk = gk + dot(g_scores, jnp.where(mine, q_b, 0), TN)
            gv = gv + dot(probs, g_mine, TN)
        gq_all[rows_b, :] = gq
        gk_pad[span_b, :] += gk
        gv_pad[span_b, :] += gv
    scale = HEAD_DIM**-0.5
    for b in range(blocks):
        rows_b = slice(b * WINDOW, (b + 1) * WINDOW)
        inner = slice(half + b * WINDOW, half + (b + 1) * WINDOW)
        c = jnp.concatenate([cosine[rows_b, :]] * 3, axis=1)
        s = jnp.concatenate([sine[rows_b, :]] * 3, axis=1)
        qk = jnp.concatenate([gq_all[rows_b, :], gk_pad[inner, :]], axis=1) * scale
        turned = qk * c - swap_halves(qk) * s
        g_raw[rows_b, : 2 * width] = turned.astype(BF)
        g_raw[rows_b, 2 * width :] = gv_pad[inner, :].astype(BF)


def attend_grads_kernel(slots, rows, ids, n1, g_raw, gy, gy_far, att, send, keep, total):
    columns = g_raw.shape[1]
    total[:, :columns] = dot(n1[...], g_raw[...], TN)
    near = jnp.concatenate([att[rows_of(ids[i]), :] for i in (0, 1)], axis=0)
    far = jnp.concatenate([att[rows_of(ids[i]), :] for i in (2, 3)], axis=0)
    total[:, columns:] = dot(gy[...], near, TN) + dot(gy_far[...], far, TN)
    if slots:
        emit_slots(ids, slots, rows, total, send, keep)
    else:
        send[...] = total[...]
        keep[...] = jnp.zeros(keep.shape, BF)


def first_back_kernel(ids, g_raw, qkv_w, n1, gain, gain_two, g_send, g_keep, gains):
    gain_sum = jnp.zeros(gain_two.shape, F32)
    for i in (2, 3, 0, 1):
        at = slice((i % 2) * WINDOW, (i % 2 + 1) * WINDOW)
        g_n1 = dot(g_raw[rows_of(ids[i]), :], qkv_w[...], NT)
        gain_sum += jnp.sum(g_n1 * n1[rows_of(ids[i]), :].astype(F32), axis=0, keepdims=True)
        if i < 2:
            g_keep[at, :] = g_n1
        else:
            g_send[at, :] = g_n1.astype(BF)
    gains[0:1, :] = gain_sum / gain[...].astype(F32)
    gains[1:2, :] = gain_two[...]


def merge_kernel(keep, got, first, *others):
    first[...] = keep[0].astype(F32) + got[0].astype(F32)
    for k, other in enumerate(others):
        other[...] = (keep[k + 1].astype(F32) + got[k + 1].astype(F32)).astype(BF)


def deliver_kernel(first, *rest):
    wide, turned = rest[-2:]
    total = first[...]
    for part in rest[:-2]:
        total = total + part[...].astype(F32)
    _, count, width = wide.shape
    for j in range(count):
        wide[:, j, :] = total[:, j * width : (j + 1) * width]
    turned[...] = total[:, count * width :].T


def finish_kernel(
    g_keep, g_core, b_keep, b_core, received, h, tokens, gain, gh, mixed_out, grad_out
):
    gain_row = gain[...].astype(F32)
    grad = g_keep[:WINDOW, :] + g_core[:WINDOW, :].astype(F32) + received[:WINDOW, :].astype(F32)
    unit, scale = normed(tokens[...].astype(F32))
    grad_out[...] = (gh[...] + norm_back(grad, gain_row, unit, scale)).astype(BF)
    branch = b_keep[:WINDOW, :] + b_core[:WINDOW, :].astype(F32) + received[WINDOW:, :].astype(F32)
    mixed_out[...] = (h[:WINDOW, :] + branch).astype(BF)


def swap(values, axis, bit, size):
    return lax.ppermute(values, axis, [(i, i ^ bit) for i in range(size)])


def local(
    tokens, block_count, block_first, norm1_gain, w_qkv, w_out, norm2_gain, w_in, w_down, cotangent
):
    n_dp = lax.axis_size("dp")
    width = tokens.shape[1]
    shard = width // n_dp
    head_width = w_qkv.shape[2]
    units = w_in.shape[2]
    heads = head_width // HEAD_DIM
    total_rows = block_count.shape[0] * WINDOW
    pair_rows = 2 * WINDOW
    slots = n_dp // 2 if shard % 16 == 0 and n_dp % 2 == 0 and n_dp <= 8 else 0
    place = lax.axis_index("tensor").astype(jnp.int32)
    ids = jnp.stack(
        [place, place ^ 2, place ^ 1, place ^ 3, lax.axis_index("dp").astype(jnp.int32)]
    )
    core = functools.partial(swap, axis="tensor", bit=1, size=4)
    across = functools.partial(swap, axis="tensor", bit=2, size=4)
    dp = functools.partial(swap, axis="dp", size=n_dp)

    def along(value):
        if not slots:
            return [lax.all_gather(value, "dp", axis=0, tiled=True)]
        return [dp(value, bit=2 * k) for k in range(1, slots)]

    def aside(pieces):
        if not slots:
            return []
        return list(dp(jnp.stack(pieces), bit=1))

    def picked(own, near, far):
        return (own, *near, *far) if slots else tuple(near)

    def merge(keep, got):
        _, rows, columns = keep.shape
        return call(
            merge_kernel,
            (shape(rows, columns, dtype=F32),) + (shape(rows, columns),) * (slots - 1),
            (keep, got),
        )

    def deliver(parts, count):
        columns = parts[0].shape[1]
        each = columns // (count + 1)
        if not slots:
            total = parts[0]
            return total[:, : count * each].reshape(shard, count, each), total[:, count * each :].T
        return call(
            deliver_kernel,
            (shape(shard, count, each, dtype=F32), shape(each, shard, dtype=F32)),
            parts,
        )

    def slot_shapes(columns):
        if not slots:
            return (shape(width, columns, dtype=F32), shape(16, 128))
        return (shape(slots, shard, columns), shape(slots, shard, columns))

    gain_one = norm1_gain.reshape(1, width)
    gain_two = norm2_gain.reshape(1, width)
    freqs = ROPE_BASE ** (-(np.arange(HEAD_DIM // 2, dtype=np.float32) * 2.0) / HEAD_DIM)
    freq = jnp.asarray(np.tile(freqs, 128 // (HEAD_DIM // 2))[None, :], F32)

    offsets = tuple(range(0, n_dp, 2)) + tuple(range(1, n_dp, 2)) if slots else None
    pin = lax.optimization_barrier

    qkv_own = w_qkv.reshape(shard, 3 * head_width)
    qkv_near = along(qkv_own)
    token_blocks = [tokens, across(tokens), core(tokens)]
    token_blocks.append(core(token_blocks[1]))
    n1, cosine, sine = call(
        prepare_kernel,
        (shape(total_rows, width), shape(total_rows, 128, dtype=F32), shape(total_rows, 128, dtype=F32)),
        tuple(token_blocks) + (gain_one, freq),
        (ids, block_first),
    )
    out_own = w_out.T
    unit_own = jnp.concatenate([w_in.reshape(shard, 2 * units), w_down.T], axis=1)
    qkv_near, n1, out_own, unit_own, cot = pin((qkv_near, n1, out_own, unit_own, cotangent))
    qkv_far = aside([qkv_own] + qkv_near)
    out_near = along(out_own)
    unit_near = along(unit_own)
    cot_blocks = [cotangent, across(cot), core(cot)]
    cot_blocks.append(core(cot_blocks[1]))
    cot_blocks = tuple(cot_blocks)
    qkv_pieces = picked(qkv_own, qkv_near, qkv_far)
    out_near, _ = pin((out_near, qkv_far))
    out_far = aside([out_own] + out_near)
    out_pieces = picked(out_own, out_near, out_far)
    flat = shape(total_rows, head_width)
    query, keys, values, probs, attended, qkv_w = call(
        functools.partial(attend_kernel, offsets, len(qkv_pieces), shard),
        (flat, flat, flat, shape(heads, total_rows, 2 * WINDOW), flat, shape(width, 3 * head_width)),
        (n1, cosine, sine) + qkv_pieces,
        (ids, block_count, block_first),
        [pltpu.VMEM((total_rows + WINDOW, head_width), BF)] * 2,
        flops=2 * total_rows * width * 3 * head_width,
    )
    attended, unit_near, out_pieces = pin((attended, unit_near, out_pieces))
    unit_far = aside([unit_own] + unit_near)
    unit_pieces = picked(unit_own, unit_near, unit_far)
    in_w, down_w = call(
        functools.partial(collect_kernel, offsets, len(unit_pieces), shard, 2 * units),
        (shape(width, 2 * units), shape(width, units)),
        unit_pieces,
        (ids,),
    )
    pair_f32 = shape(pair_rows, width, dtype=F32)
    pair_bf = shape(pair_rows, width)
    a_send, a_keep, out_w = call(
        functools.partial(project_kernel, offsets, len(out_pieces), shard),
        (pair_bf, pair_f32, shape(width, head_width)),
        (attended,) + out_pieces,
        (ids,),
        flops=2 * total_rows * width * head_width,
    )
    a_sum = (a_keep + core(a_send).astype(F32)).astype(BF)
    h, n2 = call(
        middle_kernel,
        (pair_f32, pair_bf),
        (a_sum, across(a_sum), token_blocks[0], token_blocks[1], gain_two),
    )
    n2_far = core(n2)
    u_send, u_keep, both, act = call(
        units_kernel,
        (pair_bf, pair_f32, shape(total_rows, 2 * units), shape(total_rows, units)),
        (n2, n2_far) + cot_blocks + (in_w, down_w),
        flops=2 * total_rows * width * 5 * units,
    )
    u_sum = (u_keep + core(u_send).astype(F32)).astype(BF)
    u_got = across(u_sum)
    s_shapes = slot_shapes(3 * units)
    in_send, in_keep, b_send, b_keep = call(
        functools.partial(unit_grads_kernel, slots, shard),
        s_shapes + (pair_bf, pair_f32),
        (n2, n2_far) + cot_blocks + (both, act, down_w),
        (ids,),
        [pltpu.VMEM((width, 3 * units), F32)],
        flops=2 * total_rows * width * 4 * units,
    )
    b_core = core(b_send)
    if slots:
        in_parts = merge(in_keep, dp(in_send, bit=1))
    gh, gy, gain_part_two = call(
        residual_kernel,
        (shape(WINDOW, width, dtype=F32), pair_bf, shape(1, width, dtype=F32)),
        (u_sum, u_got, h, cot_blocks[0], cot_blocks[1], gain_two),
    )
    gy_far = core(gy)
    (g_raw,) = call(
        attend_back_kernel,
        (shape(total_rows, 3 * head_width),),
        (gy, gy_far, out_w, query, keys, values, probs, cosine, sine),
        (ids,),
        [
            pltpu.VMEM((total_rows, head_width), BF),
            pltpu.VMEM((total_rows + WINDOW, head_width), BF),
            pltpu.VMEM((total_rows + WINDOW, head_width), BF),
            pltpu.VMEM((total_rows + WINDOW, head_width), F32),
            pltpu.VMEM((total_rows + WINDOW, head_width), F32),
            pltpu.VMEM((total_rows, head_width), F32),
        ],
        flops=2 * total_rows * width * 3 * head_width,
    )
    att_send, att_keep = call(
        functools.partial(attend_grads_kernel, slots, shard),
        slot_shapes(4 * head_width),
        (n1, g_raw, gy, gy_far, attended),
        (ids,),
        [pltpu.VMEM((width, 4 * head_width), F32)],
        flops=2 * total_rows * width * 4 * head_width,
    )
    g_send, g_keep, gains = call(
        first_back_kernel,
        (pair_bf, pair_f32, shape(2, width, dtype=F32)),
        (g_raw, qkv_w, n1, gain_one, gain_part_two),
        (ids,),
        flops=2 * total_rows * width * 3 * head_width,
    )
    g_core = core(g_send)
    back = jnp.concatenate(
        [
            (g_keep[WINDOW:] + g_core[WINDOW:].astype(F32)).astype(BF),
            (b_keep[WINDOW:] + b_core[WINDOW:].astype(F32)).astype(BF),
        ],
        axis=0,
    )
    mixed, input_grad = call(
        finish_kernel,
        (shape(WINDOW, width), shape(WINDOW, width)),
        (g_keep, g_core, b_keep, b_core, across(back), h, tokens, gain_one, gh),
    )
    if slots:
        att_got = dp(att_send, bit=1)
        in_parts = (in_parts[0], *(dp(in_parts[k], bit=2 * k) for k in range(1, slots)))
        gains = gains + core(gains)
        gains = gains + across(gains)
        gains = gains + dp(gains, bit=1)
        att_got, gains, in_parts = pin((att_got, gains, in_parts))
        att_parts = merge(att_keep, att_got)
        att_parts = (att_parts[0], *(dp(att_parts[k], bit=2 * k) for k in range(1, slots)))
        for part in [dp(gains, bit=2 * k) for k in range(1, slots)]:
            gains = gains + part
    else:
        gains = lax.psum(gains, ("dp", "tensor"))
        in_parts = (lax.psum_scatter(in_send, "dp", scatter_dimension=0, tiled=True),)
        att_parts = (lax.psum_scatter(att_send, "dp", scatter_dimension=0, tiled=True),)
    in_grad, down_grad = deliver(in_parts, 2)
    att_parts, mixed, input_grad, in_grad, down_grad = pin(
        (att_parts, mixed, input_grad, in_grad, down_grad)
    )
    qkv_grad, out_grad = deliver(att_parts, 3)
    return (mixed, input_grad, gains[0], qkv_grad, out_grad, gains[1], in_grad, down_grad)


def solution(mesh):
    return jax.shard_map(
        local,
        mesh=mesh,
        in_specs=(
            P(("dp", "tensor"), None),
            P("dp"),
            P("dp"),
            P(),
            P("dp", None, "tensor"),
            P("tensor", "dp"),
            P(),
            P("dp", None, "tensor"),
            P("tensor", "dp"),
            P(("dp", "tensor"), None),
        ),
        out_specs=(
            P(("dp", "tensor"), None),
            P(("dp", "tensor"), None),
            P(),
            P("dp", None, "tensor"),
            P("tensor", "dp"),
            P(),
            P("dp", None, "tensor"),
            P("tensor", "dp"),
        ),
        check_vma=False,
    )
```

```python
import functools

import jax
import jax.numpy as jnp
import numpy as np
from jax import lax
from jax.experimental import pallas as pl
from jax.experimental.pallas import tpu as pltpu
from jax.sharding import PartitionSpec as P

HEAD_DIM = 64
WINDOW = 128
EPS = 1e-05
ROPE_BASE = 10000.0
NEG_FILL = -1e30
BF = jnp.bfloat16
F32 = jnp.float32

NN = (((1,), (0,)), ((), ()))
NT = (((1,), (1,)), ((), ()))
TN = (((0,), (0,)), ((), ()))


def dot(left, right, dims=NN):
    return lax.dot_general(left, right, dims, preferred_element_type=F32)


def call(kernel, outs, args, scalars=(), scratch=(), flops=0):
    size = sum(int(np.prod(a.shape)) * a.dtype.itemsize for a in list(args) + list(outs))
    return pl.pallas_call(
        kernel,
        out_shape=tuple(outs),
        in_specs=[pl.BlockSpec(memory_space=pltpu.SMEM)] * len(scalars)
        + [pl.BlockSpec(memory_space=pltpu.VMEM)] * len(args),
        out_specs=tuple(pl.BlockSpec(memory_space=pltpu.VMEM) for _ in outs),
        scratch_shapes=list(scratch),
        compiler_params=pltpu.CompilerParams(vmem_limit_bytes=48 * 1024 * 1024),
        cost_estimate=pl.CostEstimate(flops=1, bytes_accessed=1, transcendentals=0),
    )(*scalars, *args)


def shape(*dims, dtype=BF):
    return jax.ShapeDtypeStruct(dims, dtype)


def rows_of(index, count=WINDOW):
    return pl.ds(pl.multiple_of(index * count, 16), count)


def normed(values):
    center = jnp.mean(values, axis=-1, keepdims=True)
    centred = values - center
    spread = jnp.mean(centred * centred, axis=-1, keepdims=True)
    scale = lax.rsqrt(spread + EPS)
    return centred * scale, scale


def norm_back(grad, gain, unit, scale):
    scaled = grad * gain
    first = jnp.mean(scaled, axis=-1, keepdims=True)
    second = jnp.mean(scaled * unit, axis=-1, keepdims=True)
    return scale * (scaled - first - unit * second)


def swap_halves(values):
    width = values.shape[1]
    lane = lax.broadcasted_iota(jnp.int32, values.shape, 1)
    return jnp.where(
        lane % HEAD_DIM < HEAD_DIM // 2,
        pltpu.roll(values, width - HEAD_DIM // 2, 1),
        pltpu.roll(values, HEAD_DIM // 2, 1),
    )


def head_lanes(shape_of, head):
    lane = lax.broadcasted_iota(jnp.int32, shape_of, 1)
    return (lane >= head * HEAD_DIM) & (lane < (head + 1) * HEAD_DIM)


def pack_kernel(wide, tall, packed):
    parts = [wide[j] for j in range(wide.shape[0])]
    packed[...] = jnp.concatenate(parts + [tall[...].T], axis=1)


def prepare_kernel(ids, first, t0, t1, t2, t3, gain, freq, n1, cosine, sine):
    gain_row = gain[...].astype(F32)
    for i, source in enumerate((t0, t1, t2, t3)):
        unit, _ = normed(source[...].astype(F32))
        n1[rows_of(ids[i]), :] = (unit * gain_row).astype(BF)
    start = jnp.int32(0)
    lane = lax.broadcasted_iota(jnp.int32, (WINDOW, 128), 1)
    sign = jnp.where(lane % HEAD_DIM < HEAD_DIM // 2, -1.0, 1.0)
    for b in range(4):
        start = jnp.where(first[b] > 0, b, start)
        place = lax.broadcasted_iota(jnp.int32, (WINDOW, 128), 0) + (b - start) * WINDOW
        angle = place.astype(F32) * freq[...]
        cosine[b * WINDOW : (b + 1) * WINDOW, :] = jnp.cos(angle)
        sine[b * WINDOW : (b + 1) * WINDOW, :] = jnp.sin(angle) * sign


def put_pieces(ids, offsets, pieces, left, right, rows):
    cut = left.shape[1]
    for j, piece in enumerate(pieces):
        if offsets is None:
            at = slice(None)
        else:
            at = rows_of(jnp.bitwise_xor(ids[4], offsets[j]), rows)
        value = piece[...]
        left[at, :] = value[:, :cut]
        right[at, :] = value[:, cut:]


def attend_kernel(offsets, n_pieces, rows, ids, count, first, n1, cosine, sine, *rest):
    pieces = rest[:n_pieces]
    q_out, k_out, v_out, probs_out, att_out, whole, out_w = rest[n_pieces : n_pieces + 7]
    k_pad, v_pad = rest[n_pieces + 7 :]
    put_pieces(ids, offsets, pieces, whole, out_w, rows)
    half = WINDOW // 2
    width = q_out.shape[1]
    heads = width // HEAD_DIM
    total_rows = q_out.shape[0]
    blocks = total_rows // WINDOW
    for pad in (k_pad, v_pad):
        pad[0:half, :] = jnp.zeros((half, width), BF)
        pad[half + total_rows :, :] = jnp.zeros((half, width), BF)
    for b in range(blocks):
        rows_b = slice(b * WINDOW, (b + 1) * WINDOW)
        raw = dot(n1[rows_b, :], whole[...])
        c = jnp.concatenate([cosine[rows_b, :]] * 3, axis=1)
        s = jnp.concatenate([sine[rows_b, :]] * 3, axis=1)
        qk = raw[:, : 2 * width]
        turned = (qk * c + swap_halves(qk) * s).astype(BF)
        q_out[rows_b, :] = turned[:, :width]
        k_b = turned[:, width:]
        v_b = raw[:, 2 * width :].astype(BF)
        k_out[rows_b, :] = k_b
        v_out[rows_b, :] = v_b
        k_pad[half + b * WINDOW : half + (b + 1) * WINDOW, :] = k_b
        v_pad[half + b * WINDOW : half + (b + 1) * WINDOW, :] = v_b
    span = 2 * WINDOW
    column = lax.broadcasted_iota(jnp.int32, (WINDOW, span), 1)
    row = lax.broadcasted_iota(jnp.int32, (WINDOW, span), 0)
    near = jnp.abs(row + half - column) <= half
    for b in range(blocks):
        rows_b = slice(b * WINDOW, (b + 1) * WINDOW)
        span_b = slice(b * WINDOW, b * WINDOW + span)
        before = jnp.where(first[b] == 0, count[b - 1], 0) if b > 0 else 0
        after = jnp.where(first[b + 1] == 0, count[b + 1], 0) if b + 1 < blocks else 0
        limit = jnp.where(
            column < half,
            before - half,
            jnp.where(column < half + WINDOW, count[b] + half, after + half + WINDOW),
        )
        allowed = near & (column < limit) & (row < count[b])
        spare = (lax.broadcasted_iota(jnp.int32, (WINDOW, 1), 0) >= count[b]).astype(F32)
        q_b = q_out[rows_b, :]
        keys = k_pad[span_b, :]
        values = v_pad[span_b, :]
        mixed = jnp.zeros((WINDOW, width), F32)
        for h in range(heads):
            mine = head_lanes((WINDOW, width), h)
            scores = dot(jnp.where(mine, q_b, 0), keys, NT) * (HEAD_DIM**-0.5)
            masked = jnp.where(allowed, scores, NEG_FILL)
            peak = jnp.max(masked, axis=-1, keepdims=True)
            raised = jnp.where(allowed, jnp.exp(masked - peak), 0.0)
            total = jnp.sum(raised, axis=-1, keepdims=True) + spare
            probs = (raised * (1.0 / total)).astype(BF)
            probs_out[h, rows_b, :] = probs
            mixed = jnp.where(mine, dot(probs, values), mixed)
        att_out[rows_b, :] = mixed.astype(BF)


def collect_kernel(offsets, n_pieces, rows, ids, *rest):
    put_pieces(ids, offsets, rest[:n_pieces], rest[n_pieces], rest[n_pieces + 1], rows)


def project_kernel(ids, att, out_w, send, keep):
    for i in range(4):
        part = dot(att[rows_of(ids[i]), :], out_w[...], NT)
        at = slice((i % 2) * WINDOW, (i % 2 + 1) * WINDOW)
        if i < 2:
            keep[at, :] = part
        else:
            send[at, :] = part.astype(BF)


def middle_kernel(own, received, t0, t1, gain, h_out, n2_out):
    for i, tokens in enumerate((t0, t1)):
        at = slice(i * WINDOW, (i + 1) * WINDOW)
        back = slice((1 - i) * WINDOW, (2 - i) * WINDOW)
        branch = own[at, :].astype(F32) + received[back, :].astype(F32)
        h = tokens[...].astype(F32) + branch
        h_out[at, :] = h
        unit, _ = normed(h)
        n2_out[at, :] = (unit * gain[...].astype(F32)).astype(BF)


def units_kernel(n2, n2_far, c0, c1, c2, c3, in_w, down_w, send, keep, both_out, act_out):
    units = act_out.shape[1]
    gate_w, up_w = in_w[:, :units], in_w[:, units:]
    for i in (2, 3, 0, 1):
        at = slice((i % 2) * WINDOW, (i % 2 + 1) * WINDOW)
        rows_n = (n2 if i < 2 else n2_far)[at, :]
        rows_g = (c0, c1, c2, c3)[i][...]
        gate = dot(rows_n, gate_w)
        up = dot(rows_n, up_w)
        g_act = dot(rows_g, down_w[...])
        phi = 0.5 * (1.0 + lax.erf(gate * np.float32(np.sqrt(0.5))))
        gelu = gate * phi
        slope = phi + gate * (jnp.exp(-0.5 * gate * gate) * np.float32(1.0 / np.sqrt(2.0 * np.pi)))
        act_out[i * WINDOW : (i + 1) * WINDOW, :] = (gelu * up).astype(BF)
        g_both = jnp.concatenate([g_act * up * slope, g_act * gelu], axis=1).astype(BF)
        both_out[i * WINDOW : (i + 1) * WINDOW, :] = g_both
        part = dot(g_both, in_w[...], NT)
        if i < 2:
            keep[at, :] = part
        else:
            send[at, :] = part.astype(BF)


def emit_slots(ids, slots, rows, total, send, keep):
    for k in range(slots):
        near = jnp.bitwise_xor(ids[4], 2 * k)
        far = jnp.bitwise_xor(ids[4], 2 * k + 1)
        send[k] = total[rows_of(far, rows), :].astype(BF)
        keep[k] = total[rows_of(near, rows), :].astype(BF)


def unit_grads_kernel(
    slots, rows, ids, n2, n2_far, c0, c1, c2, c3, both, act, down_w, send, keep, b_send, b_keep, total
):
    pair = 2 * WINDOW
    units2 = both.shape[1]
    in_part = dot(n2[...], both[:pair, :], TN) + dot(n2_far[...], both[pair:, :], TN)
    total[:, :units2] = in_part
    gz = jnp.concatenate([c0[...], c1[...], c2[...], c3[...]], axis=0)
    down_part = dot(gz, act[...], TN)
    total[:, units2:] = down_part
    if slots:
        emit_slots(ids, slots, rows, total, send, keep)
    else:
        send[...] = total[...]
        keep[...] = jnp.zeros(keep.shape, BF)
    b_keep[...] = dot(act[:pair, :], down_w[...], NT)
    b_send[...] = dot(act[pair:, :], down_w[...], NT).astype(BF)


def residual_kernel(own, received, h, c0, c1, gain, gh_out, gy_out, gain_out):
    gain_row = gain[...].astype(F32)
    for i, cot in enumerate((c0, c1)):
        at = slice(i * WINDOW, (i + 1) * WINDOW)
        back = slice((1 - i) * WINDOW, (2 - i) * WINDOW)
        grad = own[at, :].astype(F32) + received[back, :].astype(F32)
        unit, scale = normed(h[at, :])
        gh = cot[...].astype(F32) + norm_back(grad, gain_row, unit, scale)
        gy_out[at, :] = gh.astype(BF)
        if i == 0:
            gh_out[...] = gh
            gain_out[...] = jnp.sum(grad * unit, axis=0, keepdims=True)


def attend_back_kernel(
    ids, gy, gy_far, out_w, q_in, k_in, v_in, probs_in, cosine, sine,
    g_raw,
    g_att_all, k_pad, v_pad, gk_pad, gv_pad, gq_all,
):
    half = WINDOW // 2
    total_rows, width = q_in.shape
    heads = width // HEAD_DIM
    blocks = total_rows // WINDOW
    span = 2 * WINDOW
    for i in range(4):
        source = gy if i < 2 else gy_far
        part = dot(source[(i % 2) * WINDOW : (i % 2 + 1) * WINDOW, :], out_w[...])
        g_att_all[rows_of(ids[i]), :] = part.astype(BF)
    for pad, source in ((k_pad, k_in), (v_pad, v_in)):
        pad[0:half, :] = jnp.zeros((half, width), BF)
        pad[half + total_rows :, :] = jnp.zeros((half, width), BF)
        pad[half : half + total_rows, :] = source[...]
    gk_pad[...] = jnp.zeros(gk_pad.shape, F32)
    gv_pad[...] = jnp.zeros(gv_pad.shape, F32)
    for b in range(blocks):
        rows_b = slice(b * WINDOW, (b + 1) * WINDOW)
        span_b = slice(b * WINDOW, b * WINDOW + span)
        g_att = g_att_all[rows_b, :]
        q_b = q_in[rows_b, :]
        keys = k_pad[span_b, :]
        values = v_pad[span_b, :]
        gq = jnp.zeros((WINDOW, width), F32)
        gk = jnp.zeros((span, width), F32)
        gv = jnp.zeros((span, width), F32)
        for h in range(heads):
            mine = head_lanes((WINDOW, width), h)
            g_mine = jnp.where(mine, g_att, 0)
            probs = probs_in[h, rows_b, :]
            wide = probs.astype(F32)
            g_probs = dot(g_mine, values, NT)
            delta = jnp.sum(wide * g_probs, axis=-1, keepdims=True)
            g_scores = (wide * (g_probs - delta)).astype(BF)
            gq = jnp.where(mine, dot(g_scores, keys), gq)
            gk = gk + dot(g_scores, jnp.where(mine, q_b, 0), TN)
            gv = gv + dot(probs, g_mine, TN)
        gq_all[rows_b, :] = gq
        gk_pad[span_b, :] += gk
        gv_pad[span_b, :] += gv
    scale = HEAD_DIM**-0.5
    for b in range(blocks):
        rows_b = slice(b * WINDOW, (b + 1) * WINDOW)
        inner = slice(half + b * WINDOW, half + (b + 1) * WINDOW)
        c = jnp.concatenate([cosine[rows_b, :]] * 3, axis=1)
        s = jnp.concatenate([sine[rows_b, :]] * 3, axis=1)
        qk = jnp.concatenate([gq_all[rows_b, :], gk_pad[inner, :]], axis=1) * scale
        turned = qk * c - swap_halves(qk) * s
        g_raw[rows_b, : 2 * width] = turned.astype(BF)
        g_raw[rows_b, 2 * width :] = gv_pad[inner, :].astype(BF)


def attend_grads_kernel(slots, rows, ids, n1, g_raw, gy, gy_far, att, send, keep, total):
    columns = g_raw.shape[1]
    total[:, :columns] = dot(n1[...], g_raw[...], TN)
    near = jnp.concatenate([att[rows_of(ids[i]), :] for i in (0, 1)], axis=0)
    far = jnp.concatenate([att[rows_of(ids[i]), :] for i in (2, 3)], axis=0)
    total[:, columns:] = dot(gy[...], near, TN) + dot(gy_far[...], far, TN)
    if slots:
        emit_slots(ids, slots, rows, total, send, keep)
    else:
        send[...] = total[...]
        keep[...] = jnp.zeros(keep.shape, BF)


def first_back_kernel(ids, g_raw, qkv_w, n1, gain, gain_two, g_send, g_keep, gains):
    gain_sum = jnp.zeros(gain_two.shape, F32)
    for i in (2, 3, 0, 1):
        at = slice((i % 2) * WINDOW, (i % 2 + 1) * WINDOW)
        g_n1 = dot(g_raw[rows_of(ids[i]), :], qkv_w[...], NT)
        gain_sum += jnp.sum(g_n1 * n1[rows_of(ids[i]), :].astype(F32), axis=0, keepdims=True)
        if i < 2:
            g_keep[at, :] = g_n1
        else:
            g_send[at, :] = g_n1.astype(BF)
    gains[0:1, :] = gain_sum / gain[...].astype(F32)
    gains[1:2, :] = gain_two[...]


def merge_kernel(keep, got, first, *others):
    first[...] = keep[0].astype(F32) + got[0].astype(F32)
    for k, other in enumerate(others):
        other[...] = (keep[k + 1].astype(F32) + got[k + 1].astype(F32)).astype(BF)


EXTRA = 8


def merge_gains_kernel(keep, got, gains, gains_got, first, *others):
    rows, columns = keep.shape[1:]
    first[:rows, :] = keep[0].astype(F32) + got[0].astype(F32)
    total = gains[...] + gains_got[...]
    high = total.astype(BF).astype(F32)
    low = (total - high).astype(BF).astype(F32)
    first[rows:, :] = jnp.concatenate([total, jnp.zeros((EXTRA - 2, columns), F32)], axis=0)
    coded = jnp.concatenate([high, low, jnp.zeros((EXTRA - 4, columns), F32)], axis=0).astype(BF)
    for k, other in enumerate(others):
        other[:rows, :] = (keep[k + 1].astype(F32) + got[k + 1].astype(F32)).astype(BF)
        other[rows:, :] = coded


def deliver_kernel(with_gains, first, *rest):
    if with_gains:
        rows = first.shape[0] - EXTRA
        parts = rest[:-4]
        gains = first[rows : rows + 2, :]
        for part in parts:
            coded = part[rows:, :].astype(F32)
            gains = gains + coded[0:2, :] + coded[2:4, :]
        rest[-4][...] = gains[0:1, :]
        rest[-3][...] = gains[1:2, :]
        total = first[:rows, :]
        for part in parts:
            total = total + part[:rows, :].astype(F32)
    else:
        total = first[...]
        for part in rest[:-2]:
            total = total + part[...].astype(F32)
    wide, turned = rest[-2:]
    count, _, width = wide.shape
    for j in range(count):
        wide[j] = total[:, j * width : (j + 1) * width]
    turned[...] = total[:, count * width :].T


def finish_kernel(
    g_keep, g_core, b_keep, b_core, received, h, tokens, gain, gh, mixed_out, grad_out
):
    gain_row = gain[...].astype(F32)
    grad = g_keep[:WINDOW, :] + g_core[:WINDOW, :].astype(F32) + received[:WINDOW, :].astype(F32)
    unit, scale = normed(tokens[...].astype(F32))
    grad_out[...] = (gh[...] + norm_back(grad, gain_row, unit, scale)).astype(BF)
    branch = b_keep[:WINDOW, :] + b_core[:WINDOW, :].astype(F32) + received[WINDOW:, :].astype(F32)
    mixed_out[...] = (h[:WINDOW, :] + branch).astype(BF)


def swap(values, axis, bit, size):
    return lax.ppermute(values, axis, [(i, i ^ bit) for i in range(size)])


def local(
    tokens, block_count, block_first, norm1_gain, w_qkv, w_out, norm2_gain, w_in, w_down, cotangent
):
    n_dp = lax.axis_size("dp")
    width = tokens.shape[1]
    shard = width // n_dp
    head_width = w_qkv.shape[2]
    units = w_in.shape[2]
    heads = head_width // HEAD_DIM
    total_rows = block_count.shape[0] * WINDOW
    pair_rows = 2 * WINDOW
    slots = n_dp // 2 if shard % 16 == 0 and n_dp % 2 == 0 and n_dp <= 8 else 0
    place = lax.axis_index("tensor").astype(jnp.int32)
    ids = jnp.stack(
        [place, place ^ 2, place ^ 1, place ^ 3, lax.axis_index("dp").astype(jnp.int32)]
    )
    core = functools.partial(swap, axis="tensor", bit=1, size=4)
    across = functools.partial(swap, axis="tensor", bit=2, size=4)
    dp = functools.partial(swap, axis="dp", size=n_dp)

    def along(value):
        if not slots:
            return [lax.all_gather(value, "dp", axis=0, tiled=True)]
        return [dp(value, bit=2 * k) for k in range(1, slots)]

    def aside(pieces):
        if not slots:
            return []
        return list(dp(jnp.stack(pieces), bit=1))

    def picked(own, near, far):
        return (own, *near, *far) if slots else tuple(near)

    def merge(keep, got, gains=()):
        _, rows, columns = keep.shape
        rows += EXTRA if gains else 0
        return call(
            merge_gains_kernel if gains else merge_kernel,
            (shape(rows, columns, dtype=F32),) + (shape(rows, columns),) * (slots - 1),
            (keep, got, *gains),
        )

    def deliver(parts, count, with_gains=False):
        columns = parts[0].shape[1]
        each = columns // (count + 1)
        if not slots:
            total = parts[0]
            return total[:, : count * each].reshape(shard, count, each), total[:, count * each :].T
        *gains, wide, tall = call(
            functools.partial(deliver_kernel, with_gains),
            ((shape(1, columns, dtype=F32),) * 2 if with_gains else ())
            + (shape(count, shard, each, dtype=F32), shape(each, shard, dtype=F32)),
            parts,
        )
        return *(gain.reshape(columns) for gain in gains), jnp.transpose(wide, (1, 0, 2)), tall

    def slot_shapes(columns):
        if not slots:
            return (shape(width, columns, dtype=F32), shape(16, 128))
        return (shape(slots, shard, columns), shape(slots, shard, columns))

    gain_one = norm1_gain.reshape(1, width)
    gain_two = norm2_gain.reshape(1, width)
    freqs = ROPE_BASE ** (-(np.arange(HEAD_DIM // 2, dtype=np.float32) * 2.0) / HEAD_DIM)
    freq = jnp.asarray(np.tile(freqs, 128 // (HEAD_DIM // 2))[None, :], F32)

    offsets = tuple(range(0, n_dp, 2)) + tuple(range(1, n_dp, 2)) if slots else None
    pin = lax.optimization_barrier

    def pack(wide, tall):
        count, _, each = wide.shape
        if not slots:
            return jnp.concatenate([*wide, tall.T], axis=1)
        return call(pack_kernel, (shape(shard, count * each + tall.shape[0]),), (wide, tall))[0]

    qkv_own = pack(jnp.transpose(w_qkv, (1, 0, 2)), w_out)
    qkv_near, tokens_across = pin((along(qkv_own), across(tokens)))
    token_blocks = (tokens, tokens_across, core(tokens), core(tokens_across))
    qkv_far = aside([qkv_own] + qkv_near)
    n1, cosine, sine = call(
        prepare_kernel,
        (shape(total_rows, width), shape(total_rows, 128, dtype=F32), shape(total_rows, 128, dtype=F32)),
        token_blocks + (gain_one, freq),
        (ids, block_first),
    )
    unit_own = pack(jnp.transpose(w_in, (1, 0, 2)), w_down)
    unit_own, cot, _ = pin((unit_own, cotangent, qkv_near))
    unit_near = along(unit_own)
    cot_across = across(cot)
    qkv_far, n1, cot_across = pin((qkv_far, n1, cot_across))
    cot_blocks = (cotangent, cot_across, core(cot), core(cot_across))
    qkv_pieces = picked(qkv_own, qkv_near, qkv_far)
    flat = shape(total_rows, head_width)
    query, keys, values, probs, attended, qkv_w, out_w = call(
        functools.partial(attend_kernel, offsets, len(qkv_pieces), shard),
        (
            flat,
            flat,
            flat,
            shape(heads, total_rows, 2 * WINDOW),
            flat,
            shape(width, 3 * head_width),
            shape(width, head_width),
        ),
        (n1, cosine, sine) + qkv_pieces,
        (ids, block_count, block_first),
        [pltpu.VMEM((total_rows + WINDOW, head_width), BF)] * 2,
        flops=2 * total_rows * width * 3 * head_width,
    )
    attended, unit_near = pin((attended, unit_near))
    unit_far = aside([unit_own] + unit_near)
    unit_pieces = picked(unit_own, unit_near, unit_far)
    in_w, down_w = call(
        functools.partial(collect_kernel, offsets, len(unit_pieces), shard),
        (shape(width, 2 * units), shape(width, units)),
        unit_pieces,
        (ids,),
    )
    pair_f32 = shape(pair_rows, width, dtype=F32)
    pair_bf = shape(pair_rows, width)
    a_send, a_keep = call(
        project_kernel,
        (pair_bf, pair_f32),
        (attended, out_w),
        (ids,),
        flops=2 * total_rows * width * head_width,
    )
    a_sum = (a_keep + core(a_send).astype(F32)).astype(BF)
    h, n2 = call(
        middle_kernel,
        (pair_f32, pair_bf),
        (a_sum, across(a_sum), token_blocks[0], token_blocks[1], gain_two),
    )
    n2_far = core(n2)
    u_send, u_keep, both, act = call(
        units_kernel,
        (pair_bf, pair_f32, shape(total_rows, 2 * units), shape(total_rows, units)),
        (n2, n2_far) + cot_blocks + (in_w, down_w),
        flops=2 * total_rows * width * 5 * units,
    )
    u_sum = (u_keep + core(u_send).astype(F32)).astype(BF)
    u_got = across(u_sum)
    s_shapes = slot_shapes(3 * units)
    in_send, in_keep, b_send, b_keep = call(
        functools.partial(unit_grads_kernel, slots, shard),
        s_shapes + (pair_bf, pair_f32),
        (n2, n2_far) + cot_blocks + (both, act, down_w),
        (ids,),
        [pltpu.VMEM((width, 3 * units), F32)],
        flops=2 * total_rows * width * 4 * units,
    )
    b_core = core(b_send)
    u_got, in_keep = pin((u_got, in_keep))
    gh, gy, gain_part_two = call(
        residual_kernel,
        (shape(WINDOW, width, dtype=F32), pair_bf, shape(1, width, dtype=F32)),
        (u_sum, u_got, h, cot_blocks[0], cot_blocks[1], gain_two),
    )
    gy_far = core(gy)
    (g_raw,) = call(
        attend_back_kernel,
        (shape(total_rows, 3 * head_width),),
        (gy, gy_far, out_w, query, keys, values, probs, cosine, sine),
        (ids,),
        [
            pltpu.VMEM((total_rows, head_width), BF),
            pltpu.VMEM((total_rows + WINDOW, head_width), BF),
            pltpu.VMEM((total_rows + WINDOW, head_width), BF),
            pltpu.VMEM((total_rows + WINDOW, head_width), F32),
            pltpu.VMEM((total_rows + WINDOW, head_width), F32),
            pltpu.VMEM((total_rows, head_width), F32),
        ],
        flops=2 * total_rows * width * 3 * head_width,
    )
    if slots:
        g_raw, in_got = pin((g_raw, dp(in_send, bit=1)))
        in_parts = merge(in_keep, in_got)
    att_send, att_keep = call(
        functools.partial(attend_grads_kernel, slots, shard),
        slot_shapes(4 * head_width),
        (n1, g_raw, gy, gy_far, attended),
        (ids,),
        [pltpu.VMEM((width, 4 * head_width), F32)],
        flops=2 * total_rows * width * 4 * head_width,
    )
    g_raw, att_keep = pin((g_raw, att_keep))
    g_send, g_keep, gains = call(
        first_back_kernel,
        (pair_bf, pair_f32, shape(2, width, dtype=F32)),
        (g_raw, qkv_w, n1, gain_one, gain_part_two),
        (ids,),
        flops=2 * total_rows * width * 3 * head_width,
    )
    g_core = core(g_send)
    if slots:
        gains = gains + core(gains)
        gains, g_core, b_core = pin((gains + across(gains), g_core, b_core))
    back = jnp.concatenate(
        [
            (g_keep[WINDOW:] + g_core[WINDOW:].astype(F32)).astype(BF),
            (b_keep[WINDOW:] + b_core[WINDOW:].astype(F32)).astype(BF),
        ],
        axis=0,
    )
    mixed, input_grad = call(
        finish_kernel,
        (shape(WINDOW, width), shape(WINDOW, width)),
        (g_keep, g_core, b_keep, b_core, across(back), h, tokens, gain_one, gh),
    )
    if slots:
        in_parts = (in_parts[0], *(dp(in_parts[k], bit=2 * k) for k in range(1, slots)))
        att_got, gains_got, in_parts = pin((dp(att_send, bit=1), dp(gains, bit=1), in_parts))
        att_parts = merge(att_keep, att_got, (gains, gains_got))
        att_parts = (att_parts[0], *(dp(att_parts[k], bit=2 * k) for k in range(1, slots)))
    else:
        gains = lax.psum(gains, ("dp", "tensor"))
        in_parts = (lax.psum_scatter(in_send, "dp", scatter_dimension=0, tiled=True),)
        att_parts = (lax.psum_scatter(att_send, "dp", scatter_dimension=0, tiled=True),)
    in_grad, down_grad = deliver(in_parts, 2)
    att_parts, mixed, input_grad, in_grad, down_grad = pin(
        (att_parts, mixed, input_grad, in_grad, down_grad)
    )
    if slots:
        *gains, qkv_grad, out_grad = deliver(att_parts, 3, True)
    else:
        qkv_grad, out_grad = deliver(att_parts, 3)
    return (mixed, input_grad, gains[0], qkv_grad, out_grad, gains[1], in_grad, down_grad)


def solution(mesh):
    return jax.shard_map(
        local,
        mesh=mesh,
        in_specs=(
            P(("dp", "tensor"), None),
            P("dp"),
            P("dp"),
            P(),
            P("dp", None, "tensor"),
            P("tensor", "dp"),
            P(),
            P("dp", None, "tensor"),
            P("tensor", "dp"),
            P(("dp", "tensor"), None),
        ),
        out_specs=(
            P(("dp", "tensor"), None),
            P(("dp", "tensor"), None),
            P(),
            P("dp", None, "tensor"),
            P("tensor", "dp"),
            P(),
            P("dp", None, "tensor"),
            P("tensor", "dp"),
        ),
        check_vma=False,
    )
```

```python
import functools

import jax
import jax.numpy as jnp
import numpy as np
from jax import lax
from jax.experimental import pallas as pl
from jax.experimental.pallas import tpu as pltpu
from jax.sharding import PartitionSpec as P

HEAD_DIM = 64
WINDOW = 128
EPS = 1e-05
ROPE_BASE = 10000.0
NEG_FILL = -1e30
BF = jnp.bfloat16
F32 = jnp.float32

NN = (((1,), (0,)), ((), ()))
NT = (((1,), (1,)), ((), ()))
TN = (((0,), (0,)), ((), ()))


def dot(left, right, dims=NN):
    return lax.dot_general(left, right, dims, preferred_element_type=F32)


def call(kernel, outs, args, scalars=(), scratch=(), flops=0, space=pltpu.VMEM):
    size = sum(int(np.prod(a.shape)) * a.dtype.itemsize for a in list(args) + list(outs))
    return pl.pallas_call(
        kernel,
        name=getattr(kernel, "func", kernel).__name__,
        out_shape=tuple(outs),
        in_specs=[pl.BlockSpec(memory_space=pltpu.SMEM)] * len(scalars)
        + [pl.BlockSpec(memory_space=space)] * len(args),
        out_specs=tuple(pl.BlockSpec(memory_space=pltpu.VMEM) for _ in outs),
        scratch_shapes=list(scratch),
        compiler_params=pltpu.CompilerParams(vmem_limit_bytes=48 * 1024 * 1024),
        cost_estimate=pl.CostEstimate(flops=1, bytes_accessed=1, transcendentals=0),
    )(*scalars, *args)


def shape(*dims, dtype=BF):
    return jax.ShapeDtypeStruct(dims, dtype)


def rows_of(index, count=WINDOW):
    return pl.ds(pl.multiple_of(index * count, 16), count)


def normed(values):
    center = jnp.mean(values, axis=-1, keepdims=True)
    centred = values - center
    spread = jnp.mean(centred * centred, axis=-1, keepdims=True)
    scale = lax.rsqrt(spread + EPS)
    return centred * scale, scale


def norm_back(grad, gain, unit, scale):
    scaled = grad * gain
    first = jnp.mean(scaled, axis=-1, keepdims=True)
    second = jnp.mean(scaled * unit, axis=-1, keepdims=True)
    return scale * (scaled - first - unit * second)


def swap_halves(values):
    width = values.shape[1]
    lane = lax.broadcasted_iota(jnp.int32, values.shape, 1)
    return jnp.where(
        lane % HEAD_DIM < HEAD_DIM // 2,
        pltpu.roll(values, width - HEAD_DIM // 2, 1),
        pltpu.roll(values, HEAD_DIM // 2, 1),
    )


def head_lanes(shape_of, head):
    lane = lax.broadcasted_iota(jnp.int32, shape_of, 1)
    return (lane >= head * HEAD_DIM) & (lane < (head + 1) * HEAD_DIM)


def pack_kernel(wide_far, tall_far, packed, wide, tall, sems):
    copies = [
        pltpu.make_async_copy(wide_far, wide, sems.at[0]),
        pltpu.make_async_copy(tall_far, tall, sems.at[1]),
    ]
    for copy in copies:
        copy.start()
    for copy in copies:
        copy.wait()
    parts = [wide[j] for j in range(wide.shape[0])]
    packed[...] = jnp.concatenate(parts + [tall[...].T], axis=1)


def prepare_kernel(ids, t0, t1, t2, t3, gain, freq, n1, cosine, sine):
    gain_row = gain[...].astype(F32)
    for i, source in enumerate((t0, t1, t2, t3)):
        unit, _ = normed(source[...].astype(F32))
        n1[rows_of(ids[i]), :] = (unit * gain_row).astype(BF)
    start = jnp.int32(0)
    lane = lax.broadcasted_iota(jnp.int32, (WINDOW, 128), 1)
    sign = jnp.where(lane % HEAD_DIM < HEAD_DIM // 2, -1.0, 1.0)
    for b in range(4):
        start = jnp.where(ids[9 + b] > 0, b, start)
        place = lax.broadcasted_iota(jnp.int32, (WINDOW, 128), 0) + (b - start) * WINDOW
        angle = place.astype(F32) * freq[...]
        cosine[b * WINDOW : (b + 1) * WINDOW, :] = jnp.cos(angle)
        sine[b * WINDOW : (b + 1) * WINDOW, :] = jnp.sin(angle) * sign


def put_pieces(ids, offsets, pieces, left, right, rows):
    cut = left.shape[1]
    for j, piece in enumerate(pieces):
        if offsets is None:
            at = slice(None)
        else:
            at = rows_of(jnp.bitwise_xor(ids[4], offsets[j]), rows)
        value = piece[...]
        left[at, :] = value[:, :cut]
        right[at, :] = value[:, cut:]


def attend_kernel(offsets, n_pieces, rows, ids, n1, cosine, sine, *rest):
    pieces = rest[:n_pieces]
    q_out, k_out, v_out, probs_out, att_out, whole, out_w = rest[n_pieces : n_pieces + 7]
    k_pad, v_pad = rest[n_pieces + 7 :]
    put_pieces(ids, offsets, pieces, whole, out_w, rows)
    half = WINDOW // 2
    width = q_out.shape[1]
    heads = width // HEAD_DIM
    total_rows = q_out.shape[0]
    blocks = total_rows // WINDOW
    count = [ids[5 + b] for b in range(blocks)]
    first = [ids[5 + blocks + b] for b in range(blocks)]
    for pad in (k_pad, v_pad):
        pad[0:half, :] = jnp.zeros((half, width), BF)
        pad[half + total_rows :, :] = jnp.zeros((half, width), BF)
    for b in range(blocks):
        rows_b = slice(b * WINDOW, (b + 1) * WINDOW)
        raw = dot(n1[rows_b, :], whole[...])
        c = jnp.concatenate([cosine[rows_b, :]] * 3, axis=1)
        s = jnp.concatenate([sine[rows_b, :]] * 3, axis=1)
        qk = raw[:, : 2 * width]
        turned = (qk * c + swap_halves(qk) * s).astype(BF)
        q_out[rows_b, :] = turned[:, :width]
        k_b = turned[:, width:]
        v_b = raw[:, 2 * width :].astype(BF)
        k_out[rows_b, :] = k_b
        v_out[rows_b, :] = v_b
        k_pad[half + b * WINDOW : half + (b + 1) * WINDOW, :] = k_b
        v_pad[half + b * WINDOW : half + (b + 1) * WINDOW, :] = v_b
    span = 2 * WINDOW
    column = lax.broadcasted_iota(jnp.int32, (WINDOW, span), 1)
    row = lax.broadcasted_iota(jnp.int32, (WINDOW, span), 0)
    near = jnp.abs(row + half - column) <= half
    for b in range(blocks):
        rows_b = slice(b * WINDOW, (b + 1) * WINDOW)
        span_b = slice(b * WINDOW, b * WINDOW + span)
        before = jnp.where(first[b] == 0, count[b - 1], 0) if b > 0 else 0
        after = jnp.where(first[b + 1] == 0, count[b + 1], 0) if b + 1 < blocks else 0
        limit = jnp.where(
            column < half,
            before - half,
            jnp.where(column < half + WINDOW, count[b] + half, after + half + WINDOW),
        )
        allowed = near & (column < limit) & (row < count[b])
        spare = (lax.broadcasted_iota(jnp.int32, (WINDOW, 1), 0) >= count[b]).astype(F32)
        q_b = q_out[rows_b, :]
        keys = k_pad[span_b, :]
        values = v_pad[span_b, :]
        mixed = jnp.zeros((WINDOW, width), F32)
        for h in range(heads):
            mine = head_lanes((WINDOW, width), h)
            scores = dot(jnp.where(mine, q_b, 0), keys, NT) * (HEAD_DIM**-0.5)
            masked = jnp.where(allowed, scores, NEG_FILL)
            peak = jnp.max(masked, axis=-1, keepdims=True)
            raised = jnp.where(allowed, jnp.exp(masked - peak), 0.0)
            total = jnp.sum(raised, axis=-1, keepdims=True) + spare
            probs = (raised * (1.0 / total)).astype(BF)
            probs_out[h, rows_b, :] = probs
            mixed = jnp.where(mine, dot(probs, values), mixed)
        att_out[rows_b, :] = mixed.astype(BF)


def collect_kernel(offsets, n_pieces, rows, ids, *rest):
    put_pieces(ids, offsets, rest[:n_pieces], rest[n_pieces], rest[n_pieces + 1], rows)


def project_kernel(ids, att, out_w, send, keep):
    for i in range(4):
        part = dot(att[rows_of(ids[i]), :], out_w[...], NT)
        at = slice((i % 2) * WINDOW, (i % 2 + 1) * WINDOW)
        if i < 2:
            keep[at, :] = part
        else:
            send[at, :] = part.astype(BF)


def middle_kernel(own, received, t0, t1, gain, h_out, n2_out):
    for i, tokens in enumerate((t0, t1)):
        at = slice(i * WINDOW, (i + 1) * WINDOW)
        back = slice((1 - i) * WINDOW, (2 - i) * WINDOW)
        branch = own[at, :].astype(F32) + received[back, :].astype(F32)
        h = tokens[...].astype(F32) + branch
        h_out[at, :] = h
        unit, _ = normed(h)
        n2_out[at, :] = (unit * gain[...].astype(F32)).astype(BF)


def units_kernel(n2, n2_far, c0, c1, c2, c3, in_w, down_w, send, keep, both_out, act_out):
    units = act_out.shape[1]
    gate_w, up_w = in_w[:, :units], in_w[:, units:]
    for i in (2, 3, 0, 1):
        at = slice((i % 2) * WINDOW, (i % 2 + 1) * WINDOW)
        rows_n = (n2 if i < 2 else n2_far)[at, :]
        rows_g = (c0, c1, c2, c3)[i][...]
        gate = dot(rows_n, gate_w)
        up = dot(rows_n, up_w)
        g_act = dot(rows_g, down_w[...])
        phi = 0.5 * (1.0 + lax.erf(gate * np.float32(np.sqrt(0.5))))
        gelu = gate * phi
        slope = phi + gate * (jnp.exp(-0.5 * gate * gate) * np.float32(1.0 / np.sqrt(2.0 * np.pi)))
        act_out[i * WINDOW : (i + 1) * WINDOW, :] = (gelu * up).astype(BF)
        g_both = jnp.concatenate([g_act * up * slope, g_act * gelu], axis=1).astype(BF)
        both_out[i * WINDOW : (i + 1) * WINDOW, :] = g_both
        part = dot(g_both, in_w[...], NT)
        if i < 2:
            keep[at, :] = part
        else:
            send[at, :] = part.astype(BF)


def emit_slots(ids, slots, rows, total, send, keep):
    for k in range(slots):
        near = jnp.bitwise_xor(ids[4], 2 * k)
        far = jnp.bitwise_xor(ids[4], 2 * k + 1)
        send[k] = total[rows_of(far, rows), :].astype(BF)
        keep[k] = total[rows_of(near, rows), :].astype(BF)


def unit_grads_kernel(
    slots, rows, ids, n2, n2_far, c0, c1, c2, c3, both, act, down_w, send, keep, b_send, b_keep, total
):
    pair = 2 * WINDOW
    units2 = both.shape[1]
    in_part = dot(n2[...], both[:pair, :], TN) + dot(n2_far[...], both[pair:, :], TN)
    total[:, :units2] = in_part
    gz = jnp.concatenate([c0[...], c1[...], c2[...], c3[...]], axis=0)
    down_part = dot(gz, act[...], TN)
    total[:, units2:] = down_part
    if slots:
        emit_slots(ids, slots, rows, total, send, keep)
    else:
        send[...] = total[...]
        keep[...] = jnp.zeros(keep.shape, BF)
    b_keep[...] = dot(act[:pair, :], down_w[...], NT)
    b_send[...] = dot(act[pair:, :], down_w[...], NT).astype(BF)


def residual_kernel(own, received, h, c0, c1, gain, gh_out, gy_out, gain_out):
    gain_row = gain[...].astype(F32)
    for i, cot in enumerate((c0, c1)):
        at = slice(i * WINDOW, (i + 1) * WINDOW)
        back = slice((1 - i) * WINDOW, (2 - i) * WINDOW)
        grad = own[at, :].astype(F32) + received[back, :].astype(F32)
        unit, scale = normed(h[at, :])
        gh = cot[...].astype(F32) + norm_back(grad, gain_row, unit, scale)
        gy_out[at, :] = gh.astype(BF)
        if i == 0:
            gh_out[...] = gh
            gain_out[...] = jnp.sum(grad * unit, axis=0, keepdims=True)


def attend_back_kernel(
    ids, gy, gy_far, out_w, q_in, k_in, v_in, probs_in, cosine, sine, n1, qkv_w, gain, gain_two,
    g_raw, g_send, g_keep, gains,
    g_att_all, k_pad, v_pad, gk_pad, gv_pad, gq_all,
):
    half = WINDOW // 2
    total_rows, width = q_in.shape
    heads = width // HEAD_DIM
    blocks = total_rows // WINDOW
    span = 2 * WINDOW
    for i in range(4):
        source = gy if i < 2 else gy_far
        part = dot(source[(i % 2) * WINDOW : (i % 2 + 1) * WINDOW, :], out_w[...])
        g_att_all[rows_of(ids[i]), :] = part.astype(BF)
    for pad, source in ((k_pad, k_in), (v_pad, v_in)):
        pad[0:half, :] = jnp.zeros((half, width), BF)
        pad[half + total_rows :, :] = jnp.zeros((half, width), BF)
        pad[half : half + total_rows, :] = source[...]
    gk_pad[...] = jnp.zeros(gk_pad.shape, F32)
    gv_pad[...] = jnp.zeros(gv_pad.shape, F32)
    for b in range(blocks):
        rows_b = slice(b * WINDOW, (b + 1) * WINDOW)
        span_b = slice(b * WINDOW, b * WINDOW + span)
        g_att = g_att_all[rows_b, :]
        q_b = q_in[rows_b, :]
        keys = k_pad[span_b, :]
        values = v_pad[span_b, :]
        gq = jnp.zeros((WINDOW, width), F32)
        gk = jnp.zeros((span, width), F32)
        gv = jnp.zeros((span, width), F32)
        for h in range(heads):
            mine = head_lanes((WINDOW, width), h)
            g_mine = jnp.where(mine, g_att, 0)
            probs = probs_in[h, rows_b, :]
            wide = probs.astype(F32)
            g_probs = dot(g_mine, values, NT)
            delta = jnp.sum(wide * g_probs, axis=-1, keepdims=True)
            g_scores = (wide * (g_probs - delta)).astype(BF)
            gq = jnp.where(mine, dot(g_scores, keys), gq)
            gk = gk + dot(g_scores, jnp.where(mine, q_b, 0), TN)
            gv = gv + dot(probs, g_mine, TN)
        gq_all[rows_b, :] = gq
        gk_pad[span_b, :] += gk
        gv_pad[span_b, :] += gv
    scale = HEAD_DIM**-0.5
    for b in range(blocks):
        rows_b = slice(b * WINDOW, (b + 1) * WINDOW)
        inner = slice(half + b * WINDOW, half + (b + 1) * WINDOW)
        c = jnp.concatenate([cosine[rows_b, :]] * 3, axis=1)
        s = jnp.concatenate([sine[rows_b, :]] * 3, axis=1)
        qk = jnp.concatenate([gq_all[rows_b, :], gk_pad[inner, :]], axis=1) * scale
        turned = qk * c - swap_halves(qk) * s
        g_raw[rows_b, : 2 * width] = turned.astype(BF)
        g_raw[rows_b, 2 * width :] = gv_pad[inner, :].astype(BF)
    gain_sum = jnp.zeros(gain_two.shape, F32)
    for i in (2, 3, 0, 1):
        at = slice((i % 2) * WINDOW, (i % 2 + 1) * WINDOW)
        g_n1 = dot(g_raw[rows_of(ids[i]), :], qkv_w[...], NT)
        gain_sum += jnp.sum(g_n1 * n1[rows_of(ids[i]), :].astype(F32), axis=0, keepdims=True)
        if i < 2:
            g_keep[at, :] = g_n1
        else:
            g_send[at, :] = g_n1.astype(BF)
    gains[0:1, :] = gain_sum / gain[...].astype(F32)
    gains[1:2, :] = gain_two[...]


def attend_grads_kernel(slots, rows, ids, n1, g_raw, gy, gy_far, att, send, keep, total):
    columns = g_raw.shape[1]
    total[:, :columns] = dot(n1[...], g_raw[...], TN)
    near = jnp.concatenate([att[rows_of(ids[i]), :] for i in (0, 1)], axis=0)
    far = jnp.concatenate([att[rows_of(ids[i]), :] for i in (2, 3)], axis=0)
    total[:, columns:] = dot(gy[...], near, TN) + dot(gy_far[...], far, TN)
    if slots:
        emit_slots(ids, slots, rows, total, send, keep)
    else:
        send[...] = total[...]
        keep[...] = jnp.zeros(keep.shape, BF)


def merge_kernel(keep, got, first, *others):
    first[...] = keep[0].astype(F32) + got[0].astype(F32)
    for k, other in enumerate(others):
        other[...] = (keep[k + 1].astype(F32) + got[k + 1].astype(F32)).astype(BF)


EXTRA = 8


def merge_gains_kernel(keep, got, gains, gains_got, first, *rest):
    others, total_out = rest[:-1], rest[-1]
    rows, columns = keep.shape[1:]
    first[...] = keep[0].astype(F32) + got[0].astype(F32)
    total = gains[...] + gains_got[...]
    total_out[...] = total
    high = total.astype(BF).astype(F32)
    low = (total - high).astype(BF).astype(F32)
    coded = jnp.concatenate([high, low, jnp.zeros((EXTRA - 4, columns), F32)], axis=0).astype(BF)
    for k, other in enumerate(others):
        other[:rows, :] = (keep[k + 1].astype(F32) + got[k + 1].astype(F32)).astype(BF)
        other[rows:, :] = coded


def deliver_kernel(with_gains, count, first, *rest):
    count_parts = len(rest) - 2
    if with_gains:
        count_parts = len(rest) - 5
        gains = rest[count_parts][...]
        rows = first.shape[0]
        for part in rest[:count_parts]:
            coded = part[rows:, :].astype(F32)
            gains = gains + coded[0:2, :] + coded[2:4, :]
        for j in range(gains.shape[1] // 128):
            rest[-4][j : j + 1, :] = gains[0:1, j * 128 : (j + 1) * 128]
            rest[-3][j : j + 1, :] = gains[1:2, j * 128 : (j + 1) * 128]
    total = first[...]
    for part in rest[:count_parts]:
        total = total + part[: first.shape[0], :].astype(F32)
    wide, turned = rest[-2:]
    width = wide.shape[2]
    for j in range(count):
        value = total[:, j * width : (j + 1) * width]
        if with_gains:
            wide[j] = value
        else:
            wide[:, j, :] = value
    turned[...] = total[:, count * width :].T


def finish_kernel(
    g_keep, g_core, b_keep, b_core, received, h, tokens, gain, gh, mixed_out, grad_out
):
    gain_row = gain[...].astype(F32)
    grad = g_keep[:WINDOW, :] + g_core[:WINDOW, :].astype(F32) + received[:WINDOW, :].astype(F32)
    unit, scale = normed(tokens[...].astype(F32))
    grad_out[...] = (gh[...] + norm_back(grad, gain_row, unit, scale)).astype(BF)
    branch = b_keep[:WINDOW, :] + b_core[:WINDOW, :].astype(F32) + received[WINDOW:, :].astype(F32)
    mixed_out[...] = (h[:WINDOW, :] + branch).astype(BF)


def swap(values, axis, bit, size):
    return lax.ppermute(values, axis, [(i, i ^ bit) for i in range(size)])


def local(
    tokens, block_count, block_first, norm1_gain, w_qkv, w_out, norm2_gain, w_in, w_down, cotangent
):
    n_dp = lax.axis_size("dp")
    width = tokens.shape[1]
    shard = width // n_dp
    head_width = w_qkv.shape[2]
    units = w_in.shape[2]
    heads = head_width // HEAD_DIM
    total_rows = block_count.shape[0] * WINDOW
    pair_rows = 2 * WINDOW
    slots = n_dp // 2 if shard % 16 == 0 and n_dp % 2 == 0 and n_dp <= 8 else 0
    place = lax.axis_index("tensor").astype(jnp.int32)
    ids = jnp.concatenate(
        [
            jnp.stack(
                [place, place ^ 2, place ^ 1, place ^ 3, lax.axis_index("dp").astype(jnp.int32)]
            ),
            block_count,
            block_first,
        ]
    )
    core = functools.partial(swap, axis="tensor", bit=1, size=4)
    across = functools.partial(swap, axis="tensor", bit=2, size=4)
    dp = functools.partial(swap, axis="dp", size=n_dp)

    def diagonal(values):
        pairs = [(4 * d + t, 4 * (d ^ 1) + (t ^ 2)) for d in range(n_dp) for t in range(4)]
        return lax.ppermute(values, ("dp", "tensor"), pairs)

    def along(value):
        if not slots:
            return [lax.all_gather(value, "dp", axis=0, tiled=True)]
        return [dp(value, bit=2 * k) for k in range(1, slots)]

    def aside(pieces):
        if not slots:
            return []
        if len(pieces) == 1:
            return [dp(pieces[0], bit=1)]
        return list(dp(jnp.stack(pieces), bit=1))

    def picked(own, near, far):
        return (own, *near, *far) if slots else tuple(near)

    def merge(keep, got, gains=()):
        _, rows, columns = keep.shape
        extra = EXTRA if gains else 0
        return call(
            merge_gains_kernel if gains else merge_kernel,
            (shape(rows, columns, dtype=F32),)
            + (shape(rows + extra, columns),) * (slots - 1)
            + ((shape(2, columns, dtype=F32),) if gains else ()),
            (keep, got, *gains),
        )

    def deliver(parts, count, gains=()):
        columns = parts[0].shape[1]
        each = columns // (count + 1)
        if not slots:
            total = parts[0]
            return total[:, : count * each].reshape(shard, count, each), total[:, count * each :].T
        with_gains = bool(gains)
        whole = (count, shard, each) if with_gains else (shard, count, each)
        *sums, wide, tall = call(
            functools.partial(deliver_kernel, with_gains, count),
            ((shape(columns // 128, 128, dtype=F32),) * 2 if with_gains else ())
            + (shape(*whole, dtype=F32), shape(each, shard, dtype=F32)),
            tuple(parts) + tuple(gains),
        )
        if with_gains:
            wide = jnp.transpose(wide, (1, 0, 2))
        return *(gain.reshape(columns) for gain in sums), wide, tall

    def slot_shapes(columns):
        if not slots:
            return (shape(width, columns, dtype=F32), shape(16, 128))
        return (shape(slots, shard, columns), shape(slots, shard, columns))

    gain_one = norm1_gain.reshape(1, width)
    gain_two = norm2_gain.reshape(1, width)
    freqs = ROPE_BASE ** (-(np.arange(HEAD_DIM // 2, dtype=np.float32) * 2.0) / HEAD_DIM)
    freq = jnp.asarray(np.tile(freqs, 128 // (HEAD_DIM // 2))[None, :], F32)

    offsets = tuple(range(0, n_dp, 2)) + tuple(range(1, n_dp, 2)) if slots else None
    pin = lax.optimization_barrier

    def pack(wide, tall):
        count, _, each = wide.shape
        if not slots:
            return jnp.concatenate([*wide, tall.T], axis=1)
        return call(
            pack_kernel,
            (shape(shard, count * each + tall.shape[0]),),
            (wide, tall),
            scratch=[
                pltpu.VMEM(wide.shape, BF),
                pltpu.VMEM(tall.shape, BF),
                pltpu.SemaphoreType.DMA((2,)),
            ],
            space=pltpu.HBM,
        )[0]

    qkv_own = pack(jnp.transpose(w_qkv, (1, 0, 2)), w_out)
    unit_own = pack(jnp.transpose(w_in, (1, 0, 2)), w_down)
    qkv_near, qkv_side, unit_side, tokens_across, ids, gain_one, gain_two = pin(
        (
            along(qkv_own),
            aside([qkv_own]),
            aside([unit_own]),
            across(tokens),
            ids,
            gain_one,
            gain_two,
        )
    )
    token_blocks = (tokens, tokens_across, core(tokens), core(tokens_across))
    qkv_far = qkv_side + aside(qkv_near)
    n1, cosine, sine = call(
        prepare_kernel,
        (shape(total_rows, width), shape(total_rows, 128, dtype=F32), shape(total_rows, 128, dtype=F32)),
        token_blocks + (gain_one, freq),
        (ids,),
    )
    unit_own, cot, _ = pin((unit_own, cotangent, qkv_near))
    unit_near = along(unit_own)
    cot_across = across(cot)
    qkv_far, n1 = pin((qkv_far, n1))
    qkv_pieces = picked(qkv_own, qkv_near, qkv_far)
    flat = shape(total_rows, head_width)
    query, keys, values, probs, attended, qkv_w, out_w = call(
        functools.partial(attend_kernel, offsets, len(qkv_pieces), shard),
        (
            flat,
            flat,
            flat,
            shape(heads, total_rows, 2 * WINDOW),
            flat,
            shape(width, 3 * head_width),
            shape(width, head_width),
        ),
        (n1, cosine, sine) + qkv_pieces,
        (ids,),
        [pltpu.VMEM((total_rows + WINDOW, head_width), BF)] * 2,
        flops=2 * total_rows * width * 3 * head_width,
    )
    attended, unit_near, cot_across = pin((attended, unit_near, cot_across))
    cot_blocks = (cotangent, cot_across, core(cot), core(cot_across))
    unit_far = unit_side + aside(unit_near)
    unit_pieces = picked(unit_own, unit_near, unit_far)
    in_w, down_w = call(
        functools.partial(collect_kernel, offsets, len(unit_pieces), shard),
        (shape(width, 2 * units), shape(width, units)),
        unit_pieces,
        (ids,),
    )
    pair_f32 = shape(pair_rows, width, dtype=F32)
    pair_bf = shape(pair_rows, width)
    a_send, a_keep = call(
        project_kernel,
        (pair_bf, pair_f32),
        (attended, out_w),
        (ids,),
        flops=2 * total_rows * width * head_width,
    )
    a_sum = (a_keep + core(a_send).astype(F32)).astype(BF)
    a_got = across(a_sum)
    h, n2 = call(
        middle_kernel,
        (pair_f32, pair_bf),
        (a_sum, a_got, token_blocks[0], token_blocks[1], gain_two),
    )
    n2_far = core(n2)
    u_send, u_keep, both, act = call(
        units_kernel,
        (pair_bf, pair_f32, shape(total_rows, 2 * units), shape(total_rows, units)),
        (n2, n2_far) + cot_blocks + (in_w, down_w),
        flops=2 * total_rows * width * 5 * units,
    )
    u_sum = (u_keep + core(u_send).astype(F32)).astype(BF)
    u_got = across(u_sum)
    s_shapes = slot_shapes(3 * units)
    in_send, in_keep, b_send, b_keep = call(
        functools.partial(unit_grads_kernel, slots, shard),
        s_shapes + (pair_bf, pair_f32),
        (n2, n2_far) + cot_blocks + (both, act, down_w),
        (ids,),
        [pltpu.VMEM((width, 3 * units), F32)],
        flops=2 * total_rows * width * 4 * units,
    )
    b_core = core(b_send)
    u_got, in_keep = pin((u_got, in_keep))
    gh, gy, gain_part_two = call(
        residual_kernel,
        (shape(WINDOW, width, dtype=F32), pair_bf, shape(1, width, dtype=F32)),
        (u_sum, u_got, h, cot_blocks[0], cot_blocks[1], gain_two),
    )
    gy_far = core(gy)
    g_raw, g_send, g_keep, gains = call(
        attend_back_kernel,
        (
            shape(total_rows, 3 * head_width),
            pair_bf,
            pair_f32,
            shape(2, width, dtype=F32),
        ),
        (gy, gy_far, out_w, query, keys, values, probs, cosine, sine, n1, qkv_w)
        + (gain_one, gain_part_two),
        (ids,),
        [
            pltpu.VMEM((total_rows, head_width), BF),
            pltpu.VMEM((total_rows + WINDOW, head_width), BF),
            pltpu.VMEM((total_rows + WINDOW, head_width), BF),
            pltpu.VMEM((total_rows + WINDOW, head_width), F32),
            pltpu.VMEM((total_rows + WINDOW, head_width), F32),
            pltpu.VMEM((total_rows, head_width), F32),
        ],
    )
    if slots:
        g_raw, g_send, gains, in_got = pin((g_raw, g_send, gains, dp(in_send, bit=1)))
    att_send, att_keep = call(
        functools.partial(attend_grads_kernel, slots, shard),
        slot_shapes(4 * head_width),
        (n1, g_raw, gy, gy_far, attended),
        (ids,),
        [pltpu.VMEM((width, 4 * head_width), F32)],
    )
    if slots:
        in_got, att_keep = pin((in_got, att_keep))
        in_parts = merge(in_keep, in_got)
        in_near = [dp(in_parts[k], bit=2 * k) for k in range(1, slots)]
        gains = gains + core(gains)
        gains = gains + across(gains)
    g_core = core(g_send)
    if slots:
        gains, g_core, b_core = pin((gains, g_core, b_core))
    back = jnp.concatenate(
        [
            (g_keep[WINDOW:] + g_core[WINDOW:].astype(F32)).astype(BF),
            (b_keep[WINDOW:] + b_core[WINDOW:].astype(F32)).astype(BF),
        ],
        axis=0,
    )
    mixed, input_grad = call(
        finish_kernel,
        (shape(WINDOW, width), shape(WINDOW, width)),
        (g_keep, g_core, b_keep, b_core, across(back), h, tokens, gain_one, gh),
    )
    if slots:
        att_got, in_near[0], gains_x = pin((dp(att_send, bit=1), in_near[0], dp(gains, bit=1)))
        in_parts = (in_parts[0], *in_near)
        *att_parts, gains = merge(att_keep, att_got, (gains, gains_x))
        att_parts = (att_parts[0], *(dp(att_parts[k], bit=2 * k) for k in range(1, slots)))
        gains = [gains]
    else:
        gains = lax.psum(gains, ("dp", "tensor"))
        in_parts = (lax.psum_scatter(in_send, "dp", scatter_dimension=0, tiled=True),)
        att_parts = (lax.psum_scatter(att_send, "dp", scatter_dimension=0, tiled=True),)
    in_grad, down_grad = deliver(in_parts, 2)
    att_parts, mixed, input_grad, in_grad, down_grad = pin(
        (att_parts, mixed, input_grad, in_grad, down_grad)
    )
    if slots:
        *gains, qkv_grad, out_grad = deliver(att_parts, 3, gains)
    else:
        qkv_grad, out_grad = deliver(att_parts, 3)
    return (mixed, input_grad, gains[0], qkv_grad, out_grad, gains[1], in_grad, down_grad)


def solution(mesh):
    return jax.shard_map(
        local,
        mesh=mesh,
        in_specs=(
            P(("dp", "tensor"), None),
            P("dp"),
            P("dp"),
            P(),
            P("dp", None, "tensor"),
            P("tensor", "dp"),
            P(),
            P("dp", None, "tensor"),
            P("tensor", "dp"),
            P(("dp", "tensor"), None),
        ),
        out_specs=(
            P(("dp", "tensor"), None),
            P(("dp", "tensor"), None),
            P(),
            P("dp", None, "tensor"),
            P("tensor", "dp"),
            P(),
            P("dp", None, "tensor"),
            P("tensor", "dp"),
        ),
        check_vma=False,
    )
```

```python
import functools

import jax
import jax.numpy as jnp
import numpy as np
from jax import lax
from jax.experimental import pallas as pl
from jax.experimental.pallas import tpu as pltpu
from jax.sharding import PartitionSpec as P

HEAD_DIM = 64
WINDOW = 128
EPS = 1e-05
ROPE_BASE = 10000.0
NEG_FILL = -1e30
BF = jnp.bfloat16
F32 = jnp.float32

NN = (((1,), (0,)), ((), ()))
NT = (((1,), (1,)), ((), ()))
TN = (((0,), (0,)), ((), ()))


def dot(left, right, dims=NN):
    return lax.dot_general(left, right, dims, preferred_element_type=F32)


def call(kernel, outs, args, scalars=(), scratch=(), flops=0, space=pltpu.VMEM):
    size = sum(int(np.prod(a.shape)) * a.dtype.itemsize for a in list(args) + list(outs))
    return pl.pallas_call(
        kernel,
        name=getattr(kernel, "func", kernel).__name__,
        out_shape=tuple(outs),
        in_specs=[pl.BlockSpec(memory_space=pltpu.SMEM)] * len(scalars)
        + [pl.BlockSpec(memory_space=space)] * len(args),
        out_specs=tuple(pl.BlockSpec(memory_space=pltpu.VMEM) for _ in outs),
        scratch_shapes=list(scratch),
        compiler_params=pltpu.CompilerParams(vmem_limit_bytes=48 * 1024 * 1024),
        cost_estimate=pl.CostEstimate(flops=1, bytes_accessed=1, transcendentals=0),
    )(*scalars, *args)


def shape(*dims, dtype=BF):
    return jax.ShapeDtypeStruct(dims, dtype)


def rows_of(index, count=WINDOW):
    return pl.ds(pl.multiple_of(index * count, 16), count)


def normed(values):
    center = jnp.mean(values, axis=-1, keepdims=True)
    centred = values - center
    spread = jnp.mean(centred * centred, axis=-1, keepdims=True)
    scale = lax.rsqrt(spread + EPS)
    return centred * scale, scale


def norm_back(grad, gain, unit, scale):
    scaled = grad * gain
    first = jnp.mean(scaled, axis=-1, keepdims=True)
    second = jnp.mean(scaled * unit, axis=-1, keepdims=True)
    return scale * (scaled - first - unit * second)


def swap_halves(values):
    width = values.shape[1]
    lane = lax.broadcasted_iota(jnp.int32, values.shape, 1)
    return jnp.where(
        lane % HEAD_DIM < HEAD_DIM // 2,
        pltpu.roll(values, width - HEAD_DIM // 2, 1),
        pltpu.roll(values, HEAD_DIM // 2, 1),
    )


def head_lanes(shape_of, head):
    lane = lax.broadcasted_iota(jnp.int32, shape_of, 1)
    return (lane >= head * HEAD_DIM) & (lane < (head + 1) * HEAD_DIM)


def pack_kernel(wide_far, tall_far, packed, wide, tall, sems):
    copies = [
        pltpu.make_async_copy(wide_far, wide, sems.at[0]),
        pltpu.make_async_copy(tall_far, tall, sems.at[1]),
    ]
    for copy in copies:
        copy.start()
    for copy in copies:
        copy.wait()
    parts = [wide[j] for j in range(wide.shape[0])]
    packed[...] = jnp.concatenate(parts + [tall[...].T], axis=1)


def prepare_kernel(ids, t0, t1, t2, t3, gain, freq, n1, cosine, sine):
    gain_row = gain[...].astype(F32)
    for i, source in enumerate((t0, t1, t2, t3)):
        unit, _ = normed(source[...].astype(F32))
        n1[rows_of(ids[i]), :] = (unit * gain_row).astype(BF)
    start = jnp.int32(0)
    lane = lax.broadcasted_iota(jnp.int32, (WINDOW, 128), 1)
    sign = jnp.where(lane % HEAD_DIM < HEAD_DIM // 2, -1.0, 1.0)
    for b in range(4):
        start = jnp.where(ids[9 + b] > 0, b, start)
        place = lax.broadcasted_iota(jnp.int32, (WINDOW, 128), 0) + (b - start) * WINDOW
        angle = place.astype(F32) * freq[...]
        cosine[b * WINDOW : (b + 1) * WINDOW, :] = jnp.cos(angle)
        sine[b * WINDOW : (b + 1) * WINDOW, :] = jnp.sin(angle) * sign


def put_pieces(ids, offsets, pieces, left, right, rows):
    cut = left.shape[1]
    for j, piece in enumerate(pieces):
        if offsets is None:
            at = slice(None)
        else:
            at = rows_of(jnp.bitwise_xor(ids[4], offsets[j]), rows)
        value = piece[...]
        left[at, :] = value[:, :cut]
        right[at, :] = value[:, cut:]


def attend_kernel(offsets, n_pieces, rows, ids, n1, cosine, sine, *rest):
    pieces = rest[:n_pieces]
    q_out, k_out, v_out, probs_out, att_out, whole, out_w, send, keep = rest[n_pieces : n_pieces + 9]
    k_pad, v_pad = rest[n_pieces + 9 :]
    put_pieces(ids, offsets, pieces, whole, out_w, rows)
    half = WINDOW // 2
    width = q_out.shape[1]
    heads = width // HEAD_DIM
    total_rows = q_out.shape[0]
    blocks = total_rows // WINDOW
    count = [ids[5 + b] for b in range(blocks)]
    first = [ids[5 + blocks + b] for b in range(blocks)]
    for pad in (k_pad, v_pad):
        pad[0:half, :] = jnp.zeros((half, width), BF)
        pad[half + total_rows :, :] = jnp.zeros((half, width), BF)
    for b in range(blocks):
        rows_b = slice(b * WINDOW, (b + 1) * WINDOW)
        raw = dot(n1[rows_b, :], whole[...])
        c = jnp.concatenate([cosine[rows_b, :]] * 3, axis=1)
        s = jnp.concatenate([sine[rows_b, :]] * 3, axis=1)
        qk = raw[:, : 2 * width]
        turned = (qk * c + swap_halves(qk) * s).astype(BF)
        q_out[rows_b, :] = turned[:, :width]
        k_b = turned[:, width:]
        v_b = raw[:, 2 * width :].astype(BF)
        k_out[rows_b, :] = k_b
        v_out[rows_b, :] = v_b
        k_pad[half + b * WINDOW : half + (b + 1) * WINDOW, :] = k_b
        v_pad[half + b * WINDOW : half + (b + 1) * WINDOW, :] = v_b
    span = 2 * WINDOW
    column = lax.broadcasted_iota(jnp.int32, (WINDOW, span), 1)
    row = lax.broadcasted_iota(jnp.int32, (WINDOW, span), 0)
    near = jnp.abs(row + half - column) <= half
    lanes = [head_lanes((WINDOW, width), h) for h in range(heads)]
    for b in range(blocks):
        rows_b = slice(b * WINDOW, (b + 1) * WINDOW)
        span_b = slice(b * WINDOW, b * WINDOW + span)
        before = jnp.where(first[b] == 0, count[b - 1], 0) if b > 0 else 0
        after = jnp.where(first[b + 1] == 0, count[b + 1], 0) if b + 1 < blocks else 0
        limit = jnp.where(
            column < half,
            before - half,
            jnp.where(column < half + WINDOW, count[b] + half, after + half + WINDOW),
        )
        allowed = near & (column < limit) & (row < count[b])
        spare = (lax.broadcasted_iota(jnp.int32, (WINDOW, 1), 0) >= count[b]).astype(F32)
        q_b = q_out[rows_b, :]
        stacked = jnp.concatenate([jnp.where(mine, q_b, 0) for mine in lanes], axis=0)
        scores = dot(stacked, k_pad[span_b, :], NT) * (HEAD_DIM**-0.5)
        allowed = jnp.concatenate([allowed] * heads, axis=0)
        masked = jnp.where(allowed, scores, NEG_FILL)
        peak = jnp.max(masked, axis=-1, keepdims=True)
        raised = jnp.where(allowed, jnp.exp(masked - peak), 0.0)
        total = jnp.sum(raised, axis=-1, keepdims=True) + jnp.concatenate([spare] * heads, axis=0)
        probs = (raised * (1.0 / total)).astype(BF)
        parts = dot(probs, v_pad[span_b, :])
        mixed = jnp.zeros((WINDOW, width), F32)
        for h, mine in enumerate(lanes):
            rows_h = slice(h * WINDOW, (h + 1) * WINDOW)
            probs_out[h, rows_b, :] = probs[rows_h, :]
            mixed = jnp.where(mine, parts[rows_h, :], mixed)
        att_out[rows_b, :] = mixed.astype(BF)
    for i in (2, 3, 0, 1):
        part = dot(att_out[rows_of(ids[i]), :], out_w[...], NT)
        at = slice((i % 2) * WINDOW, (i % 2 + 1) * WINDOW)
        if i < 2:
            keep[at, :] = part
        else:
            send[at, :] = part.astype(BF)


def middle_kernel(own, received, t0, t1, gain, h_out, n2_out):
    for i, tokens in enumerate((t0, t1)):
        at = slice(i * WINDOW, (i + 1) * WINDOW)
        back = slice((1 - i) * WINDOW, (2 - i) * WINDOW)
        branch = own[at, :].astype(F32) + received[back, :].astype(F32)
        h = tokens[...].astype(F32) + branch
        h_out[at, :] = h
        unit, _ = normed(h)
        n2_out[at, :] = (unit * gain[...].astype(F32)).astype(BF)


def units_kernel(offsets, n_pieces, rows, ids, n2, n2_far, c0, c1, c2, c3, *rest):
    send, keep, both_out, act_out, down_w, in_w = rest[n_pieces:]
    put_pieces(ids, offsets, rest[:n_pieces], in_w, down_w, rows)
    units = act_out.shape[1]
    gate_w, up_w = in_w[:, :units], in_w[:, units:]
    for i in (2, 3, 0, 1):
        at = slice((i % 2) * WINDOW, (i % 2 + 1) * WINDOW)
        rows_n = (n2 if i < 2 else n2_far)[at, :]
        rows_g = (c0, c1, c2, c3)[i][...]
        gate = dot(rows_n, gate_w)
        up = dot(rows_n, up_w)
        g_act = dot(rows_g, down_w[...])
        phi = 0.5 * (1.0 + lax.erf(gate * np.float32(np.sqrt(0.5))))
        gelu = gate * phi
        slope = phi + gate * (jnp.exp(-0.5 * gate * gate) * np.float32(1.0 / np.sqrt(2.0 * np.pi)))
        act_out[i * WINDOW : (i + 1) * WINDOW, :] = (gelu * up).astype(BF)
        g_both = jnp.concatenate([g_act * up * slope, g_act * gelu], axis=1).astype(BF)
        both_out[i * WINDOW : (i + 1) * WINDOW, :] = g_both
        part = dot(g_both, in_w[...], NT)
        if i < 2:
            keep[at, :] = part
        else:
            send[at, :] = part.astype(BF)


def emit_slots(ids, slots, rows, total, send, keep):
    for k in range(slots):
        near = jnp.bitwise_xor(ids[4], 2 * k)
        far = jnp.bitwise_xor(ids[4], 2 * k + 1)
        send[k] = total[rows_of(far, rows), :].astype(BF)
        keep[k] = total[rows_of(near, rows), :].astype(BF)


def unit_grads_kernel(
    slots, rows, ids, n2, n2_far, c0, c1, c2, c3, both, act, down_w, send, keep, b_send, b_keep, total
):
    pair = 2 * WINDOW
    units2 = both.shape[1]
    in_part = dot(n2[...], both[:pair, :], TN) + dot(n2_far[...], both[pair:, :], TN)
    total[:, :units2] = in_part
    gz = jnp.concatenate([c0[...], c1[...], c2[...], c3[...]], axis=0)
    down_part = dot(gz, act[...], TN)
    total[:, units2:] = down_part
    if slots:
        emit_slots(ids, slots, rows, total, send, keep)
    else:
        send[...] = total[...]
        keep[...] = jnp.zeros(keep.shape, BF)
    b_keep[...] = dot(act[:pair, :], down_w[...], NT)
    b_send[...] = dot(act[pair:, :], down_w[...], NT).astype(BF)


def residual_kernel(own, received, h, c0, c1, gain, gh_out, gy_out, gain_out):
    gain_row = gain[...].astype(F32)
    for i, cot in enumerate((c0, c1)):
        at = slice(i * WINDOW, (i + 1) * WINDOW)
        back = slice((1 - i) * WINDOW, (2 - i) * WINDOW)
        grad = own[at, :].astype(F32) + received[back, :].astype(F32)
        unit, scale = normed(h[at, :])
        gh = cot[...].astype(F32) + norm_back(grad, gain_row, unit, scale)
        gy_out[at, :] = gh.astype(BF)
        if i == 0:
            gh_out[...] = gh
            gain_out[...] = jnp.sum(grad * unit, axis=0, keepdims=True)


def attend_back_kernel(
    ids, gy, gy_far, out_w, q_in, k_in, v_in, probs_in, cosine, sine, n1, qkv_w, gain, gain_two,
    g_raw, g_send, g_keep, gains,
    g_att_all, k_pad, v_pad, gk_pad, gv_pad, gq_all,
):
    half = WINDOW // 2
    total_rows, width = q_in.shape
    heads = width // HEAD_DIM
    blocks = total_rows // WINDOW
    span = 2 * WINDOW
    for i in range(4):
        source = gy if i < 2 else gy_far
        part = dot(source[(i % 2) * WINDOW : (i % 2 + 1) * WINDOW, :], out_w[...])
        g_att_all[rows_of(ids[i]), :] = part.astype(BF)
    for pad, source in ((k_pad, k_in), (v_pad, v_in)):
        pad[0:half, :] = jnp.zeros((half, width), BF)
        pad[half + total_rows :, :] = jnp.zeros((half, width), BF)
        pad[half : half + total_rows, :] = source[...]
    lanes = [head_lanes((WINDOW, width), h) for h in range(heads)]
    gk_pad[...] = jnp.zeros(gk_pad.shape, F32)
    gv_pad[...] = jnp.zeros(gv_pad.shape, F32)
    for b in range(blocks):
        rows_b = slice(b * WINDOW, (b + 1) * WINDOW)
        span_b = slice(b * WINDOW, b * WINDOW + span)
        g_att = g_att_all[rows_b, :]
        q_b = q_in[rows_b, :]
        keys = k_pad[span_b, :]
        values = v_pad[span_b, :]
        g_stacked = jnp.concatenate([jnp.where(mine, g_att, 0) for mine in lanes], axis=0)
        q_stacked = jnp.concatenate([jnp.where(mine, q_b, 0) for mine in lanes], axis=0)
        probs = jnp.concatenate([probs_in[h, rows_b, :] for h in range(heads)], axis=0)
        wide = probs.astype(F32)
        g_probs = dot(g_stacked, values, NT)
        delta = jnp.sum(wide * g_probs, axis=-1, keepdims=True)
        g_scores = (wide * (g_probs - delta)).astype(BF)
        parts = dot(g_scores, keys)
        gq = jnp.zeros((WINDOW, width), F32)
        for h, mine in enumerate(lanes):
            gq = jnp.where(mine, parts[h * WINDOW : (h + 1) * WINDOW, :], gq)
        gk = dot(g_scores, q_stacked, TN)
        gv = dot(probs, g_stacked, TN)
        gq_all[rows_b, :] = gq
        gk_pad[span_b, :] += gk
        gv_pad[span_b, :] += gv
    scale = HEAD_DIM**-0.5
    for b in range(blocks):
        rows_b = slice(b * WINDOW, (b + 1) * WINDOW)
        inner = slice(half + b * WINDOW, half + (b + 1) * WINDOW)
        c = jnp.concatenate([cosine[rows_b, :]] * 3, axis=1)
        s = jnp.concatenate([sine[rows_b, :]] * 3, axis=1)
        qk = jnp.concatenate([gq_all[rows_b, :], gk_pad[inner, :]], axis=1) * scale
        turned = qk * c - swap_halves(qk) * s
        g_raw[rows_b, : 2 * width] = turned.astype(BF)
        g_raw[rows_b, 2 * width :] = gv_pad[inner, :].astype(BF)
    gain_sum = jnp.zeros(gain_two.shape, F32)
    for i in (2, 3, 0, 1):
        at = slice((i % 2) * WINDOW, (i % 2 + 1) * WINDOW)
        g_n1 = dot(g_raw[rows_of(ids[i]), :], qkv_w[...], NT)
        gain_sum += jnp.sum(g_n1 * n1[rows_of(ids[i]), :].astype(F32), axis=0, keepdims=True)
        if i < 2:
            g_keep[at, :] = g_n1
        else:
            g_send[at, :] = g_n1.astype(BF)
    gains[0:1, :] = gain_sum / gain[...].astype(F32)
    gains[1:2, :] = gain_two[...]


def attend_grads_kernel(slots, rows, ids, n1, g_raw, gy, gy_far, att, send, keep, total):
    columns = g_raw.shape[1]
    total[:, :columns] = dot(n1[...], g_raw[...], TN)
    near = jnp.concatenate([att[rows_of(ids[i]), :] for i in (0, 1)], axis=0)
    far = jnp.concatenate([att[rows_of(ids[i]), :] for i in (2, 3)], axis=0)
    total[:, columns:] = dot(gy[...], near, TN) + dot(gy_far[...], far, TN)
    if slots:
        emit_slots(ids, slots, rows, total, send, keep)
    else:
        send[...] = total[...]
        keep[...] = jnp.zeros(keep.shape, BF)


def merge_kernel(keep, got, first, *others):
    first[...] = keep[0].astype(F32) + got[0].astype(F32)
    for k, other in enumerate(others):
        other[...] = (keep[k + 1].astype(F32) + got[k + 1].astype(F32)).astype(BF)


EXTRA = 8


def merge_gains_kernel(keep, got, gains, gains_got, first, *rest):
    others, total_out = rest[:-1], rest[-1]
    rows, columns = keep.shape[1:]
    first[...] = keep[0].astype(F32) + got[0].astype(F32)
    total = gains[...] + gains_got[...]
    total_out[...] = total
    high = total.astype(BF).astype(F32)
    low = (total - high).astype(BF).astype(F32)
    coded = jnp.concatenate([high, low, jnp.zeros((EXTRA - 4, columns), F32)], axis=0).astype(BF)
    for k, other in enumerate(others):
        other[:rows, :] = (keep[k + 1].astype(F32) + got[k + 1].astype(F32)).astype(BF)
        other[rows:, :] = coded


def deliver_kernel(with_gains, count, first, *rest):
    count_parts = len(rest) - 2
    if with_gains:
        count_parts = len(rest) - 5
        gains = rest[count_parts][...]
        rows = first.shape[0]
        for part in rest[:count_parts]:
            coded = part[rows:, :].astype(F32)
            gains = gains + coded[0:2, :] + coded[2:4, :]
        for j in range(gains.shape[1] // 128):
            rest[-4][j : j + 1, :] = gains[0:1, j * 128 : (j + 1) * 128]
            rest[-3][j : j + 1, :] = gains[1:2, j * 128 : (j + 1) * 128]
    total = first[...]
    for part in rest[:count_parts]:
        total = total + part[: first.shape[0], :].astype(F32)
    wide, turned = rest[-2:]
    width = wide.shape[2]
    for j in range(count):
        value = total[:, j * width : (j + 1) * width]
        if with_gains:
            wide[j] = value
        else:
            wide[:, j, :] = value
    turned[...] = total[:, count * width :].T


def finish_kernel(
    g_keep, g_core, b_keep, b_core, received, h, tokens, gain, gh, mixed_out, grad_out
):
    gain_row = gain[...].astype(F32)
    grad = g_keep[:WINDOW, :] + g_core[:WINDOW, :].astype(F32) + received[:WINDOW, :].astype(F32)
    unit, scale = normed(tokens[...].astype(F32))
    grad_out[...] = (gh[...] + norm_back(grad, gain_row, unit, scale)).astype(BF)
    branch = b_keep[:WINDOW, :] + b_core[:WINDOW, :].astype(F32) + received[WINDOW:, :].astype(F32)
    mixed_out[...] = (h[:WINDOW, :] + branch).astype(BF)


def swap(values, axis, bit, size):
    return lax.ppermute(values, axis, [(i, i ^ bit) for i in range(size)])


def local(
    tokens, block_count, block_first, norm1_gain, w_qkv, w_out, norm2_gain, w_in, w_down, cotangent
):
    n_dp = lax.axis_size("dp")
    width = tokens.shape[1]
    shard = width // n_dp
    head_width = w_qkv.shape[2]
    units = w_in.shape[2]
    heads = head_width // HEAD_DIM
    total_rows = block_count.shape[0] * WINDOW
    pair_rows = 2 * WINDOW
    slots = n_dp // 2 if shard % 16 == 0 and n_dp % 2 == 0 and n_dp <= 8 else 0
    place = lax.axis_index("tensor").astype(jnp.int32)
    ids = jnp.concatenate(
        [
            jnp.stack(
                [place, place ^ 2, place ^ 1, place ^ 3, lax.axis_index("dp").astype(jnp.int32)]
            ),
            block_count,
            block_first,
        ]
    )
    core = functools.partial(swap, axis="tensor", bit=1, size=4)
    across = functools.partial(swap, axis="tensor", bit=2, size=4)
    dp = functools.partial(swap, axis="dp", size=n_dp)

    def diagonal(values):
        pairs = [(4 * d + t, 4 * (d ^ 1) + (t ^ 2)) for d in range(n_dp) for t in range(4)]
        return lax.ppermute(values, ("dp", "tensor"), pairs)

    pin = lax.optimization_barrier

    def along(value, wait=None):
        if not slots:
            return [lax.all_gather(value, "dp", axis=0, tiled=True)]
        pieces = {0: value}
        for bit in reversed([1 << b for b in range(1, slots.bit_length())]):
            pieces.update({have ^ bit: dp(piece, bit=bit) for have, piece in pieces.items()})
            if wait is not None and len(pieces) == 2:
                pieces[bit], _ = pin((pieces[bit], wait))
        return [pieces[2 * k] for k in range(1, slots)]

    def aside(pieces):
        if not slots:
            return []
        if len(pieces) == 1:
            return [dp(pieces[0], bit=1)]
        return list(dp(jnp.stack(pieces), bit=1))

    def picked(own, near, far):
        return (own, *near, *far) if slots else tuple(near)

    def merge(keep, got, gains=()):
        _, rows, columns = keep.shape
        extra = EXTRA if gains else 0
        return call(
            merge_gains_kernel if gains else merge_kernel,
            (shape(rows, columns, dtype=F32),)
            + (shape(rows + extra, columns),) * (slots - 1)
            + ((shape(2, columns, dtype=F32),) if gains else ()),
            (keep, got, *gains),
        )

    def deliver(parts, count, gains=()):
        columns = parts[0].shape[1]
        each = columns // (count + 1)
        if not slots:
            total = parts[0]
            return total[:, : count * each].reshape(shard, count, each), total[:, count * each :].T
        with_gains = bool(gains)
        whole = (count, shard, each) if with_gains else (shard, count, each)
        *sums, wide, tall = call(
            functools.partial(deliver_kernel, with_gains, count),
            ((shape(columns // 128, 128, dtype=F32),) * 2 if with_gains else ())
            + (shape(*whole, dtype=F32), shape(each, shard, dtype=F32)),
            tuple(parts) + tuple(gains),
        )
        if with_gains:
            wide = jnp.transpose(wide, (1, 0, 2))
        return *(gain.reshape(columns) for gain in sums), wide, tall

    def slot_shapes(columns):
        if not slots:
            return (shape(width, columns, dtype=F32), shape(16, 128))
        return (shape(slots, shard, columns), shape(slots, shard, columns))

    gain_one = norm1_gain.reshape(1, width)
    gain_two = norm2_gain.reshape(1, width)
    freqs = ROPE_BASE ** (-(np.arange(HEAD_DIM // 2, dtype=np.float32) * 2.0) / HEAD_DIM)
    freq = jnp.asarray(np.tile(freqs, 128 // (HEAD_DIM // 2))[None, :], F32)

    offsets = tuple(range(0, n_dp, 2)) + tuple(range(1, n_dp, 2)) if slots else None

    def pack(wide, tall):
        count, _, each = wide.shape
        if not slots:
            return jnp.concatenate([*wide, tall.T], axis=1)
        return call(
            pack_kernel,
            (shape(shard, count * each + tall.shape[0]),),
            (wide, tall),
            scratch=[
                pltpu.VMEM(wide.shape, BF),
                pltpu.VMEM(tall.shape, BF),
                pltpu.SemaphoreType.DMA((2,)),
            ],
            space=pltpu.HBM,
        )[0]

    qkv_own = pack(jnp.transpose(w_qkv, (1, 0, 2)), w_out)
    unit_own = pack(jnp.transpose(w_in, (1, 0, 2)), w_down)
    qkv_near, qkv_side, unit_side, tokens_across, ids, gain_one, gain_two = pin(
        (
            along(qkv_own),
            aside([qkv_own]),
            aside([unit_own]),
            across(tokens),
            ids,
            gain_one,
            gain_two,
        )
    )
    token_blocks = (tokens, tokens_across, core(tokens), core(tokens_across))
    qkv_far = qkv_side + aside(qkv_near)
    n1, cosine, sine = call(
        prepare_kernel,
        (shape(total_rows, width), shape(total_rows, 128, dtype=F32), shape(total_rows, 128, dtype=F32)),
        token_blocks + (gain_one, freq),
        (ids,),
    )
    unit_own, cot, _ = pin((unit_own, cotangent, qkv_near))
    unit_near = along(unit_own, n1)
    cot_across = across(cot)
    qkv_far, n1 = pin((qkv_far, n1))
    qkv_pieces = picked(qkv_own, qkv_near, qkv_far)
    flat = shape(total_rows, head_width)
    pair_f32 = shape(pair_rows, width, dtype=F32)
    pair_bf = shape(pair_rows, width)
    query, keys, values, probs, attended, qkv_w, out_w, a_send, a_keep = call(
        functools.partial(attend_kernel, offsets, len(qkv_pieces), shard),
        (
            flat,
            flat,
            flat,
            shape(heads, total_rows, 2 * WINDOW),
            flat,
            shape(width, 3 * head_width),
            shape(width, head_width),
            pair_bf,
            pair_f32,
        ),
        (n1, cosine, sine) + qkv_pieces,
        (ids,),
        [pltpu.VMEM((total_rows + WINDOW, head_width), BF)] * 2,
        flops=2 * total_rows * width * 3 * head_width,
    )
    a_send, unit_near, cot_across = pin((a_send, unit_near, cot_across))
    cot_blocks = (cotangent, cot_across, core(cot), core(cot_across))
    unit_far = unit_side + aside(unit_near)
    unit_pieces = picked(unit_own, unit_near, unit_far)
    a_sum = (a_keep + core(a_send).astype(F32)).astype(BF)
    a_got = across(a_sum)
    h, n2 = call(
        middle_kernel,
        (pair_f32, pair_bf),
        (a_sum, a_got, token_blocks[0], token_blocks[1], gain_two),
    )
    n2_far = core(n2)
    u_send, u_keep, both, act, down_w = call(
        functools.partial(units_kernel, offsets, len(unit_pieces), shard),
        (
            pair_bf,
            pair_f32,
            shape(total_rows, 2 * units),
            shape(total_rows, units),
            shape(width, units),
        ),
        (n2, n2_far) + cot_blocks + unit_pieces,
        (ids,),
        [pltpu.VMEM((width, 2 * units), BF)],
    )
    u_sum = (u_keep + core(u_send).astype(F32)).astype(BF)
    u_got = across(u_sum)
    s_shapes = slot_shapes(3 * units)
    in_send, in_keep, b_send, b_keep = call(
        functools.partial(unit_grads_kernel, slots, shard),
        s_shapes + (pair_bf, pair_f32),
        (n2, n2_far) + cot_blocks + (both, act, down_w),
        (ids,),
        [pltpu.VMEM((width, 3 * units), F32)],
        flops=2 * total_rows * width * 4 * units,
    )
    b_core = core(b_send)
    u_got, in_keep = pin((u_got, in_keep))
    gh, gy, gain_part_two = call(
        residual_kernel,
        (shape(WINDOW, width, dtype=F32), pair_bf, shape(1, width, dtype=F32)),
        (u_sum, u_got, h, cot_blocks[0], cot_blocks[1], gain_two),
    )
    gy_far = core(gy)
    g_raw, g_send, g_keep, gains = call(
        attend_back_kernel,
        (
            shape(total_rows, 3 * head_width),
            pair_bf,
            pair_f32,
            shape(2, width, dtype=F32),
        ),
        (gy, gy_far, out_w, query, keys, values, probs, cosine, sine, n1, qkv_w)
        + (gain_one, gain_part_two),
        (ids,),
        [
            pltpu.VMEM((total_rows, head_width), BF),
            pltpu.VMEM((total_rows + WINDOW, head_width), BF),
            pltpu.VMEM((total_rows + WINDOW, head_width), BF),
            pltpu.VMEM((total_rows + WINDOW, head_width), F32),
            pltpu.VMEM((total_rows + WINDOW, head_width), F32),
            pltpu.VMEM((total_rows, head_width), F32),
        ],
    )
    if slots:
        g_raw, g_send, gains, in_got = pin((g_raw, g_send, gains, dp(in_send, bit=1)))
    att_send, att_keep = call(
        functools.partial(attend_grads_kernel, slots, shard),
        slot_shapes(4 * head_width),
        (n1, g_raw, gy, gy_far, attended),
        (ids,),
        [pltpu.VMEM((width, 4 * head_width), F32)],
    )
    if slots:
        in_got, att_keep = pin((in_got, att_keep))
        in_parts = merge(in_keep, in_got)
        in_near = [dp(in_parts[k], bit=2 * k) for k in range(1, slots)]
        gains = gains + core(gains)
        gains = gains + across(gains)
    g_core = core(g_send)
    if slots:
        gains, g_core, b_core = pin((gains, g_core, b_core))
    back = jnp.concatenate(
        [
            (g_keep[WINDOW:] + g_core[WINDOW:].astype(F32)).astype(BF),
            (b_keep[WINDOW:] + b_core[WINDOW:].astype(F32)).astype(BF),
        ],
        axis=0,
    )
    mixed, input_grad = call(
        finish_kernel,
        (shape(WINDOW, width), shape(WINDOW, width)),
        (g_keep, g_core, b_keep, b_core, across(back), h, tokens, gain_one, gh),
    )
    if slots:
        att_got, in_near[0], gains_x = pin((dp(att_send, bit=1), in_near[0], dp(gains, bit=1)))
        in_parts = (in_parts[0], *in_near)
        *att_parts, gains = merge(att_keep, att_got, (gains, gains_x))
        att_parts = (att_parts[0], *(dp(att_parts[k], bit=2 * k) for k in range(1, slots)))
        gains = [gains]
    else:
        gains = lax.psum(gains, ("dp", "tensor"))
        in_parts = (lax.psum_scatter(in_send, "dp", scatter_dimension=0, tiled=True),)
        att_parts = (lax.psum_scatter(att_send, "dp", scatter_dimension=0, tiled=True),)
    in_grad, down_grad = deliver(in_parts, 2)
    att_parts, mixed, input_grad, in_grad, down_grad = pin(
        (att_parts, mixed, input_grad, in_grad, down_grad)
    )
    if slots:
        *gains, qkv_grad, out_grad = deliver(att_parts, 3, gains)
    else:
        qkv_grad, out_grad = deliver(att_parts, 3)
    return (mixed, input_grad, gains[0], qkv_grad, out_grad, gains[1], in_grad, down_grad)


def solution(mesh):
    return jax.shard_map(
        local,
        mesh=mesh,
        in_specs=(
            P(("dp", "tensor"), None),
            P("dp"),
            P("dp"),
            P(),
            P("dp", None, "tensor"),
            P("tensor", "dp"),
            P(),
            P("dp", None, "tensor"),
            P("tensor", "dp"),
            P(("dp", "tensor"), None),
        ),
        out_specs=(
            P(("dp", "tensor"), None),
            P(("dp", "tensor"), None),
            P(),
            P("dp", None, "tensor"),
            P("tensor", "dp"),
            P(),
            P("dp", None, "tensor"),
            P("tensor", "dp"),
        ),
        check_vma=False,
    )
```

```python
import functools

import jax
import jax.numpy as jnp
import numpy as np
from jax import lax
from jax.experimental import pallas as pl
from jax.experimental.pallas import tpu as pltpu
from jax.sharding import PartitionSpec as P

HEAD_DIM = 64
WINDOW = 128
EPS = 1e-05
ROPE_BASE = 10000.0
NEG_FILL = -1e30
BF = jnp.bfloat16
F32 = jnp.float32

NN = (((1,), (0,)), ((), ()))
NT = (((1,), (1,)), ((), ()))
TN = (((0,), (0,)), ((), ()))


def dot(left, right, dims=NN):
    return lax.dot_general(left, right, dims, preferred_element_type=F32)


def call(kernel, outs, args, scalars=(), scratch=(), flops=0, space=pltpu.VMEM):
    size = sum(int(np.prod(a.shape)) * a.dtype.itemsize for a in list(args) + list(outs))
    return pl.pallas_call(
        kernel,
        name=getattr(kernel, "func", kernel).__name__,
        out_shape=tuple(outs),
        in_specs=[pl.BlockSpec(memory_space=pltpu.SMEM)] * len(scalars)
        + [pl.BlockSpec(memory_space=space)] * len(args),
        out_specs=tuple(pl.BlockSpec(memory_space=pltpu.VMEM) for _ in outs),
        scratch_shapes=list(scratch),
        compiler_params=pltpu.CompilerParams(vmem_limit_bytes=48 * 1024 * 1024),
        cost_estimate=pl.CostEstimate(flops=1, bytes_accessed=1, transcendentals=0),
    )(*scalars, *args)


def shape(*dims, dtype=BF):
    return jax.ShapeDtypeStruct(dims, dtype)


def rows_of(index, count=WINDOW):
    return pl.ds(pl.multiple_of(index * count, 16), count)


def normed(values):
    center = jnp.mean(values, axis=-1, keepdims=True)
    centred = values - center
    spread = jnp.mean(centred * centred, axis=-1, keepdims=True)
    scale = lax.rsqrt(spread + EPS)
    return centred * scale, scale


def norm_back(grad, gain, unit, scale):
    scaled = grad * gain
    first = jnp.mean(scaled, axis=-1, keepdims=True)
    second = jnp.mean(scaled * unit, axis=-1, keepdims=True)
    return scale * (scaled - first - unit * second)


def swap_halves(values):
    width = values.shape[1]
    lane = lax.broadcasted_iota(jnp.int32, values.shape, 1)
    return jnp.where(
        lane % HEAD_DIM < HEAD_DIM // 2,
        pltpu.roll(values, width - HEAD_DIM // 2, 1),
        pltpu.roll(values, HEAD_DIM // 2, 1),
    )


def head_lanes(shape_of, head):
    lane = lax.broadcasted_iota(jnp.int32, shape_of, 1)
    return (lane >= head * HEAD_DIM) & (lane < (head + 1) * HEAD_DIM)


def pack_kernel(wide_far, tall_far, packed, wide, tall, sems):
    copies = [
        pltpu.make_async_copy(wide_far, wide, sems.at[0]),
        pltpu.make_async_copy(tall_far, tall, sems.at[1]),
    ]
    for copy in copies:
        copy.start()
    for copy in copies:
        copy.wait()
    parts = [wide[j] for j in range(wide.shape[0])]
    packed[...] = jnp.concatenate(parts + [tall[...].T], axis=1)


def prepare_kernel(ids, t0, t1, t2, t3, gain, freq, n1, cosine, sine):
    gain_row = gain[...].astype(F32)
    for i, source in enumerate((t0, t1, t2, t3)):
        unit, _ = normed(source[...].astype(F32))
        n1[rows_of(ids[i]), :] = (unit * gain_row).astype(BF)
    start = jnp.int32(0)
    lane = lax.broadcasted_iota(jnp.int32, (WINDOW, 128), 1)
    sign = jnp.where(lane % HEAD_DIM < HEAD_DIM // 2, -1.0, 1.0)
    for b in range(4):
        start = jnp.where(ids[9 + b] > 0, b, start)
        place = lax.broadcasted_iota(jnp.int32, (WINDOW, 128), 0) + (b - start) * WINDOW
        angle = place.astype(F32) * freq[...]
        cosine[b * WINDOW : (b + 1) * WINDOW, :] = jnp.cos(angle)
        sine[b * WINDOW : (b + 1) * WINDOW, :] = jnp.sin(angle) * sign


def put_pieces(ids, offsets, pieces, left, right, rows):
    cut = left.shape[1]
    for j, piece in enumerate(pieces):
        if offsets is None:
            at = slice(None)
        else:
            at = rows_of(jnp.bitwise_xor(ids[4], offsets[j]), rows)
        value = piece[...]
        left[at, :] = value[:, :cut]
        right[at, :] = value[:, cut:]


def attend_kernel(offsets, n_pieces, rows, ids, n1, cosine, sine, *rest):
    pieces = rest[:n_pieces]
    q_out, k_out, v_out, probs_out, att_out, whole, out_w, send, keep = rest[n_pieces : n_pieces + 9]
    k_pad, v_pad, raw_all = rest[n_pieces + 9 :]
    put_pieces(ids, offsets, pieces, whole, out_w, rows)
    half = WINDOW // 2
    width = q_out.shape[1]
    heads = width // HEAD_DIM
    total_rows = q_out.shape[0]
    blocks = total_rows // WINDOW
    raw_all[...] = dot(n1[...], whole[...])
    count = [ids[5 + b] for b in range(blocks)]
    first = [ids[5 + blocks + b] for b in range(blocks)]
    for pad in (k_pad, v_pad):
        pad[0:half, :] = jnp.zeros((half, width), BF)
        pad[half + total_rows :, :] = jnp.zeros((half, width), BF)
    for b in range(blocks):
        rows_b = slice(b * WINDOW, (b + 1) * WINDOW)
        raw = raw_all[rows_b, :]
        c = jnp.concatenate([cosine[rows_b, :]] * 3, axis=1)
        s = jnp.concatenate([sine[rows_b, :]] * 3, axis=1)
        qk = raw[:, : 2 * width]
        turned = (qk * c + swap_halves(qk) * s).astype(BF)
        q_out[rows_b, :] = turned[:, :width]
        k_b = turned[:, width:]
        v_b = raw[:, 2 * width :].astype(BF)
        k_out[rows_b, :] = k_b
        v_out[rows_b, :] = v_b
        k_pad[half + b * WINDOW : half + (b + 1) * WINDOW, :] = k_b
        v_pad[half + b * WINDOW : half + (b + 1) * WINDOW, :] = v_b
    span = 2 * WINDOW
    column = lax.broadcasted_iota(jnp.int32, (WINDOW, span), 1)
    row = lax.broadcasted_iota(jnp.int32, (WINDOW, span), 0)
    near = jnp.abs(row + half - column) <= half
    lanes = [head_lanes((WINDOW, width), h) for h in range(heads)]
    for b in range(blocks):
        rows_b = slice(b * WINDOW, (b + 1) * WINDOW)
        span_b = slice(b * WINDOW, b * WINDOW + span)
        before = jnp.where(first[b] == 0, count[b - 1], 0) if b > 0 else 0
        after = jnp.where(first[b + 1] == 0, count[b + 1], 0) if b + 1 < blocks else 0
        limit = jnp.where(
            column < half,
            before - half,
            jnp.where(column < half + WINDOW, count[b] + half, after + half + WINDOW),
        )
        allowed = near & (column < limit) & (row < count[b])
        spare = (lax.broadcasted_iota(jnp.int32, (WINDOW, 1), 0) >= count[b]).astype(F32)
        q_b = q_out[rows_b, :]
        stacked = jnp.concatenate([jnp.where(mine, q_b, 0) for mine in lanes], axis=0)
        scores = dot(stacked, k_pad[span_b, :], NT) * (HEAD_DIM**-0.5)
        allowed = jnp.concatenate([allowed] * heads, axis=0)
        masked = jnp.where(allowed, scores, NEG_FILL)
        peak = jnp.max(masked, axis=-1, keepdims=True)
        raised = jnp.where(allowed, jnp.exp(masked - peak), 0.0)
        total = jnp.sum(raised, axis=-1, keepdims=True) + jnp.concatenate([spare] * heads, axis=0)
        probs = (raised * (1.0 / total)).astype(BF)
        parts = dot(probs, v_pad[span_b, :])
        mixed = jnp.zeros((WINDOW, width), F32)
        for h, mine in enumerate(lanes):
            rows_h = slice(h * WINDOW, (h + 1) * WINDOW)
            probs_out[h, rows_b, :] = probs[rows_h, :]
            mixed = jnp.where(mine, parts[rows_h, :], mixed)
        att_out[rows_b, :] = mixed.astype(BF)
    for i in (2, 3, 0, 1):
        part = dot(att_out[rows_of(ids[i]), :], out_w[...], NT)
        at = slice((i % 2) * WINDOW, (i % 2 + 1) * WINDOW)
        if i < 2:
            keep[at, :] = part
        else:
            send[at, :] = part.astype(BF)


def middle_kernel(own, received, t0, t1, gain, h_out, n2_out):
    for i, tokens in enumerate((t0, t1)):
        at = slice(i * WINDOW, (i + 1) * WINDOW)
        back = slice((1 - i) * WINDOW, (2 - i) * WINDOW)
        branch = own[at, :].astype(F32) + received[back, :].astype(F32)
        h = tokens[...].astype(F32) + branch
        h_out[at, :] = h
        unit, _ = normed(h)
        n2_out[at, :] = (unit * gain[...].astype(F32)).astype(BF)


def units_rows(rows_n, rows_g, in_w, down_w, both_out, act_out, gate, up, g_act):
    units = act_out.shape[1]
    gate[...] = dot(rows_n[...], in_w[:, :units])
    up[...] = dot(rows_n[...], in_w[:, units:])
    g_act[...] = dot(jnp.concatenate([block[...] for block in rows_g], axis=0), down_w[...])
    step = 64
    for start in range(0, act_out.shape[0], step):
        at = slice(start, start + step)
        gate_c, up_c, g_c = gate[at, :], up[at, :], g_act[at, :]
        phi = 0.5 * (1.0 + lax.erf(gate_c * np.float32(np.sqrt(0.5))))
        gelu = gate_c * phi
        slope = phi + gate_c * (
            jnp.exp(-0.5 * gate_c * gate_c) * np.float32(1.0 / np.sqrt(2.0 * np.pi))
        )
        act_out[at, :] = (gelu * up_c).astype(BF)
        both_out[at, :] = jnp.concatenate([g_c * up_c * slope, g_c * gelu], axis=1).astype(BF)
    return dot(both_out[...], in_w[...], NT)


def units_far_kernel(offsets, n_pieces, rows, ids, n2_far, c2, c3, *rest):
    send, both_out, act_out, in_w, down_w, *temps = rest[n_pieces:]
    put_pieces(ids, offsets, rest[:n_pieces], in_w, down_w, rows)
    part = units_rows(n2_far, (c2, c3), in_w, down_w, both_out, act_out, *temps)
    send[...] = part.astype(BF)


def units_near_kernel(n2, c0, c1, in_w, down_w, keep, both_out, act_out, *temps):
    keep[...] = units_rows(n2, (c0, c1), in_w, down_w, both_out, act_out, *temps)


def emit_slots(ids, slots, rows, total, send, keep):
    for k in range(slots):
        near = jnp.bitwise_xor(ids[4], 2 * k)
        far = jnp.bitwise_xor(ids[4], 2 * k + 1)
        send[k] = total[rows_of(far, rows), :].astype(BF)
        keep[k] = total[rows_of(near, rows), :].astype(BF)


def unit_grads_kernel(
    slots, rows, ids, n2, n2_far, c0, c1, c2, c3, both, both_far, act, act_far, down_w,
    send, keep, b_send, b_keep, total,
):
    units2 = both.shape[1]
    total[:, :units2] = dot(n2[...], both[...], TN) + dot(n2_far[...], both_far[...], TN)
    gz = jnp.concatenate([c0[...], c1[...]], axis=0)
    gz_far = jnp.concatenate([c2[...], c3[...]], axis=0)
    total[:, units2:] = dot(gz, act[...], TN) + dot(gz_far, act_far[...], TN)
    if slots:
        emit_slots(ids, slots, rows, total, send, keep)
    else:
        send[...] = total[...]
        keep[...] = jnp.zeros(keep.shape, BF)
    b_keep[...] = dot(act[...], down_w[...], NT)
    b_send[...] = dot(act_far[...], down_w[...], NT).astype(BF)


def residual_kernel(own, received, h, c0, c1, gain, gh_out, gy_out, gain_out):
    gain_row = gain[...].astype(F32)
    for i, cot in enumerate((c0, c1)):
        at = slice(i * WINDOW, (i + 1) * WINDOW)
        back = slice((1 - i) * WINDOW, (2 - i) * WINDOW)
        grad = own[at, :].astype(F32) + received[back, :].astype(F32)
        unit, scale = normed(h[at, :])
        gh = cot[...].astype(F32) + norm_back(grad, gain_row, unit, scale)
        gy_out[at, :] = gh.astype(BF)
        if i == 0:
            gh_out[...] = gh
            gain_out[...] = jnp.sum(grad * unit, axis=0, keepdims=True)


def attend_back_kernel(
    ids, gy, gy_far, out_w, q_in, k_in, v_in, probs_in, cosine, sine, n1, qkv_w, gain, gain_two,
    g_raw, g_send, g_keep, gains,
    g_att_all, k_pad, v_pad, gk_pad, gv_pad, gq_all, g_all,
):
    half = WINDOW // 2
    total_rows, width = q_in.shape
    heads = width // HEAD_DIM
    blocks = total_rows // WINDOW
    span = 2 * WINDOW
    for i in (0, 2):
        part = dot((gy_far if i else gy)[...], out_w[...]).astype(BF)
        g_att_all[rows_of(ids[i]), :] = part[:WINDOW, :]
        g_att_all[rows_of(ids[i + 1]), :] = part[WINDOW:, :]
    for pad, source in ((k_pad, k_in), (v_pad, v_in)):
        pad[0:half, :] = jnp.zeros((half, width), BF)
        pad[half + total_rows :, :] = jnp.zeros((half, width), BF)
        pad[half : half + total_rows, :] = source[...]
    lanes = [head_lanes((WINDOW, width), h) for h in range(heads)]
    gk_pad[...] = jnp.zeros(gk_pad.shape, F32)
    gv_pad[...] = jnp.zeros(gv_pad.shape, F32)
    for b in range(blocks):
        rows_b = slice(b * WINDOW, (b + 1) * WINDOW)
        span_b = slice(b * WINDOW, b * WINDOW + span)
        g_att = g_att_all[rows_b, :]
        q_b = q_in[rows_b, :]
        keys = k_pad[span_b, :]
        values = v_pad[span_b, :]
        g_stacked = jnp.concatenate([jnp.where(mine, g_att, 0) for mine in lanes], axis=0)
        q_stacked = jnp.concatenate([jnp.where(mine, q_b, 0) for mine in lanes], axis=0)
        probs = jnp.concatenate([probs_in[h, rows_b, :] for h in range(heads)], axis=0)
        wide = probs.astype(F32)
        g_probs = dot(g_stacked, values, NT)
        delta = jnp.sum(wide * g_probs, axis=-1, keepdims=True)
        g_scores = (wide * (g_probs - delta)).astype(BF)
        parts = dot(g_scores, keys)
        gq = jnp.zeros((WINDOW, width), F32)
        for h, mine in enumerate(lanes):
            gq = jnp.where(mine, parts[h * WINDOW : (h + 1) * WINDOW, :], gq)
        gk = dot(g_scores, q_stacked, TN)
        gv = dot(probs, g_stacked, TN)
        gq_all[rows_b, :] = gq
        gk_pad[span_b, :] += gk
        gv_pad[span_b, :] += gv
    scale = HEAD_DIM**-0.5
    for b in range(blocks):
        rows_b = slice(b * WINDOW, (b + 1) * WINDOW)
        inner = slice(half + b * WINDOW, half + (b + 1) * WINDOW)
        c = jnp.concatenate([cosine[rows_b, :]] * 3, axis=1)
        s = jnp.concatenate([sine[rows_b, :]] * 3, axis=1)
        qk = jnp.concatenate([gq_all[rows_b, :], gk_pad[inner, :]], axis=1) * scale
        turned = qk * c - swap_halves(qk) * s
        g_raw[rows_b, : 2 * width] = turned.astype(BF)
        g_raw[rows_b, 2 * width :] = gv_pad[inner, :].astype(BF)
    ordered = jnp.concatenate([g_raw[rows_of(ids[i]), :] for i in range(4)], axis=0)
    g_all[...] = dot(ordered, qkv_w[...], NT)
    gain_sum = jnp.zeros(gain_two.shape, F32)
    for i in range(4):
        at = slice((i % 2) * WINDOW, (i % 2 + 1) * WINDOW)
        g_n1 = g_all[i * WINDOW : (i + 1) * WINDOW, :]
        gain_sum += jnp.sum(g_n1 * n1[rows_of(ids[i]), :].astype(F32), axis=0, keepdims=True)
        if i < 2:
            g_keep[at, :] = g_n1
        else:
            g_send[at, :] = g_n1.astype(BF)
    gains[0:1, :] = gain_sum / gain[...].astype(F32)
    gains[1:2, :] = gain_two[...]


def attend_grads_kernel(slots, rows, ids, n1, g_raw, gy, gy_far, att, send, keep, total):
    columns = g_raw.shape[1]
    total[:, :columns] = dot(n1[...], g_raw[...], TN)
    near = jnp.concatenate([att[rows_of(ids[i]), :] for i in (0, 1)], axis=0)
    far = jnp.concatenate([att[rows_of(ids[i]), :] for i in (2, 3)], axis=0)
    total[:, columns:] = dot(gy[...], near, TN) + dot(gy_far[...], far, TN)
    if slots:
        emit_slots(ids, slots, rows, total, send, keep)
    else:
        send[...] = total[...]
        keep[...] = jnp.zeros(keep.shape, BF)


def merge_kernel(keep, got, first, *others):
    first[...] = keep[0].astype(F32) + got[0].astype(F32)
    for k, other in enumerate(others):
        other[...] = (keep[k + 1].astype(F32) + got[k + 1].astype(F32)).astype(BF)


EXTRA = 8


def merge_gains_kernel(keep, got, gains, gains_got, first, *rest):
    others, total_out = rest[:-1], rest[-1]
    rows, columns = keep.shape[1:]
    first[...] = keep[0].astype(F32) + got[0].astype(F32)
    total = gains[...] + gains_got[...]
    total_out[...] = total
    high = total.astype(BF).astype(F32)
    low = (total - high).astype(BF).astype(F32)
    coded = jnp.concatenate([high, low, jnp.zeros((EXTRA - 4, columns), F32)], axis=0).astype(BF)
    for k, other in enumerate(others):
        other[:rows, :] = (keep[k + 1].astype(F32) + got[k + 1].astype(F32)).astype(BF)
        other[rows:, :] = coded


def deliver_kernel(with_gains, count, first, *rest):
    count_parts = len(rest) - 2
    if with_gains:
        count_parts = len(rest) - 5
        gains = rest[count_parts][...]
        rows = first.shape[0]
        for part in rest[:count_parts]:
            coded = part[rows:, :].astype(F32)
            gains = gains + coded[0:2, :] + coded[2:4, :]
        for j in range(gains.shape[1] // 128):
            rest[-4][j : j + 1, :] = gains[0:1, j * 128 : (j + 1) * 128]
            rest[-3][j : j + 1, :] = gains[1:2, j * 128 : (j + 1) * 128]
    total = first[...]
    for part in rest[:count_parts]:
        total = total + part[: first.shape[0], :].astype(F32)
    wide, turned = rest[-2:]
    width = wide.shape[2]
    for j in range(count):
        value = total[:, j * width : (j + 1) * width]
        if with_gains:
            wide[j] = value
        else:
            wide[:, j, :] = value
    turned[...] = total[:, count * width :].T


def finish_kernel(
    g_keep, g_core, b_keep, b_core, received, h, tokens, gain, gh, mixed_out, grad_out
):
    gain_row = gain[...].astype(F32)
    grad = g_keep[:WINDOW, :] + g_core[:WINDOW, :].astype(F32) + received[:WINDOW, :].astype(F32)
    unit, scale = normed(tokens[...].astype(F32))
    grad_out[...] = (gh[...] + norm_back(grad, gain_row, unit, scale)).astype(BF)
    branch = b_keep[:WINDOW, :] + b_core[:WINDOW, :].astype(F32) + received[WINDOW:, :].astype(F32)
    mixed_out[...] = (h[:WINDOW, :] + branch).astype(BF)


def swap(values, axis, bit, size):
    return lax.ppermute(values, axis, [(i, i ^ bit) for i in range(size)])


def local(
    tokens, block_count, block_first, norm1_gain, w_qkv, w_out, norm2_gain, w_in, w_down, cotangent
):
    n_dp = lax.axis_size("dp")
    width = tokens.shape[1]
    shard = width // n_dp
    head_width = w_qkv.shape[2]
    units = w_in.shape[2]
    heads = head_width // HEAD_DIM
    total_rows = block_count.shape[0] * WINDOW
    pair_rows = 2 * WINDOW
    slots = n_dp // 2 if shard % 16 == 0 and n_dp % 2 == 0 and n_dp <= 8 else 0
    place = lax.axis_index("tensor").astype(jnp.int32)
    ids = jnp.concatenate(
        [
            jnp.stack(
                [place, place ^ 2, place ^ 1, place ^ 3, lax.axis_index("dp").astype(jnp.int32)]
            ),
            block_count,
            block_first,
        ]
    )
    core = functools.partial(swap, axis="tensor", bit=1, size=4)
    across = functools.partial(swap, axis="tensor", bit=2, size=4)
    dp = functools.partial(swap, axis="dp", size=n_dp)

    def diagonal(values):
        pairs = [(4 * d + t, 4 * (d ^ 1) + (t ^ 2)) for d in range(n_dp) for t in range(4)]
        return lax.ppermute(values, ("dp", "tensor"), pairs)

    pin = lax.optimization_barrier

    def along(value, wait=None):
        if not slots:
            return [lax.all_gather(value, "dp", axis=0, tiled=True)]
        pieces = {0: value}
        for bit in reversed([1 << b for b in range(1, slots.bit_length())]):
            pieces.update({have ^ bit: dp(piece, bit=bit) for have, piece in pieces.items()})
            if wait is not None and len(pieces) == 2:
                pieces[bit], _ = pin((pieces[bit], wait))
        return [pieces[2 * k] for k in range(1, slots)]

    def aside(pieces):
        if not slots:
            return []
        if len(pieces) == 1:
            return [dp(pieces[0], bit=1)]
        return list(dp(jnp.stack(pieces), bit=1))

    def picked(own, near, far):
        return (own, *near, *far) if slots else tuple(near)

    def merge(keep, got, gains=()):
        _, rows, columns = keep.shape
        extra = EXTRA if gains else 0
        return call(
            merge_gains_kernel if gains else merge_kernel,
            (shape(rows, columns, dtype=F32),)
            + (shape(rows + extra, columns),) * (slots - 1)
            + ((shape(2, columns, dtype=F32),) if gains else ()),
            (keep, got, *gains),
        )

    def deliver(parts, count, gains=()):
        columns = parts[0].shape[1]
        each = columns // (count + 1)
        if not slots:
            total = parts[0]
            return total[:, : count * each].reshape(shard, count, each), total[:, count * each :].T
        with_gains = bool(gains)
        whole = (count, shard, each) if with_gains else (shard, count, each)
        *sums, wide, tall = call(
            functools.partial(deliver_kernel, with_gains, count),
            ((shape(columns // 128, 128, dtype=F32),) * 2 if with_gains else ())
            + (shape(*whole, dtype=F32), shape(each, shard, dtype=F32)),
            tuple(parts) + tuple(gains),
        )
        if with_gains:
            wide = jnp.transpose(wide, (1, 0, 2))
        return *(gain.reshape(columns) for gain in sums), wide, tall

    def slot_shapes(columns):
        if not slots:
            return (shape(width, columns, dtype=F32), shape(16, 128))
        return (shape(slots, shard, columns), shape(slots, shard, columns))

    gain_one = norm1_gain.reshape(1, width)
    gain_two = norm2_gain.reshape(1, width)
    freqs = ROPE_BASE ** (-(np.arange(HEAD_DIM // 2, dtype=np.float32) * 2.0) / HEAD_DIM)
    freq = jnp.asarray(np.tile(freqs, 128 // (HEAD_DIM // 2))[None, :], F32)

    offsets = tuple(range(0, n_dp, 2)) + tuple(range(1, n_dp, 2)) if slots else None

    def pack(wide, tall):
        count, _, each = wide.shape
        if not slots:
            return jnp.concatenate([*wide, tall.T], axis=1)
        return call(
            pack_kernel,
            (shape(shard, count * each + tall.shape[0]),),
            (wide, tall),
            scratch=[
                pltpu.VMEM(wide.shape, BF),
                pltpu.VMEM(tall.shape, BF),
                pltpu.SemaphoreType.DMA((2,)),
            ],
            space=pltpu.HBM,
        )[0]

    qkv_own = pack(jnp.transpose(w_qkv, (1, 0, 2)), w_out)
    unit_own = pack(jnp.transpose(w_in, (1, 0, 2)), w_down)
    qkv_near, qkv_side, unit_side, tokens_across, ids, gain_one, gain_two = pin(
        (
            along(qkv_own),
            aside([qkv_own]),
            aside([unit_own]),
            across(tokens),
            ids,
            gain_one,
            gain_two,
        )
    )
    token_blocks = (tokens, tokens_across, core(tokens), core(tokens_across))
    qkv_far = qkv_side + aside(qkv_near)
    n1, cosine, sine = call(
        prepare_kernel,
        (shape(total_rows, width), shape(total_rows, 128, dtype=F32), shape(total_rows, 128, dtype=F32)),
        token_blocks + (gain_one, freq),
        (ids,),
    )
    unit_own, cot, _ = pin((unit_own, cotangent, qkv_near))
    unit_near = along(unit_own, n1)
    cot_across = across(cot)
    qkv_far, n1 = pin((qkv_far, n1))
    qkv_pieces = picked(qkv_own, qkv_near, qkv_far)
    flat = shape(total_rows, head_width)
    pair_f32 = shape(pair_rows, width, dtype=F32)
    pair_bf = shape(pair_rows, width)
    query, keys, values, probs, attended, qkv_w, out_w, a_send, a_keep = call(
        functools.partial(attend_kernel, offsets, len(qkv_pieces), shard),
        (
            flat,
            flat,
            flat,
            shape(heads, total_rows, 2 * WINDOW),
            flat,
            shape(width, 3 * head_width),
            shape(width, head_width),
            pair_bf,
            pair_f32,
        ),
        (n1, cosine, sine) + qkv_pieces,
        (ids,),
        [pltpu.VMEM((total_rows + WINDOW, head_width), BF)] * 2
        + [pltpu.VMEM((total_rows, 3 * head_width), F32)],
        flops=2 * total_rows * width * 3 * head_width,
    )
    a_send, unit_near, cot_across = pin((a_send, unit_near, cot_across))
    cot_blocks = (cotangent, cot_across, core(cot), core(cot_across))
    unit_far = unit_side + aside(unit_near)
    unit_pieces = picked(unit_own, unit_near, unit_far)
    a_sum = (a_keep + core(a_send).astype(F32)).astype(BF)
    a_got = across(a_sum)
    h, n2 = call(
        middle_kernel,
        (pair_f32, pair_bf),
        (a_sum, a_got, token_blocks[0], token_blocks[1], gain_two),
    )
    n2_far = core(n2)
    halves = (shape(pair_rows, 2 * units), shape(pair_rows, units))
    u_send, both_far, act_far, in_w, down_w = call(
        functools.partial(units_far_kernel, offsets, len(unit_pieces), shard),
        (pair_bf,) + halves + (shape(width, 2 * units), shape(width, units)),
        (n2_far,) + cot_blocks[2:] + unit_pieces,
        (ids,),
        [pltpu.VMEM((pair_rows, units), F32)] * 3,
    )
    u_keep, both, act = call(
        units_near_kernel,
        (pair_f32,) + halves,
        (n2,) + cot_blocks[:2] + (in_w, down_w),
        scratch=[pltpu.VMEM((pair_rows, units), F32)] * 3,
    )
    u_sum = (u_keep + core(u_send).astype(F32)).astype(BF)
    u_got = across(u_sum)
    s_shapes = slot_shapes(3 * units)
    in_send, in_keep, b_send, b_keep = call(
        functools.partial(unit_grads_kernel, slots, shard),
        s_shapes + (pair_bf, pair_f32),
        (n2, n2_far) + cot_blocks + (both, both_far, act, act_far, down_w),
        (ids,),
        [pltpu.VMEM((width, 3 * units), F32)],
        flops=2 * total_rows * width * 4 * units,
    )
    b_core = core(b_send)
    u_got, in_keep = pin((u_got, in_keep))
    gh, gy, gain_part_two = call(
        residual_kernel,
        (shape(WINDOW, width, dtype=F32), pair_bf, shape(1, width, dtype=F32)),
        (u_sum, u_got, h, cot_blocks[0], cot_blocks[1], gain_two),
    )
    gy_far = core(gy)
    g_raw, g_send, g_keep, gains = call(
        attend_back_kernel,
        (
            shape(total_rows, 3 * head_width),
            pair_bf,
            pair_f32,
            shape(2, width, dtype=F32),
        ),
        (gy, gy_far, out_w, query, keys, values, probs, cosine, sine, n1, qkv_w)
        + (gain_one, gain_part_two),
        (ids,),
        [
            pltpu.VMEM((total_rows, head_width), BF),
            pltpu.VMEM((total_rows + WINDOW, head_width), BF),
            pltpu.VMEM((total_rows + WINDOW, head_width), BF),
            pltpu.VMEM((total_rows + WINDOW, head_width), F32),
            pltpu.VMEM((total_rows + WINDOW, head_width), F32),
            pltpu.VMEM((total_rows, head_width), F32),
            pltpu.VMEM((total_rows, width), F32),
        ],
    )
    if slots:
        g_raw, g_send, gains, in_got = pin((g_raw, g_send, gains, dp(in_send, bit=1)))
    att_send, att_keep = call(
        functools.partial(attend_grads_kernel, slots, shard),
        slot_shapes(4 * head_width),
        (n1, g_raw, gy, gy_far, attended),
        (ids,),
        [pltpu.VMEM((width, 4 * head_width), F32)],
    )
    if slots:
        in_got, att_keep = pin((in_got, att_keep))
        in_parts = merge(in_keep, in_got)
        in_near = [dp(in_parts[k], bit=2 * k) for k in range(1, slots)]
        gains = gains + core(gains)
        gains = gains + across(gains)
    g_core = core(g_send)
    if slots:
        gains, g_core, b_core = pin((gains, g_core, b_core))
    back = jnp.concatenate(
        [
            (g_keep[WINDOW:] + g_core[WINDOW:].astype(F32)).astype(BF),
            (b_keep[WINDOW:] + b_core[WINDOW:].astype(F32)).astype(BF),
        ],
        axis=0,
    )
    mixed, input_grad = call(
        finish_kernel,
        (shape(WINDOW, width), shape(WINDOW, width)),
        (g_keep, g_core, b_keep, b_core, across(back), h, tokens, gain_one, gh),
    )
    if slots:
        att_got, in_near[0], gains_x = pin((dp(att_send, bit=1), in_near[0], dp(gains, bit=1)))
        in_parts = (in_parts[0], *in_near)
        *att_parts, gains = merge(att_keep, att_got, (gains, gains_x))
        att_parts = (att_parts[0], *(dp(att_parts[k], bit=2 * k) for k in range(1, slots)))
        gains = [gains]
    else:
        gains = lax.psum(gains, ("dp", "tensor"))
        in_parts = (lax.psum_scatter(in_send, "dp", scatter_dimension=0, tiled=True),)
        att_parts = (lax.psum_scatter(att_send, "dp", scatter_dimension=0, tiled=True),)
    in_grad, down_grad = deliver(in_parts, 2)
    att_parts, mixed, input_grad, in_grad, down_grad = pin(
        (att_parts, mixed, input_grad, in_grad, down_grad)
    )
    if slots:
        *gains, qkv_grad, out_grad = deliver(att_parts, 3, gains)
    else:
        qkv_grad, out_grad = deliver(att_parts, 3)
    return (mixed, input_grad, gains[0], qkv_grad, out_grad, gains[1], in_grad, down_grad)


def solution(mesh):
    return jax.shard_map(
        local,
        mesh=mesh,
        in_specs=(
            P(("dp", "tensor"), None),
            P("dp"),
            P("dp"),
            P(),
            P("dp", None, "tensor"),
            P("tensor", "dp"),
            P(),
            P("dp", None, "tensor"),
            P("tensor", "dp"),
            P(("dp", "tensor"), None),
        ),
        out_specs=(
            P(("dp", "tensor"), None),
            P(("dp", "tensor"), None),
            P(),
            P("dp", None, "tensor"),
            P("tensor", "dp"),
            P(),
            P("dp", None, "tensor"),
            P("tensor", "dp"),
        ),
        check_vma=False,
    )
```

```python
import functools

import jax
import jax.numpy as jnp
import numpy as np
from jax import lax
from jax.experimental import pallas as pl
from jax.experimental.pallas import tpu as pltpu
from jax.sharding import PartitionSpec as P

HEAD_DIM = 64
WINDOW = 128
EPS = 1e-05
ROPE_BASE = 10000.0
NEG_FILL = -1e30
BF = jnp.bfloat16
F32 = jnp.float32

NN = (((1,), (0,)), ((), ()))
NT = (((1,), (1,)), ((), ()))
TN = (((0,), (0,)), ((), ()))


def dot(left, right, dims=NN):
    return lax.dot_general(left, right, dims, preferred_element_type=F32)


def call(kernel, outs, args, scalars=(), scratch=(), flops=0, space=pltpu.VMEM):
    size = sum(int(np.prod(a.shape)) * a.dtype.itemsize for a in list(args) + list(outs))
    return pl.pallas_call(
        kernel,
        name=getattr(kernel, "func", kernel).__name__,
        out_shape=tuple(outs),
        in_specs=[pl.BlockSpec(memory_space=pltpu.SMEM)] * len(scalars)
        + [pl.BlockSpec(memory_space=space)] * len(args),
        out_specs=tuple(pl.BlockSpec(memory_space=pltpu.VMEM) for _ in outs),
        scratch_shapes=list(scratch),
        compiler_params=pltpu.CompilerParams(vmem_limit_bytes=48 * 1024 * 1024),
        cost_estimate=pl.CostEstimate(flops=1, bytes_accessed=1, transcendentals=0),
    )(*scalars, *args)


def shape(*dims, dtype=BF):
    return jax.ShapeDtypeStruct(dims, dtype)


def rows_of(index, count=WINDOW):
    return pl.ds(pl.multiple_of(index * count, 16), count)


def normed(values):
    center = jnp.mean(values, axis=-1, keepdims=True)
    centred = values - center
    spread = jnp.mean(centred * centred, axis=-1, keepdims=True)
    scale = lax.rsqrt(spread + EPS)
    return centred * scale, scale


def norm_back(grad, gain, unit, scale):
    scaled = grad * gain
    first = jnp.mean(scaled, axis=-1, keepdims=True)
    second = jnp.mean(scaled * unit, axis=-1, keepdims=True)
    return scale * (scaled - first - unit * second)


def swap_halves(values):
    width = values.shape[1]
    lane = lax.broadcasted_iota(jnp.int32, values.shape, 1)
    return jnp.where(
        lane % HEAD_DIM < HEAD_DIM // 2,
        pltpu.roll(values, width - HEAD_DIM // 2, 1),
        pltpu.roll(values, HEAD_DIM // 2, 1),
    )


def head_lanes(shape_of, head):
    lane = lax.broadcasted_iota(jnp.int32, shape_of, 1)
    return (lane >= head * HEAD_DIM) & (lane < (head + 1) * HEAD_DIM)


def pack_kernel(wide_far, tall_far, packed, wide, tall, sems):
    copies = [
        pltpu.make_async_copy(wide_far, wide, sems.at[0]),
        pltpu.make_async_copy(tall_far, tall, sems.at[1]),
    ]
    for copy in copies:
        copy.start()
    for copy in copies:
        copy.wait()
    parts = [wide[j] for j in range(wide.shape[0])]
    packed[...] = jnp.concatenate(parts + [tall[...].T], axis=1)


def prepare_kernel(ids, t0, t1, t2, t3, gain, freq, n1, cosine, sine):
    gain_row = gain[...].astype(F32)
    for i, source in enumerate((t0, t1, t2, t3)):
        unit, _ = normed(source[...].astype(F32))
        n1[rows_of(ids[i]), :] = (unit * gain_row).astype(BF)
    start = jnp.int32(0)
    lane = lax.broadcasted_iota(jnp.int32, (WINDOW, 128), 1)
    sign = jnp.where(lane % HEAD_DIM < HEAD_DIM // 2, -1.0, 1.0)
    for b in range(4):
        start = jnp.where(ids[9 + b] > 0, b, start)
        place = lax.broadcasted_iota(jnp.int32, (WINDOW, 128), 0) + (b - start) * WINDOW
        angle = place.astype(F32) * freq[...]
        cosine[b * WINDOW : (b + 1) * WINDOW, :] = jnp.cos(angle)
        sine[b * WINDOW : (b + 1) * WINDOW, :] = jnp.sin(angle) * sign


def put_pieces(ids, offsets, pieces, left, right, rows):
    cut = left.shape[1]
    for j, piece in enumerate(pieces):
        if offsets is None:
            at = slice(None)
        else:
            at = rows_of(jnp.bitwise_xor(ids[4], offsets[j]), rows)
        value = piece[...]
        left[at, :] = value[:, :cut]
        right[at, :] = value[:, cut:]


def attend_kernel(offsets, n_pieces, rows, ids, n1, cosine, sine, *rest):
    pieces = rest[:n_pieces]
    q_out, k_out, v_out, probs_out, att_out, whole, out_w, send, keep = rest[n_pieces : n_pieces + 9]
    k_pad, v_pad, raw_all = rest[n_pieces + 9 :]
    put_pieces(ids, offsets, pieces, whole, out_w, rows)
    half = WINDOW // 2
    width = q_out.shape[1]
    heads = width // HEAD_DIM
    total_rows = q_out.shape[0]
    blocks = total_rows // WINDOW
    raw_all[...] = dot(n1[...], whole[...])
    count = [ids[5 + b] for b in range(blocks)]
    first = [ids[5 + blocks + b] for b in range(blocks)]
    for pad in (k_pad, v_pad):
        pad[0:half, :] = jnp.zeros((half, width), BF)
        pad[half + total_rows :, :] = jnp.zeros((half, width), BF)
    for b in range(blocks):
        rows_b = slice(b * WINDOW, (b + 1) * WINDOW)
        raw = raw_all[rows_b, :]
        c = jnp.concatenate([cosine[rows_b, :]] * 3, axis=1)
        s = jnp.concatenate([sine[rows_b, :]] * 3, axis=1)
        qk = raw[:, : 2 * width]
        turned = (qk * c + swap_halves(qk) * s).astype(BF)
        q_out[rows_b, :] = turned[:, :width]
        k_b = turned[:, width:]
        v_b = raw[:, 2 * width :].astype(BF)
        k_out[rows_b, :] = k_b
        v_out[rows_b, :] = v_b
        k_pad[half + b * WINDOW : half + (b + 1) * WINDOW, :] = k_b
        v_pad[half + b * WINDOW : half + (b + 1) * WINDOW, :] = v_b
    span = 2 * WINDOW
    column = lax.broadcasted_iota(jnp.int32, (WINDOW, span), 1)
    row = lax.broadcasted_iota(jnp.int32, (WINDOW, span), 0)
    near = jnp.abs(row + half - column) <= half
    lanes = [head_lanes((WINDOW, width), h) for h in range(heads)]
    for b in range(blocks):
        rows_b = slice(b * WINDOW, (b + 1) * WINDOW)
        span_b = slice(b * WINDOW, b * WINDOW + span)
        before = jnp.where(first[b] == 0, count[b - 1], 0) if b > 0 else 0
        after = jnp.where(first[b + 1] == 0, count[b + 1], 0) if b + 1 < blocks else 0
        limit = jnp.where(
            column < half,
            before - half,
            jnp.where(column < half + WINDOW, count[b] + half, after + half + WINDOW),
        )
        allowed = near & (column < limit) & (row < count[b])
        spare = (lax.broadcasted_iota(jnp.int32, (WINDOW, 1), 0) >= count[b]).astype(F32)
        q_b = q_out[rows_b, :]
        stacked = jnp.concatenate([jnp.where(mine, q_b, 0) for mine in lanes], axis=0)
        scores = dot(stacked, k_pad[span_b, :], NT) * (HEAD_DIM**-0.5)
        allowed = jnp.concatenate([allowed] * heads, axis=0)
        masked = jnp.where(allowed, scores, NEG_FILL)
        peak = jnp.max(masked, axis=-1, keepdims=True)
        raised = jnp.where(allowed, jnp.exp(masked - peak), 0.0)
        total = jnp.sum(raised, axis=-1, keepdims=True) + jnp.concatenate([spare] * heads, axis=0)
        probs = (raised * (1.0 / total)).astype(BF)
        parts = dot(probs, v_pad[span_b, :])
        mixed = jnp.zeros((WINDOW, width), F32)
        for h, mine in enumerate(lanes):
            rows_h = slice(h * WINDOW, (h + 1) * WINDOW)
            probs_out[h, rows_b, :] = probs[rows_h, :]
            mixed = jnp.where(mine, parts[rows_h, :], mixed)
        att_out[rows_b, :] = mixed.astype(BF)
    for i in (2, 3, 0, 1):
        part = dot(att_out[rows_of(ids[i]), :], out_w[...], NT)
        at = slice((i % 2) * WINDOW, (i % 2 + 1) * WINDOW)
        if i < 2:
            keep[at, :] = part
        else:
            send[at, :] = part.astype(BF)


def middle_kernel(own, received, t0, t1, gain, h_out, n2_out):
    for i, tokens in enumerate((t0, t1)):
        at = slice(i * WINDOW, (i + 1) * WINDOW)
        back = slice((1 - i) * WINDOW, (2 - i) * WINDOW)
        branch = own[at, :].astype(F32) + received[back, :].astype(F32)
        h = tokens[...].astype(F32) + branch
        h_out[at, :] = h
        unit, _ = normed(h)
        n2_out[at, :] = (unit * gain[...].astype(F32)).astype(BF)


def units_rows(rows_n, rows_g, in_w, down_w, both_out, act_out, gate, up, g_act):
    units = act_out.shape[1]
    gate[...] = dot(rows_n[...], in_w[:, :units])
    up[...] = dot(rows_n[...], in_w[:, units:])
    g_act[...] = dot(jnp.concatenate([block[...] for block in rows_g], axis=0), down_w[...])
    step = 64
    for start in range(0, act_out.shape[0], step):
        at = slice(start, start + step)
        gate_c, up_c, g_c = gate[at, :], up[at, :], g_act[at, :]
        phi = 0.5 * (1.0 + lax.erf(gate_c * np.float32(np.sqrt(0.5))))
        gelu = gate_c * phi
        slope = phi + gate_c * (
            jnp.exp(-0.5 * gate_c * gate_c) * np.float32(1.0 / np.sqrt(2.0 * np.pi))
        )
        act_out[at, :] = (gelu * up_c).astype(BF)
        both_out[at, :] = jnp.concatenate([g_c * up_c * slope, g_c * gelu], axis=1).astype(BF)
    return dot(both_out[...], in_w[...], NT)


def units_far_kernel(offsets, n_pieces, rows, ids, n2_far, c2, c3, *rest):
    send, both_out, act_out, in_w, down_w, *temps = rest[n_pieces:]
    put_pieces(ids, offsets, rest[:n_pieces], in_w, down_w, rows)
    part = units_rows(n2_far, (c2, c3), in_w, down_w, both_out, act_out, *temps)
    send[...] = part.astype(BF)


def units_near_kernel(n2, c0, c1, in_w, down_w, keep, both_out, act_out, *temps):
    keep[...] = units_rows(n2, (c0, c1), in_w, down_w, both_out, act_out, *temps)


def emit_slots(ids, slots, rows, total, send, keep):
    for k in range(slots):
        near = jnp.bitwise_xor(ids[4], 2 * k)
        far = jnp.bitwise_xor(ids[4], 2 * k + 1)
        send[k] = total[rows_of(far, rows), :].astype(BF)
        keep[k] = total[rows_of(near, rows), :].astype(BF)


def unit_grads_kernel(
    slots, rows, ids, n2, n2_far, c0, c1, c2, c3, both, both_far, act, act_far, down_w,
    send, keep, b_send, b_keep, total,
):
    units2 = both.shape[1]
    total[:, :units2] = dot(n2[...], both[...], TN) + dot(n2_far[...], both_far[...], TN)
    gz = jnp.concatenate([c0[...], c1[...]], axis=0)
    gz_far = jnp.concatenate([c2[...], c3[...]], axis=0)
    total[:, units2:] = dot(gz, act[...], TN) + dot(gz_far, act_far[...], TN)
    if slots:
        emit_slots(ids, slots, rows, total, send, keep)
    else:
        send[...] = total[...]
        keep[...] = jnp.zeros(keep.shape, BF)
    b_keep[...] = dot(act[...], down_w[...], NT)
    b_send[...] = dot(act_far[...], down_w[...], NT).astype(BF)


def residual_kernel(own, received, h, c0, c1, gain, gh_out, gy_out, gain_out):
    gain_row = gain[...].astype(F32)
    for i, cot in enumerate((c0, c1)):
        at = slice(i * WINDOW, (i + 1) * WINDOW)
        back = slice((1 - i) * WINDOW, (2 - i) * WINDOW)
        grad = own[at, :].astype(F32) + received[back, :].astype(F32)
        unit, scale = normed(h[at, :])
        gh = cot[...].astype(F32) + norm_back(grad, gain_row, unit, scale)
        gy_out[at, :] = gh.astype(BF)
        if i == 0:
            gh_out[...] = gh
            gain_out[...] = jnp.sum(grad * unit, axis=0, keepdims=True)


def attend_back_kernel(
    ids, gy, gy_far, out_w, q_in, k_in, v_in, probs_in, cosine, sine, n1, qkv_w, gain, gain_two,
    g_raw, g_send, g_keep, gains,
    g_att_all, k_pad, v_pad, gk_pad, gv_pad, gq_all, g_all,
):
    half = WINDOW // 2
    total_rows, width = q_in.shape
    heads = width // HEAD_DIM
    blocks = total_rows // WINDOW
    span = 2 * WINDOW
    for i in (0, 2):
        part = dot((gy_far if i else gy)[...], out_w[...]).astype(BF)
        g_att_all[rows_of(ids[i]), :] = part[:WINDOW, :]
        g_att_all[rows_of(ids[i + 1]), :] = part[WINDOW:, :]
    for pad, source in ((k_pad, k_in), (v_pad, v_in)):
        pad[0:half, :] = jnp.zeros((half, width), BF)
        pad[half + total_rows :, :] = jnp.zeros((half, width), BF)
        pad[half : half + total_rows, :] = source[...]
    lanes = [head_lanes((WINDOW, width), h) for h in range(heads)]
    gk_pad[...] = jnp.zeros(gk_pad.shape, F32)
    gv_pad[...] = jnp.zeros(gv_pad.shape, F32)
    for b in range(blocks):
        rows_b = slice(b * WINDOW, (b + 1) * WINDOW)
        span_b = slice(b * WINDOW, b * WINDOW + span)
        g_att = g_att_all[rows_b, :]
        q_b = q_in[rows_b, :]
        keys = k_pad[span_b, :]
        values = v_pad[span_b, :]
        g_stacked = jnp.concatenate([jnp.where(mine, g_att, 0) for mine in lanes], axis=0)
        q_stacked = jnp.concatenate([jnp.where(mine, q_b, 0) for mine in lanes], axis=0)
        probs = jnp.concatenate([probs_in[h, rows_b, :] for h in range(heads)], axis=0)
        wide = probs.astype(F32)
        g_probs = dot(g_stacked, values, NT)
        delta = jnp.sum(wide * g_probs, axis=-1, keepdims=True)
        g_scores = (wide * (g_probs - delta)).astype(BF)
        parts = dot(g_scores, keys)
        gq = jnp.zeros((WINDOW, width), F32)
        for h, mine in enumerate(lanes):
            gq = jnp.where(mine, parts[h * WINDOW : (h + 1) * WINDOW, :], gq)
        gk = dot(g_scores, q_stacked, TN)
        gv = dot(probs, g_stacked, TN)
        gq_all[rows_b, :] = gq
        gk_pad[span_b, :] += gk
        gv_pad[span_b, :] += gv
    scale = HEAD_DIM**-0.5
    for b in range(blocks):
        rows_b = slice(b * WINDOW, (b + 1) * WINDOW)
        inner = slice(half + b * WINDOW, half + (b + 1) * WINDOW)
        c = jnp.concatenate([cosine[rows_b, :]] * 3, axis=1)
        s = jnp.concatenate([sine[rows_b, :]] * 3, axis=1)
        qk = jnp.concatenate([gq_all[rows_b, :], gk_pad[inner, :]], axis=1) * scale
        turned = qk * c - swap_halves(qk) * s
        g_raw[rows_b, : 2 * width] = turned.astype(BF)
        g_raw[rows_b, 2 * width :] = gv_pad[inner, :].astype(BF)
    ordered = jnp.concatenate([g_raw[rows_of(ids[i]), :] for i in range(4)], axis=0)
    g_all[...] = dot(ordered, qkv_w[...], NT)
    gain_sum = jnp.zeros(gain_two.shape, F32)
    for i in range(4):
        at = slice((i % 2) * WINDOW, (i % 2 + 1) * WINDOW)
        g_n1 = g_all[i * WINDOW : (i + 1) * WINDOW, :]
        gain_sum += jnp.sum(g_n1 * n1[rows_of(ids[i]), :].astype(F32), axis=0, keepdims=True)
        if i < 2:
            g_keep[at, :] = g_n1
        else:
            g_send[at, :] = g_n1.astype(BF)
    gains[0:1, :] = gain_sum / gain[...].astype(F32)
    gains[1:2, :] = gain_two[...]


def attend_grads_kernel(slots, rows, ids, n1, g_raw, gy, gy_far, att, send, keep, total):
    columns = g_raw.shape[1]
    total[:, :columns] = dot(n1[...], g_raw[...], TN)
    near = jnp.concatenate([att[rows_of(ids[i]), :] for i in (0, 1)], axis=0)
    far = jnp.concatenate([att[rows_of(ids[i]), :] for i in (2, 3)], axis=0)
    total[:, columns:] = dot(gy[...], near, TN) + dot(gy_far[...], far, TN)
    if slots:
        emit_slots(ids, slots, rows, total, send, keep)
    else:
        send[...] = total[...]
        keep[...] = jnp.zeros(keep.shape, BF)


def merge_kernel(keep, got, first, *others):
    first[...] = keep[0].astype(F32) + got[0].astype(F32)
    for k, other in enumerate(others):
        other[...] = (keep[k + 1].astype(F32) + got[k + 1].astype(F32)).astype(BF)


EXTRA = 8


def merge_gains_kernel(keep, got, gains, gains_got, first, *rest):
    others, total_out = rest[:-1], rest[-1]
    rows, columns = keep.shape[1:]
    first[...] = keep[0].astype(F32) + got[0].astype(F32)
    total = gains[...] + gains_got[...]
    total_out[...] = total
    high = total.astype(BF).astype(F32)
    low = (total - high).astype(BF).astype(F32)
    coded = jnp.concatenate([high, low, jnp.zeros((EXTRA - 4, columns), F32)], axis=0).astype(BF)
    for k, other in enumerate(others):
        other[:rows, :] = (keep[k + 1].astype(F32) + got[k + 1].astype(F32)).astype(BF)
        other[rows:, :] = coded


def deliver_kernel(with_gains, count, first, *rest):
    count_parts = len(rest) - 2
    if with_gains:
        count_parts = len(rest) - 5
        gains = rest[count_parts][...]
        rows = first.shape[0]
        for part in rest[:count_parts]:
            coded = part[rows:, :].astype(F32)
            gains = gains + coded[0:2, :] + coded[2:4, :]
        for j in range(gains.shape[1] // 128):
            rest[-4][j : j + 1, :] = gains[0:1, j * 128 : (j + 1) * 128]
            rest[-3][j : j + 1, :] = gains[1:2, j * 128 : (j + 1) * 128]
    total = first[...]
    for part in rest[:count_parts]:
        total = total + part[: first.shape[0], :].astype(F32)
    wide, turned = rest[-2:]
    width = wide.shape[2]
    for j in range(count):
        value = total[:, j * width : (j + 1) * width]
        if with_gains:
            wide[j] = value
        else:
            wide[:, j, :] = value
    turned[...] = total[:, count * width :].T


def finish_kernel(
    g_keep, g_core, b_keep, b_core, received, h, tokens, gain, gh, mixed_out, grad_out
):
    gain_row = gain[...].astype(F32)
    grad = g_keep[:WINDOW, :] + g_core[:WINDOW, :].astype(F32) + received[:WINDOW, :].astype(F32)
    unit, scale = normed(tokens[...].astype(F32))
    grad_out[...] = (gh[...] + norm_back(grad, gain_row, unit, scale)).astype(BF)
    branch = b_keep[:WINDOW, :] + b_core[:WINDOW, :].astype(F32) + received[WINDOW:, :].astype(F32)
    mixed_out[...] = (h[:WINDOW, :] + branch).astype(BF)


def swap(values, axis, bit, size):
    return lax.ppermute(values, axis, [(i, i ^ bit) for i in range(size)])


def local(
    tokens, block_count, block_first, norm1_gain, w_qkv, w_out, norm2_gain, w_in, w_down, cotangent
):
    n_dp = lax.axis_size("dp")
    width = tokens.shape[1]
    shard = width // n_dp
    head_width = w_qkv.shape[2]
    units = w_in.shape[2]
    heads = head_width // HEAD_DIM
    total_rows = block_count.shape[0] * WINDOW
    pair_rows = 2 * WINDOW
    slots = n_dp // 2 if shard % 16 == 0 and n_dp % 2 == 0 and n_dp <= 8 else 0
    place = lax.axis_index("tensor").astype(jnp.int32)
    ids = jnp.concatenate(
        [
            jnp.stack(
                [place, place ^ 2, place ^ 1, place ^ 3, lax.axis_index("dp").astype(jnp.int32)]
            ),
            block_count,
            block_first,
        ]
    )
    core = functools.partial(swap, axis="tensor", bit=1, size=4)
    across = functools.partial(swap, axis="tensor", bit=2, size=4)
    dp = functools.partial(swap, axis="dp", size=n_dp)

    pin = lax.optimization_barrier

    def along(value, wait=None):
        if not slots:
            return [lax.all_gather(value, "dp", axis=0, tiled=True)]
        pieces = {0: value}
        for bit in reversed([1 << b for b in range(1, slots.bit_length())]):
            pieces.update({have ^ bit: dp(piece, bit=bit) for have, piece in pieces.items()})
            if wait is not None and len(pieces) == 2:
                pieces[bit], _ = pin((pieces[bit], wait))
        return [pieces[2 * k] for k in range(1, slots)]

    def aside(pieces):
        if not slots:
            return []
        if len(pieces) == 1:
            return [dp(pieces[0], bit=1)]
        return list(dp(jnp.stack(pieces), bit=1))

    def picked(own, near, far):
        return (own, *near, *far) if slots else tuple(near)

    def merge(keep, got, gains=()):
        _, rows, columns = keep.shape
        extra = EXTRA if gains else 0
        return call(
            merge_gains_kernel if gains else merge_kernel,
            (shape(rows, columns, dtype=F32),)
            + (shape(rows + extra, columns),) * (slots - 1)
            + ((shape(2, columns, dtype=F32),) if gains else ()),
            (keep, got, *gains),
        )

    def deliver(parts, count, gains=()):
        columns = parts[0].shape[1]
        each = columns // (count + 1)
        if not slots:
            total = parts[0]
            return total[:, : count * each].reshape(shard, count, each), total[:, count * each :].T
        with_gains = bool(gains)
        whole = (count, shard, each) if with_gains else (shard, count, each)
        *sums, wide, tall = call(
            functools.partial(deliver_kernel, with_gains, count),
            ((shape(columns // 128, 128, dtype=F32),) * 2 if with_gains else ())
            + (shape(*whole, dtype=F32), shape(each, shard, dtype=F32)),
            tuple(parts) + tuple(gains),
        )
        if with_gains:
            wide = jnp.transpose(wide, (1, 0, 2))
        return *(gain.reshape(columns) for gain in sums), wide, tall

    def slot_shapes(columns):
        if not slots:
            return (shape(width, columns, dtype=F32), shape(16, 128))
        return (shape(slots, shard, columns), shape(slots, shard, columns))

    gain_one = norm1_gain.reshape(1, width)
    gain_two = norm2_gain.reshape(1, width)
    freqs = ROPE_BASE ** (-(np.arange(HEAD_DIM // 2, dtype=np.float32) * 2.0) / HEAD_DIM)
    freq = jnp.asarray(np.tile(freqs, 128 // (HEAD_DIM // 2))[None, :], F32)

    offsets = tuple(range(0, n_dp, 2)) + tuple(range(1, n_dp, 2)) if slots else None

    def pack(wide, tall):
        count, _, each = wide.shape
        if not slots:
            return jnp.concatenate([*wide, tall.T], axis=1)
        return call(
            pack_kernel,
            (shape(shard, count * each + tall.shape[0]),),
            (wide, tall),
            scratch=[
                pltpu.VMEM(wide.shape, BF),
                pltpu.VMEM(tall.shape, BF),
                pltpu.SemaphoreType.DMA((2,)),
            ],
            space=pltpu.HBM,
        )[0]

    qkv_own = pack(jnp.transpose(w_qkv, (1, 0, 2)), w_out)
    unit_own = pack(jnp.transpose(w_in, (1, 0, 2)), w_down)
    qkv_near, qkv_side, unit_side, tokens_across, ids, gain_one, gain_two = pin(
        (
            along(qkv_own),
            aside([qkv_own]),
            aside([unit_own]),
            across(tokens),
            ids,
            gain_one,
            gain_two,
        )
    )
    token_blocks = (tokens, tokens_across, core(tokens), core(tokens_across))
    qkv_far = qkv_side + aside(qkv_near)
    n1, cosine, sine = call(
        prepare_kernel,
        (shape(total_rows, width), shape(total_rows, 128, dtype=F32), shape(total_rows, 128, dtype=F32)),
        token_blocks + (gain_one, freq),
        (ids,),
    )
    unit_own, cot, _ = pin((unit_own, cotangent, qkv_near))
    unit_near = along(unit_own, n1)
    cot_across = across(cot)
    qkv_far, n1 = pin((qkv_far, n1))
    qkv_pieces = picked(qkv_own, qkv_near, qkv_far)
    flat = shape(total_rows, head_width)
    pair_f32 = shape(pair_rows, width, dtype=F32)
    pair_bf = shape(pair_rows, width)
    query, keys, values, probs, attended, qkv_w, out_w, a_send, a_keep = call(
        functools.partial(attend_kernel, offsets, len(qkv_pieces), shard),
        (
            flat,
            flat,
            flat,
            shape(heads, total_rows, 2 * WINDOW),
            flat,
            shape(width, 3 * head_width),
            shape(width, head_width),
            pair_bf,
            pair_f32,
        ),
        (n1, cosine, sine) + qkv_pieces,
        (ids,),
        [pltpu.VMEM((total_rows + WINDOW, head_width), BF)] * 2
        + [pltpu.VMEM((total_rows, 3 * head_width), F32)],
        flops=2 * total_rows * width * 3 * head_width,
    )
    a_send, unit_near, cot_across = pin((a_send, unit_near, cot_across))
    cot_blocks = (cotangent, cot_across, core(cot), core(cot_across))
    unit_far = unit_side + aside(unit_near)
    unit_pieces = picked(unit_own, unit_near, unit_far)
    a_sum = (a_keep + core(a_send).astype(F32)).astype(BF)
    a_got = across(a_sum)
    h, n2 = call(
        middle_kernel,
        (pair_f32, pair_bf),
        (a_sum, a_got, token_blocks[0], token_blocks[1], gain_two),
    )
    n2_far = core(n2)
    halves = (shape(pair_rows, 2 * units), shape(pair_rows, units))
    u_send, both_far, act_far, in_w, down_w = call(
        functools.partial(units_far_kernel, offsets, len(unit_pieces), shard),
        (pair_bf,) + halves + (shape(width, 2 * units), shape(width, units)),
        (n2_far,) + cot_blocks[2:] + unit_pieces,
        (ids,),
        [pltpu.VMEM((pair_rows, units), F32)] * 3,
    )
    u_keep, both, act = call(
        units_near_kernel,
        (pair_f32,) + halves,
        (n2,) + cot_blocks[:2] + (in_w, down_w),
        scratch=[pltpu.VMEM((pair_rows, units), F32)] * 3,
    )
    u_sum = (u_keep + core(u_send).astype(F32)).astype(BF)
    u_got = across(u_sum)
    s_shapes = slot_shapes(3 * units)
    in_send, in_keep, b_send, b_keep = call(
        functools.partial(unit_grads_kernel, slots, shard),
        s_shapes + (pair_bf, pair_f32),
        (n2, n2_far) + cot_blocks + (both, both_far, act, act_far, down_w),
        (ids,),
        [pltpu.VMEM((width, 3 * units), F32)],
        flops=2 * total_rows * width * 4 * units,
    )
    b_core = core(b_send)
    u_got, in_keep = pin((u_got, in_keep))
    gh, gy, gain_part_two = call(
        residual_kernel,
        (shape(WINDOW, width, dtype=F32), pair_bf, shape(1, width, dtype=F32)),
        (u_sum, u_got, h, cot_blocks[0], cot_blocks[1], gain_two),
    )
    gy_far = core(gy)
    g_raw, g_send, g_keep, gains = call(
        attend_back_kernel,
        (
            shape(total_rows, 3 * head_width),
            pair_bf,
            pair_f32,
            shape(2, width, dtype=F32),
        ),
        (gy, gy_far, out_w, query, keys, values, probs, cosine, sine, n1, qkv_w)
        + (gain_one, gain_part_two),
        (ids,),
        [
            pltpu.VMEM((total_rows, head_width), BF),
            pltpu.VMEM((total_rows + WINDOW, head_width), BF),
            pltpu.VMEM((total_rows + WINDOW, head_width), BF),
            pltpu.VMEM((total_rows + WINDOW, head_width), F32),
            pltpu.VMEM((total_rows + WINDOW, head_width), F32),
            pltpu.VMEM((total_rows, head_width), F32),
            pltpu.VMEM((total_rows, width), F32),
        ],
    )
    if slots:
        g_raw, g_send, gains, in_got = pin((g_raw, g_send, gains, dp(in_send, bit=1)))
    att_send, att_keep = call(
        functools.partial(attend_grads_kernel, slots, shard),
        slot_shapes(4 * head_width),
        (n1, g_raw, gy, gy_far, attended),
        (ids,),
        [pltpu.VMEM((width, 4 * head_width), F32)],
    )
    if slots:
        in_got, att_keep = pin((in_got, att_keep))
        in_parts = merge(in_keep, in_got)
        in_near = [dp(in_parts[k], bit=2 * k) for k in range(1, slots)]
        gains = gains + core(gains)
        gains = gains + across(gains)
    g_core = core(g_send)
    if slots:
        gains, g_core, b_core = pin((gains, g_core, b_core))
    back = jnp.concatenate(
        [
            (g_keep[WINDOW:] + g_core[WINDOW:].astype(F32)).astype(BF),
            (b_keep[WINDOW:] + b_core[WINDOW:].astype(F32)).astype(BF),
        ],
        axis=0,
    )
    mixed, input_grad = call(
        finish_kernel,
        (shape(WINDOW, width), shape(WINDOW, width)),
        (g_keep, g_core, b_keep, b_core, across(back), h, tokens, gain_one, gh),
    )
    if slots:
        att_got, in_near[-1], gains_x = pin((dp(att_send, bit=1), in_near[-1], dp(gains, bit=1)))
        in_parts = (in_parts[0], *in_near)
        *att_parts, gains = merge(att_keep, att_got, (gains, gains_x))
        att_parts = (att_parts[0], *(dp(att_parts[k], bit=2 * k) for k in range(1, slots)))
        gains = [gains]
    else:
        gains = lax.psum(gains, ("dp", "tensor"))
        in_parts = (lax.psum_scatter(in_send, "dp", scatter_dimension=0, tiled=True),)
        att_parts = (lax.psum_scatter(att_send, "dp", scatter_dimension=0, tiled=True),)
    in_grad, down_grad = deliver(in_parts, 2)
    att_parts, mixed, input_grad, in_grad, down_grad = pin(
        (att_parts, mixed, input_grad, in_grad, down_grad)
    )
    if slots:
        *gains, qkv_grad, out_grad = deliver(att_parts, 3, gains)
    else:
        qkv_grad, out_grad = deliver(att_parts, 3)
    return (mixed, input_grad, gains[0], qkv_grad, out_grad, gains[1], in_grad, down_grad)


def solution(mesh):
    return jax.shard_map(
        local,
        mesh=mesh,
        in_specs=(
            P(("dp", "tensor"), None),
            P("dp"),
            P("dp"),
            P(),
            P("dp", None, "tensor"),
            P("tensor", "dp"),
            P(),
            P("dp", None, "tensor"),
            P("tensor", "dp"),
            P(("dp", "tensor"), None),
        ),
        out_specs=(
            P(("dp", "tensor"), None),
            P(("dp", "tensor"), None),
            P(),
            P("dp", None, "tensor"),
            P("tensor", "dp"),
            P(),
            P("dp", None, "tensor"),
            P("tensor", "dp"),
        ),
        check_vma=False,
    )
```

```python
import functools

import jax
import jax.numpy as jnp
import numpy as np
from jax import lax
from jax.experimental import pallas as pl
from jax.experimental.pallas import tpu as pltpu
from jax.sharding import PartitionSpec as P

HEAD_DIM = 64
WINDOW = 128
EPS = 1e-05
ROPE_BASE = 10000.0
NEG_FILL = -1e30
BF = jnp.bfloat16
F32 = jnp.float32

NN = (((1,), (0,)), ((), ()))
NT = (((1,), (1,)), ((), ()))
TN = (((0,), (0,)), ((), ()))


def dot(left, right, dims=NN):
    return lax.dot_general(left, right, dims, preferred_element_type=F32)


def call(kernel, outs, args, scalars=(), scratch=(), flops=0, space=pltpu.VMEM):
    size = sum(int(np.prod(a.shape)) * a.dtype.itemsize for a in list(args) + list(outs))
    return pl.pallas_call(
        kernel,
        name=getattr(kernel, "func", kernel).__name__,
        out_shape=tuple(outs),
        in_specs=[pl.BlockSpec(memory_space=pltpu.SMEM)] * len(scalars)
        + [pl.BlockSpec(memory_space=space)] * len(args),
        out_specs=tuple(pl.BlockSpec(memory_space=pltpu.VMEM) for _ in outs),
        scratch_shapes=list(scratch),
        compiler_params=pltpu.CompilerParams(vmem_limit_bytes=48 * 1024 * 1024),
        cost_estimate=pl.CostEstimate(flops=1, bytes_accessed=1, transcendentals=0),
    )(*scalars, *args)


def shape(*dims, dtype=BF):
    return jax.ShapeDtypeStruct(dims, dtype)


def rows_of(index, count=WINDOW):
    return pl.ds(pl.multiple_of(index * count, 16), count)


def normed(values):
    center = jnp.mean(values, axis=-1, keepdims=True)
    centred = values - center
    spread = jnp.mean(centred * centred, axis=-1, keepdims=True)
    scale = lax.rsqrt(spread + EPS)
    return centred * scale, scale


def norm_back(grad, gain, unit, scale):
    scaled = grad * gain
    first = jnp.mean(scaled, axis=-1, keepdims=True)
    second = jnp.mean(scaled * unit, axis=-1, keepdims=True)
    return scale * (scaled - first - unit * second)


def swap_halves(values):
    width = values.shape[1]
    lane = lax.broadcasted_iota(jnp.int32, values.shape, 1)
    return jnp.where(
        lane % HEAD_DIM < HEAD_DIM // 2,
        pltpu.roll(values, width - HEAD_DIM // 2, 1),
        pltpu.roll(values, HEAD_DIM // 2, 1),
    )


def head_lanes(shape_of, head):
    lane = lax.broadcasted_iota(jnp.int32, shape_of, 1)
    return (lane >= head * HEAD_DIM) & (lane < (head + 1) * HEAD_DIM)


def pack_kernel(wide_far, tall_far, packed, wide, tall, sems):
    copies = [
        pltpu.make_async_copy(wide_far, wide, sems.at[0]),
        pltpu.make_async_copy(tall_far, tall, sems.at[1]),
    ]
    for copy in copies:
        copy.start()
    for copy in copies:
        copy.wait()
    parts = [wide[j] for j in range(wide.shape[0])]
    packed[...] = jnp.concatenate(parts + [tall[...].T], axis=1)


def prepare_kernel(ids, t0, t1, t2, t3, gain, freq, n1, n1_turned, cosine, sine):
    gain_row = gain[...].astype(F32)
    for i, source in enumerate((t0, t1, t2, t3)):
        unit, _ = normed(source[...].astype(F32))
        rows = (unit * gain_row).astype(BF)
        n1[rows_of(ids[i]), :] = rows
        n1_turned[:, pl.ds(pl.multiple_of(ids[i] * WINDOW, WINDOW), WINDOW)] = rows.T
    start = jnp.int32(0)
    lane = lax.broadcasted_iota(jnp.int32, (WINDOW, 128), 1)
    sign = jnp.where(lane % HEAD_DIM < HEAD_DIM // 2, -1.0, 1.0)
    for b in range(4):
        start = jnp.where(ids[9 + b] > 0, b, start)
        place = lax.broadcasted_iota(jnp.int32, (WINDOW, 128), 0) + (b - start) * WINDOW
        angle = place.astype(F32) * freq[...]
        cosine[b * WINDOW : (b + 1) * WINDOW, :] = jnp.cos(angle)
        sine[b * WINDOW : (b + 1) * WINDOW, :] = jnp.sin(angle) * sign


def put_pieces(ids, offsets, pieces, left, right, rows):
    cut = left.shape[1]
    for j, piece in enumerate(pieces):
        if offsets is None:
            at = slice(None)
        else:
            at = rows_of(jnp.bitwise_xor(ids[4], offsets[j]), rows)
        value = piece[...]
        left[at, :] = value[:, :cut]
        right[at, :] = value[:, cut:]


def attend_kernel(offsets, n_pieces, rows, ids, n1, cosine, sine, *rest):
    pieces = rest[:n_pieces]
    q_out, k_out, v_out, probs_out, att_out, whole, out_w, send, keep = rest[n_pieces : n_pieces + 9]
    k_pad, v_pad, raw_all = rest[n_pieces + 9 :]
    put_pieces(ids, offsets, pieces, whole, out_w, rows)
    half = WINDOW // 2
    width = q_out.shape[1]
    heads = width // HEAD_DIM
    total_rows = q_out.shape[0]
    blocks = total_rows // WINDOW
    raw_all[...] = dot(n1[...], whole[...])
    count = [ids[5 + b] for b in range(blocks)]
    first = [ids[5 + blocks + b] for b in range(blocks)]
    for pad in (k_pad, v_pad):
        pad[0:half, :] = jnp.zeros((half, width), BF)
        pad[half + total_rows :, :] = jnp.zeros((half, width), BF)
    for b in range(blocks):
        rows_b = slice(b * WINDOW, (b + 1) * WINDOW)
        raw = raw_all[rows_b, :]
        c = jnp.concatenate([cosine[rows_b, :]] * 3, axis=1)
        s = jnp.concatenate([sine[rows_b, :]] * 3, axis=1)
        qk = raw[:, : 2 * width]
        turned = (qk * c + swap_halves(qk) * s).astype(BF)
        q_out[rows_b, :] = turned[:, :width]
        k_b = turned[:, width:]
        v_b = raw[:, 2 * width :].astype(BF)
        k_out[rows_b, :] = k_b
        v_out[rows_b, :] = v_b
        k_pad[half + b * WINDOW : half + (b + 1) * WINDOW, :] = k_b
        v_pad[half + b * WINDOW : half + (b + 1) * WINDOW, :] = v_b
    span = 2 * WINDOW
    column = lax.broadcasted_iota(jnp.int32, (WINDOW, span), 1)
    row = lax.broadcasted_iota(jnp.int32, (WINDOW, span), 0)
    near = jnp.abs(row + half - column) <= half
    lanes = [head_lanes((WINDOW, width), h) for h in range(heads)]
    for b in range(blocks):
        rows_b = slice(b * WINDOW, (b + 1) * WINDOW)
        span_b = slice(b * WINDOW, b * WINDOW + span)
        before = jnp.where(first[b] == 0, count[b - 1], 0) if b > 0 else 0
        after = jnp.where(first[b + 1] == 0, count[b + 1], 0) if b + 1 < blocks else 0
        limit = jnp.where(
            column < half,
            before - half,
            jnp.where(column < half + WINDOW, count[b] + half, after + half + WINDOW),
        )
        allowed = near & (column < limit) & (row < count[b])
        spare = (lax.broadcasted_iota(jnp.int32, (WINDOW, 1), 0) >= count[b]).astype(F32)
        q_b = q_out[rows_b, :]
        stacked = jnp.concatenate([jnp.where(mine, q_b, 0) for mine in lanes], axis=0)
        scores = dot(stacked, k_pad[span_b, :], NT) * (HEAD_DIM**-0.5)
        allowed = jnp.concatenate([allowed] * heads, axis=0)
        masked = jnp.where(allowed, scores, NEG_FILL)
        peak = jnp.max(masked, axis=-1, keepdims=True)
        raised = jnp.where(allowed, jnp.exp(masked - peak), 0.0)
        total = jnp.sum(raised, axis=-1, keepdims=True) + jnp.concatenate([spare] * heads, axis=0)
        probs = (raised * (1.0 / total)).astype(BF)
        parts = dot(probs, v_pad[span_b, :])
        mixed = jnp.zeros((WINDOW, width), F32)
        for h, mine in enumerate(lanes):
            rows_h = slice(h * WINDOW, (h + 1) * WINDOW)
            probs_out[h, rows_b, :] = probs[rows_h, :]
            mixed = jnp.where(mine, parts[rows_h, :], mixed)
        att_out[rows_b, :] = mixed.astype(BF)
    for i in (2, 3, 0, 1):
        part = dot(att_out[rows_of(ids[i]), :], out_w[...], NT)
        at = slice((i % 2) * WINDOW, (i % 2 + 1) * WINDOW)
        if i < 2:
            keep[at, :] = part
        else:
            send[at, :] = part.astype(BF)


def middle_kernel(own, received, t0, t1, gain, h_out, n2_out):
    for i, tokens in enumerate((t0, t1)):
        at = slice(i * WINDOW, (i + 1) * WINDOW)
        back = slice((1 - i) * WINDOW, (2 - i) * WINDOW)
        branch = own[at, :].astype(F32) + received[back, :].astype(F32)
        h = tokens[...].astype(F32) + branch
        h_out[at, :] = h
        unit, _ = normed(h)
        n2_out[at, :] = (unit * gain[...].astype(F32)).astype(BF)


def units_rows(rows_n, rows_g, in_w, down_w, both_out, act_out, gate, up, g_act):
    units = act_out.shape[1]
    gate[...] = dot(rows_n[...], in_w[:, :units])
    up[...] = dot(rows_n[...], in_w[:, units:])
    g_act[...] = dot(jnp.concatenate([block[...] for block in rows_g], axis=0), down_w[...])
    step = 64
    for start in range(0, act_out.shape[0], step):
        at = slice(start, start + step)
        gate_c, up_c, g_c = gate[at, :], up[at, :], g_act[at, :]
        phi = 0.5 * (1.0 + lax.erf(gate_c * np.float32(np.sqrt(0.5))))
        gelu = gate_c * phi
        slope = phi + gate_c * (
            jnp.exp(-0.5 * gate_c * gate_c) * np.float32(1.0 / np.sqrt(2.0 * np.pi))
        )
        act_out[at, :] = (gelu * up_c).astype(BF)
        both_out[at, :] = jnp.concatenate([g_c * up_c * slope, g_c * gelu], axis=1).astype(BF)
    return dot(both_out[...], in_w[...], NT)


def units_far_kernel(offsets, n_pieces, rows, ids, n2_far, c2, c3, *rest):
    send, both_out, act_out, in_w, down_w, *temps = rest[n_pieces:]
    put_pieces(ids, offsets, rest[:n_pieces], in_w, down_w, rows)
    part = units_rows(n2_far, (c2, c3), in_w, down_w, both_out, act_out, *temps)
    send[...] = part.astype(BF)


def units_near_kernel(n2, c0, c1, in_w, down_w, keep, both_out, act_out, *temps):
    keep[...] = units_rows(n2, (c0, c1), in_w, down_w, both_out, act_out, *temps)


def emit_slots(ids, slots, rows, total, send, keep):
    for k in range(slots):
        near = jnp.bitwise_xor(ids[4], 2 * k)
        far = jnp.bitwise_xor(ids[4], 2 * k + 1)
        send[k] = total[rows_of(far, rows), :].astype(BF)
        keep[k] = total[rows_of(near, rows), :].astype(BF)


def unit_grads_kernel(
    slots, rows, ids, n2, n2_far, c0, c1, c2, c3, both, both_far, act, act_far, down_w,
    send, keep, b_send, b_keep, total,
):
    units2 = both.shape[1]
    total[:, :units2] = dot(n2[...], both[...], TN) + dot(n2_far[...], both_far[...], TN)
    gz = jnp.concatenate([c0[...], c1[...]], axis=0)
    gz_far = jnp.concatenate([c2[...], c3[...]], axis=0)
    total[:, units2:] = dot(gz, act[...], TN) + dot(gz_far, act_far[...], TN)
    if slots:
        emit_slots(ids, slots, rows, total, send, keep)
    else:
        send[...] = total[...]
        keep[...] = jnp.zeros(keep.shape, BF)
    b_keep[...] = dot(act[...], down_w[...], NT)
    b_send[...] = dot(act_far[...], down_w[...], NT).astype(BF)


def residual_kernel(own, received, h, c0, c1, gain, gh_out, gy_out, gain_out):
    gain_row = gain[...].astype(F32)
    for i, cot in enumerate((c0, c1)):
        at = slice(i * WINDOW, (i + 1) * WINDOW)
        back = slice((1 - i) * WINDOW, (2 - i) * WINDOW)
        grad = own[at, :].astype(F32) + received[back, :].astype(F32)
        unit, scale = normed(h[at, :])
        gh = cot[...].astype(F32) + norm_back(grad, gain_row, unit, scale)
        gy_out[at, :] = gh.astype(BF)
        if i == 0:
            gh_out[...] = gh
            gain_out[...] = jnp.sum(grad * unit, axis=0, keepdims=True)


def attend_back_kernel(
    ids, gy, gy_far, out_w, q_in, k_in, v_in, probs_in, cosine, sine, n1, qkv_w, gain, gain_two,
    g_raw, g_send, g_keep, gains,
    g_att_all, k_pad, v_pad, gk_pad, gv_pad, gq_all, g_all,
):
    half = WINDOW // 2
    total_rows, width = q_in.shape
    heads = width // HEAD_DIM
    blocks = total_rows // WINDOW
    span = 2 * WINDOW
    for i in (0, 2):
        part = dot((gy_far if i else gy)[...], out_w[...]).astype(BF)
        g_att_all[rows_of(ids[i]), :] = part[:WINDOW, :]
        g_att_all[rows_of(ids[i + 1]), :] = part[WINDOW:, :]
    for pad, source in ((k_pad, k_in), (v_pad, v_in)):
        pad[0:half, :] = jnp.zeros((half, width), BF)
        pad[half + total_rows :, :] = jnp.zeros((half, width), BF)
        pad[half : half + total_rows, :] = source[...]
    lanes = [head_lanes((WINDOW, width), h) for h in range(heads)]
    gk_pad[...] = jnp.zeros(gk_pad.shape, F32)
    gv_pad[...] = jnp.zeros(gv_pad.shape, F32)
    for b in range(blocks):
        rows_b = slice(b * WINDOW, (b + 1) * WINDOW)
        span_b = slice(b * WINDOW, b * WINDOW + span)
        g_att = g_att_all[rows_b, :]
        q_b = q_in[rows_b, :]
        keys = k_pad[span_b, :]
        values = v_pad[span_b, :]
        g_stacked = jnp.concatenate([jnp.where(mine, g_att, 0) for mine in lanes], axis=0)
        q_stacked = jnp.concatenate([jnp.where(mine, q_b, 0) for mine in lanes], axis=0)
        probs = jnp.concatenate([probs_in[h, rows_b, :] for h in range(heads)], axis=0)
        wide = probs.astype(F32)
        g_probs = dot(g_stacked, values, NT)
        delta = jnp.sum(wide * g_probs, axis=-1, keepdims=True)
        g_scores = (wide * (g_probs - delta)).astype(BF)
        parts = dot(g_scores, keys)
        gq = jnp.zeros((WINDOW, width), F32)
        for h, mine in enumerate(lanes):
            gq = jnp.where(mine, parts[h * WINDOW : (h + 1) * WINDOW, :], gq)
        gk = dot(g_scores, q_stacked, TN)
        gv = dot(probs, g_stacked, TN)
        gq_all[rows_b, :] = gq
        gk_pad[span_b, :] += gk
        gv_pad[span_b, :] += gv
    scale = HEAD_DIM**-0.5
    for b in range(blocks):
        rows_b = slice(b * WINDOW, (b + 1) * WINDOW)
        inner = slice(half + b * WINDOW, half + (b + 1) * WINDOW)
        c = jnp.concatenate([cosine[rows_b, :]] * 3, axis=1)
        s = jnp.concatenate([sine[rows_b, :]] * 3, axis=1)
        qk = jnp.concatenate([gq_all[rows_b, :], gk_pad[inner, :]], axis=1) * scale
        turned = qk * c - swap_halves(qk) * s
        g_raw[rows_b, : 2 * width] = turned.astype(BF)
        g_raw[rows_b, 2 * width :] = gv_pad[inner, :].astype(BF)
    ordered = jnp.concatenate([g_raw[rows_of(ids[i]), :] for i in range(4)], axis=0)
    g_all[...] = dot(ordered, qkv_w[...], NT)
    gain_sum = jnp.zeros(gain_two.shape, F32)
    for i in range(4):
        at = slice((i % 2) * WINDOW, (i % 2 + 1) * WINDOW)
        g_n1 = g_all[i * WINDOW : (i + 1) * WINDOW, :]
        gain_sum += jnp.sum(g_n1 * n1[rows_of(ids[i]), :].astype(F32), axis=0, keepdims=True)
        if i < 2:
            g_keep[at, :] = g_n1
        else:
            g_send[at, :] = g_n1.astype(BF)
    gains[0:1, :] = gain_sum / gain[...].astype(F32)
    gains[1:2, :] = gain_two[...]


def attend_grads_kernel(slots, rows, ids, n1_turned, g_raw, gy, gy_far, att, send, keep, total):
    columns = g_raw.shape[1]
    total[:, :columns] = dot(n1_turned[...], g_raw[...])
    near = jnp.concatenate([att[rows_of(ids[i]), :] for i in (0, 1)], axis=0)
    far = jnp.concatenate([att[rows_of(ids[i]), :] for i in (2, 3)], axis=0)
    total[:, columns:] = dot(gy[...], near, TN) + dot(gy_far[...], far, TN)
    if slots:
        emit_slots(ids, slots, rows, total, send, keep)
    else:
        send[...] = total[...]
        keep[...] = jnp.zeros(keep.shape, BF)


def merge_kernel(keep, got, first, *others):
    first[...] = keep[0].astype(F32) + got[0].astype(F32)
    for k, other in enumerate(others):
        other[...] = (keep[k + 1].astype(F32) + got[k + 1].astype(F32)).astype(BF)


EXTRA = 8


def merge_gains_kernel(keep, got, gains, gains_got, first, *rest):
    others, total_out = rest[:-1], rest[-1]
    rows, columns = keep.shape[1:]
    first[...] = keep[0].astype(F32) + got[0].astype(F32)
    total = gains[...] + gains_got[...]
    total_out[...] = total
    high = total.astype(BF).astype(F32)
    low = (total - high).astype(BF).astype(F32)
    coded = jnp.concatenate([high, low, jnp.zeros((EXTRA - 4, columns), F32)], axis=0).astype(BF)
    for k, other in enumerate(others):
        other[:rows, :] = (keep[k + 1].astype(F32) + got[k + 1].astype(F32)).astype(BF)
        other[rows:, :] = coded


def deliver_kernel(with_gains, count, first, *rest):
    count_parts = len(rest) - 2
    if with_gains:
        count_parts = len(rest) - 5
        gains = rest[count_parts][...]
        rows = first.shape[0]
        for part in rest[:count_parts]:
            coded = part[rows:, :].astype(F32)
            gains = gains + coded[0:2, :] + coded[2:4, :]
        for j in range(gains.shape[1] // 128):
            rest[-4][j : j + 1, :] = gains[0:1, j * 128 : (j + 1) * 128]
            rest[-3][j : j + 1, :] = gains[1:2, j * 128 : (j + 1) * 128]
    total = first[...]
    for part in rest[:count_parts]:
        total = total + part[: first.shape[0], :].astype(F32)
    wide, turned = rest[-2:]
    width = wide.shape[2]
    for j in range(count):
        value = total[:, j * width : (j + 1) * width]
        if with_gains:
            wide[j] = value
        else:
            wide[:, j, :] = value
    turned[...] = total[:, count * width :].T


def finish_kernel(
    g_keep, g_core, b_keep, b_core, received, h, tokens, gain, gh, mixed_out, grad_out
):
    gain_row = gain[...].astype(F32)
    grad = g_keep[:WINDOW, :] + g_core[:WINDOW, :].astype(F32) + received[:WINDOW, :].astype(F32)
    unit, scale = normed(tokens[...].astype(F32))
    grad_out[...] = (gh[...] + norm_back(grad, gain_row, unit, scale)).astype(BF)
    branch = b_keep[:WINDOW, :] + b_core[:WINDOW, :].astype(F32) + received[WINDOW:, :].astype(F32)
    mixed_out[...] = (h[:WINDOW, :] + branch).astype(BF)


def swap(values, axis, bit, size):
    return lax.ppermute(values, axis, [(i, i ^ bit) for i in range(size)])


def local(
    tokens, block_count, block_first, norm1_gain, w_qkv, w_out, norm2_gain, w_in, w_down, cotangent
):
    n_dp = lax.axis_size("dp")
    width = tokens.shape[1]
    shard = width // n_dp
    head_width = w_qkv.shape[2]
    units = w_in.shape[2]
    heads = head_width // HEAD_DIM
    total_rows = block_count.shape[0] * WINDOW
    pair_rows = 2 * WINDOW
    slots = n_dp // 2 if shard % 16 == 0 and n_dp % 2 == 0 and n_dp <= 8 else 0
    place = lax.axis_index("tensor").astype(jnp.int32)
    ids = jnp.concatenate(
        [
            jnp.stack(
                [place, place ^ 2, place ^ 1, place ^ 3, lax.axis_index("dp").astype(jnp.int32)]
            ),
            block_count,
            block_first,
        ]
    )
    core = functools.partial(swap, axis="tensor", bit=1, size=4)
    across = functools.partial(swap, axis="tensor", bit=2, size=4)
    dp = functools.partial(swap, axis="dp", size=n_dp)

    pin = lax.optimization_barrier

    def along(value, wait=None):
        if not slots:
            return [lax.all_gather(value, "dp", axis=0, tiled=True)]
        pieces = {0: value}
        for bit in reversed([1 << b for b in range(1, slots.bit_length())]):
            pieces.update({have ^ bit: dp(piece, bit=bit) for have, piece in pieces.items()})
            if wait is not None and len(pieces) == 2:
                pieces[bit], _ = pin((pieces[bit], wait))
        return [pieces[2 * k] for k in range(1, slots)]

    def aside(pieces):
        if not slots:
            return []
        if len(pieces) == 1:
            return [dp(pieces[0], bit=1)]
        return list(dp(jnp.stack(pieces), bit=1))

    def picked(own, near, far):
        return (own, *near, *far) if slots else tuple(near)

    def merge(keep, got, gains=()):
        _, rows, columns = keep.shape
        extra = EXTRA if gains else 0
        return call(
            merge_gains_kernel if gains else merge_kernel,
            (shape(rows, columns, dtype=F32),)
            + (shape(rows + extra, columns),) * (slots - 1)
            + ((shape(2, columns, dtype=F32),) if gains else ()),
            (keep, got, *gains),
        )

    def deliver(parts, count, gains=()):
        columns = parts[0].shape[1]
        each = columns // (count + 1)
        if not slots:
            total = parts[0]
            return total[:, : count * each].reshape(shard, count, each), total[:, count * each :].T
        with_gains = bool(gains)
        whole = (count, shard, each) if with_gains else (shard, count, each)
        *sums, wide, tall = call(
            functools.partial(deliver_kernel, with_gains, count),
            ((shape(columns // 128, 128, dtype=F32),) * 2 if with_gains else ())
            + (shape(*whole, dtype=F32), shape(each, shard, dtype=F32)),
            tuple(parts) + tuple(gains),
        )
        if with_gains:
            wide = jnp.transpose(wide, (1, 0, 2))
        return *(gain.reshape(columns) for gain in sums), wide, tall

    def slot_shapes(columns):
        if not slots:
            return (shape(width, columns, dtype=F32), shape(16, 128))
        return (shape(slots, shard, columns), shape(slots, shard, columns))

    gain_one = norm1_gain.reshape(1, width)
    gain_two = norm2_gain.reshape(1, width)
    freqs = ROPE_BASE ** (-(np.arange(HEAD_DIM // 2, dtype=np.float32) * 2.0) / HEAD_DIM)
    freq = jnp.asarray(np.tile(freqs, 128 // (HEAD_DIM // 2))[None, :], F32)

    offsets = tuple(range(0, n_dp, 2)) + tuple(range(1, n_dp, 2)) if slots else None

    def pack(wide, tall):
        count, _, each = wide.shape
        if not slots:
            return jnp.concatenate([*wide, tall.T], axis=1)
        return call(
            pack_kernel,
            (shape(shard, count * each + tall.shape[0]),),
            (wide, tall),
            scratch=[
                pltpu.VMEM(wide.shape, BF),
                pltpu.VMEM(tall.shape, BF),
                pltpu.SemaphoreType.DMA((2,)),
            ],
            space=pltpu.HBM,
        )[0]

    qkv_own = pack(jnp.transpose(w_qkv, (1, 0, 2)), w_out)
    unit_own = pack(jnp.transpose(w_in, (1, 0, 2)), w_down)
    qkv_near, qkv_side, unit_side, tokens_across, ids, gain_one, gain_two = pin(
        (
            along(qkv_own),
            aside([qkv_own]),
            aside([unit_own]),
            across(tokens),
            ids,
            gain_one,
            gain_two,
        )
    )
    token_blocks = (tokens, tokens_across, core(tokens), core(tokens_across))
    qkv_far = qkv_side + aside(qkv_near)
    n1, n1_turned, cosine, sine = call(
        prepare_kernel,
        (
            shape(total_rows, width),
            shape(width, total_rows),
            shape(total_rows, 128, dtype=F32),
            shape(total_rows, 128, dtype=F32),
        ),
        token_blocks + (gain_one, freq),
        (ids,),
    )
    unit_own, cot, _ = pin((unit_own, cotangent, qkv_near))
    unit_near = along(unit_own, n1)
    cot_across = across(cot)
    qkv_far, n1 = pin((qkv_far, n1))
    qkv_pieces = picked(qkv_own, qkv_near, qkv_far)
    flat = shape(total_rows, head_width)
    pair_f32 = shape(pair_rows, width, dtype=F32)
    pair_bf = shape(pair_rows, width)
    query, keys, values, probs, attended, qkv_w, out_w, a_send, a_keep = call(
        functools.partial(attend_kernel, offsets, len(qkv_pieces), shard),
        (
            flat,
            flat,
            flat,
            shape(heads, total_rows, 2 * WINDOW),
            flat,
            shape(width, 3 * head_width),
            shape(width, head_width),
            pair_bf,
            pair_f32,
        ),
        (n1, cosine, sine) + qkv_pieces,
        (ids,),
        [pltpu.VMEM((total_rows + WINDOW, head_width), BF)] * 2
        + [pltpu.VMEM((total_rows, 3 * head_width), F32)],
        flops=2 * total_rows * width * 3 * head_width,
    )
    a_send, unit_near, cot_across = pin((a_send, unit_near, cot_across))
    cot_blocks = (cotangent, cot_across, core(cot), core(cot_across))
    unit_far = unit_side + aside(unit_near)
    unit_pieces = picked(unit_own, unit_near, unit_far)
    a_sum = (a_keep + core(a_send).astype(F32)).astype(BF)
    a_got = across(a_sum)
    h, n2 = call(
        middle_kernel,
        (pair_f32, pair_bf),
        (a_sum, a_got, token_blocks[0], token_blocks[1], gain_two),
    )
    n2_far = core(n2)
    halves = (shape(pair_rows, 2 * units), shape(pair_rows, units))
    u_send, both_far, act_far, in_w, down_w = call(
        functools.partial(units_far_kernel, offsets, len(unit_pieces), shard),
        (pair_bf,) + halves + (shape(width, 2 * units), shape(width, units)),
        (n2_far,) + cot_blocks[2:] + unit_pieces,
        (ids,),
        [pltpu.VMEM((pair_rows, units), F32)] * 3,
    )
    u_keep, both, act = call(
        units_near_kernel,
        (pair_f32,) + halves,
        (n2,) + cot_blocks[:2] + (in_w, down_w),
        scratch=[pltpu.VMEM((pair_rows, units), F32)] * 3,
    )
    u_sum = (u_keep + core(u_send).astype(F32)).astype(BF)
    u_got = across(u_sum)
    s_shapes = slot_shapes(3 * units)
    in_send, in_keep, b_send, b_keep = call(
        functools.partial(unit_grads_kernel, slots, shard),
        s_shapes + (pair_bf, pair_f32),
        (n2, n2_far) + cot_blocks + (both, both_far, act, act_far, down_w),
        (ids,),
        [pltpu.VMEM((width, 3 * units), F32)],
        flops=2 * total_rows * width * 4 * units,
    )
    b_core = core(b_send)
    u_got, in_keep = pin((u_got, in_keep))
    gh, gy, gain_part_two = call(
        residual_kernel,
        (shape(WINDOW, width, dtype=F32), pair_bf, shape(1, width, dtype=F32)),
        (u_sum, u_got, h, cot_blocks[0], cot_blocks[1], gain_two),
    )
    gy_far = core(gy)
    g_raw, g_send, g_keep, gains = call(
        attend_back_kernel,
        (
            shape(total_rows, 3 * head_width),
            pair_bf,
            pair_f32,
            shape(2, width, dtype=F32),
        ),
        (gy, gy_far, out_w, query, keys, values, probs, cosine, sine, n1, qkv_w)
        + (gain_one, gain_part_two),
        (ids,),
        [
            pltpu.VMEM((total_rows, head_width), BF),
            pltpu.VMEM((total_rows + WINDOW, head_width), BF),
            pltpu.VMEM((total_rows + WINDOW, head_width), BF),
            pltpu.VMEM((total_rows + WINDOW, head_width), F32),
            pltpu.VMEM((total_rows + WINDOW, head_width), F32),
            pltpu.VMEM((total_rows, head_width), F32),
            pltpu.VMEM((total_rows, width), F32),
        ],
    )
    if slots:
        g_raw, g_send, gains, in_got = pin((g_raw, g_send, gains, dp(in_send, bit=1)))
    att_send, att_keep = call(
        functools.partial(attend_grads_kernel, slots, shard),
        slot_shapes(4 * head_width),
        (n1_turned, g_raw, gy, gy_far, attended),
        (ids,),
        [pltpu.VMEM((width, 4 * head_width), F32)],
    )
    if slots:
        in_got, att_keep = pin((in_got, att_keep))
        in_parts = merge(in_keep, in_got)
        in_near = [dp(in_parts[k], bit=2 * k) for k in range(1, slots)]
        gains = gains + core(gains)
        gains = gains + across(gains)
    g_core = core(g_send)
    if slots:
        gains, g_core, b_core = pin((gains, g_core, b_core))
    back = jnp.concatenate(
        [
            (g_keep[WINDOW:] + g_core[WINDOW:].astype(F32)).astype(BF),
            (b_keep[WINDOW:] + b_core[WINDOW:].astype(F32)).astype(BF),
        ],
        axis=0,
    )
    mixed, input_grad = call(
        finish_kernel,
        (shape(WINDOW, width), shape(WINDOW, width)),
        (g_keep, g_core, b_keep, b_core, across(back), h, tokens, gain_one, gh),
    )
    if slots:
        att_got, in_near[-1], gains_x = pin((dp(att_send, bit=1), in_near[-1], dp(gains, bit=1)))
        in_parts = (in_parts[0], *in_near)
        *att_parts, gains = merge(att_keep, att_got, (gains, gains_x))
        att_parts = (att_parts[0], *(dp(att_parts[k], bit=2 * k) for k in range(1, slots)))
        gains = [gains]
    else:
        gains = lax.psum(gains, ("dp", "tensor"))
        in_parts = (lax.psum_scatter(in_send, "dp", scatter_dimension=0, tiled=True),)
        att_parts = (lax.psum_scatter(att_send, "dp", scatter_dimension=0, tiled=True),)
    in_grad, down_grad = deliver(in_parts, 2)
    att_parts, mixed, input_grad, in_grad, down_grad = pin(
        (att_parts, mixed, input_grad, in_grad, down_grad)
    )
    if slots:
        *gains, qkv_grad, out_grad = deliver(att_parts, 3, gains)
    else:
        qkv_grad, out_grad = deliver(att_parts, 3)
    return (mixed, input_grad, gains[0], qkv_grad, out_grad, gains[1], in_grad, down_grad)


def solution(mesh):
    return jax.shard_map(
        local,
        mesh=mesh,
        in_specs=(
            P(("dp", "tensor"), None),
            P("dp"),
            P("dp"),
            P(),
            P("dp", None, "tensor"),
            P("tensor", "dp"),
            P(),
            P("dp", None, "tensor"),
            P("tensor", "dp"),
            P(("dp", "tensor"), None),
        ),
        out_specs=(
            P(("dp", "tensor"), None),
            P(("dp", "tensor"), None),
            P(),
            P("dp", None, "tensor"),
            P("tensor", "dp"),
            P(),
            P("dp", None, "tensor"),
            P("tensor", "dp"),
        ),
        check_vma=False,
    )
```
